32 devices in a mesh: context: 8 (over y, x, core), tensor: 4 (over z).
Axes of the slice: x: 2, y: 2, z: 4, core: 2. Of those that a mesh axis runs over, the one named last changes fastest.
Arguments:
- query_proj: bfloat16 [1024, 4096], P('context', 'tensor'), may hold values from -6 to 6
- key_proj: bfloat16 [1024, 4096], P('context', 'tensor'), may hold values from -6 to 6
- value_proj: bfloat16 [1024, 4096], P('context', 'tensor'), may hold values from -6 to 6
- short_taps: float32 [3, 7, 4096], P(None, None, 'tensor'), may hold values from -2.4 to 2.4
- long_filter: float32 [4, 1024, 1024], P('tensor', 'context'), may hold values from -1 to 1
- grad_mixed: bfloat16 [1024, 4096], P('context', 'tensor'), may hold values from -6 to 6
Outputs:
- mixed_out: bfloat16 [1024, 4096], P('context', 'tensor')
- input_grads: bfloat16 [3, 1024, 4096], P(None, 'context', 'tensor')
- filter_grad: float32 [4, 1024, 1024], P('tensor', 'context')
The draws below stay inside these ranges and needn't reach their ends.
All inputs are finite; a program needn't handle non-finite values.
Results may differ from the reference program's by a relative error of at most 0.0064.
Values may be sent and summed in bfloat16 or wider, within the bound.
No kernel may reach another device: no remote copies, remote signals or barrier semaphores. Data moves between devices by JAX's collectives and lax.ppermute only.
A program may use at most 64 MiB of HBM per device.

```python
import math
import jax
import jax.numpy as jnp
from jax import lax

D = 4096
TAPS = 7
SEQ = 1024
CH_TP = 1024


def draw_long_filter(key, part):
    subkeys = jax.random.split(key, 4)
    lag_axis = jnp.arange(SEQ, dtype=jnp.float32)
    log_tau = jax.random.uniform(subkeys[0], (D,), jnp.float32, math.log(30.0), math.log(4 * SEQ))
    rough_part = jax.random.normal(subkeys[1], (D, SEQ), jnp.float32)
    positions = jax.random.randint(subkeys[2], (D, 3), 1, SEQ)
    losses = jnp.log(jax.random.uniform(subkeys[3], (D, 3), jnp.float32, 0.5, 0.8))
    log_env = -lag_axis[None, :] * jnp.exp(-log_tau)[:, None]
    for number in range(3):
        reached = lag_axis[None, :] >= positions[:, number:number + 1].astype(jnp.float32)
        log_env = log_env + jnp.where(reached, losses[:, number:number + 1], 0.0)
    envelope = jnp.exp(log_env)
    norm_scale = jnp.sqrt(jnp.sum(envelope * envelope, axis=1, keepdims=True))
    values = jnp.clip(rough_part * envelope / norm_scale, -1.0, 1.0)
    return values.reshape(D // CH_TP, CH_TP, SEQ)


def block_scale(stream_key, dims, cuts, low, largest):
    def one(position, shards_of):
        steps = jax.random.uniform(jax.random.fold_in(jax.random.fold_in(stream_key, 6), position), (shards_of,), jnp.float32, low / len(cuts), largest / len(cuts))
        return jnp.repeat(jnp.exp(steps), dims[position] // shards_of).reshape((-1,) + (1,) * (len(dims) - position - 1))

    loudness = one(*cuts[0])
    for cut in cuts[1:]:
        loudness = loudness * one(*cut)
    return loudness


def noise(own_key, extent, scale, bound, cuts=(), kind=jnp.bfloat16):
    entries = jax.random.normal(own_key, extent, jnp.float32) * scale
    if len(cuts) > 0:
        entries = block_scale(own_key, extent, cuts, -0.22, 0.18) * entries
    return jnp.clip(entries, min=-bound, max=bound).astype(kind)


def setup_inputs(seed: int = 0) -> dict:
    arg_keys = jax.random.split(jax.random.key(seed), 7)
    return {
        "query_proj": noise(arg_keys[0], (SEQ, D), 1.0, 6.0, ((0, 8), (1, 4))),
        "key_proj": noise(arg_keys[1], (SEQ, D), 1.0, 6.0, ((0, 8), (1, 4))),
        "value_proj": noise(arg_keys[2], (SEQ, D), 1.0, 6.0, ((0, 8), (1, 4))),
        "short_taps": noise(arg_keys[3], (3, TAPS, D), 0.4, 2.4, ((2, 4),), jnp.float32),
        "long_filter": draw_long_filter(jax.random.fold_in(arg_keys[6], 71), 0),
        "grad_mixed": noise(arg_keys[5], (SEQ, D), 1.0, 6.0, ((0, 8), (1, 4))),
    }


def causal_taps(series, tap_weights):
    series = series.astype(jnp.float32)
    running = jnp.zeros(series.shape, jnp.float32)
    for offset in range(TAPS):
        shifted = jnp.pad(series, ((offset, 0), (0, 0)))[:SEQ]
        running = running + tap_weights[offset][None, :] * shifted
    return running

def reverse_taps(series, tap_weights):
    series = series.astype(jnp.float32)
    running = jnp.zeros(series.shape, jnp.float32)
    for offset in range(TAPS):
        shifted = jnp.pad(series, ((0, offset), (0, 0)))[offset:]
        running = running + tap_weights[offset][None, :] * shifted
    return running

def one_block(block_data):
    gated_rows, grad_rows, filter_rows = block_data
    fft_len = 2 * SEQ
    spec_gate = jnp.fft.rfft(gated_rows, fft_len)
    spec_filter = jnp.fft.rfft(filter_rows, fft_len)
    spec_grad = jnp.fft.rfft(grad_rows, fft_len)
    long_rows = jnp.fft.irfft(spec_gate * spec_filter, fft_len)[:, :SEQ]
    back_rows = jnp.fft.irfft(jnp.conj(spec_filter) * spec_grad, fft_len)[:, :SEQ]
    corr_rows = jnp.fft.irfft(jnp.conj(spec_gate) * spec_grad, fft_len)[:, :SEQ]
    return (long_rows, back_rows, corr_rows)

def reference(query_proj, key_proj, value_proj, short_taps, long_filter, grad_mixed):
    query_f = causal_taps(query_proj, short_taps[0])
    key_f = causal_taps(key_proj, short_taps[1])
    value_f = causal_taps(value_proj, short_taps[2])
    gated = (key_f * value_f).astype(jnp.bfloat16)
    grad_f = grad_mixed.astype(jnp.float32)
    grad_long = (grad_f * query_f).astype(jnp.bfloat16)
    groups = D // CH_TP
    gated_rows = gated.astype(jnp.float32).T.reshape(groups, CH_TP, SEQ)
    grad_rows = grad_long.astype(jnp.float32).T.reshape(groups, CH_TP, SEQ)
    long_rows, back_rows, corr_rows = lax.map(one_block, (gated_rows, grad_rows, long_filter))
    long_conv = long_rows.reshape(D, SEQ).T.astype(jnp.bfloat16)
    grad_gated = back_rows.reshape(D, SEQ).T.astype(jnp.bfloat16)
    long_f = long_conv.astype(jnp.float32)
    mixed_out = (query_f * long_f).astype(jnp.bfloat16)
    grad_query_f = (grad_f * long_f).astype(jnp.bfloat16)
    gated_back = grad_gated.astype(jnp.float32)
    grad_key_f = (gated_back * value_f).astype(jnp.bfloat16)
    grad_value_f = (gated_back * key_f).astype(jnp.bfloat16)
    input_grads = jnp.stack([reverse_taps(grad_query_f, short_taps[0]), reverse_taps(grad_key_f, short_taps[1]), reverse_taps(grad_value_f, short_taps[2])]).astype(jnp.bfloat16)
    filter_grad = corr_rows * (1.0 / math.sqrt(SEQ))
    return (mixed_out, input_grads, filter_grad)
```

```python
import functools
import math

import jax
import jax.numpy as jnp
import numpy as np
from jax import lax
from jax.experimental import pallas as pl
from jax.experimental.pallas import tpu as pltpu
from jax.sharding import PartitionSpec as P

precise = lax.Precision.HIGHEST


def from_behind(value, axis, steps):
    count = lax.axis_size(axis)
    first, last = (max(0, -steps), min(count, count - steps))
    return lax.ppermute(value, axis, [(source, source + steps) for source in range(first, last)])


def build_tables(blocks, tok_rows):
    outer_len = 2 * blocks
    full_len = outer_len * tok_rows
    k_one = jnp.arange(outer_len, dtype=jnp.int32)
    n_one = jnp.arange(blocks, dtype=jnp.int32)
    position = jnp.arange(tok_rows, dtype=jnp.int32)
    first_idx = k_one[:, None] * n_one[None, :] % outer_len
    first_angle = -2.0 * math.pi / outer_len * first_idx.astype(jnp.float32)
    second = position[:, None] * position[None, :] % tok_rows
    second_angle = -2.0 * math.pi / tok_rows * second.astype(jnp.float32)
    twist_idx = k_one[:, None] * position[None, :] % full_len
    twist_angle = -2.0 * math.pi / full_len * twist_idx.astype(jnp.float32)
    return (
        jnp.cos(first_angle),
        jnp.sin(first_angle),
        jnp.cos(second_angle),
        jnp.sin(second_angle),
        jnp.cos(twist_angle),
        jnp.sin(twist_angle),
    )


def transform(signal, tables):
    cos_first, sin_first, cos_second, sin_second, cos_twist, sin_twist = tables
    first_re = jnp.einsum("kn,gnm->gkm", cos_first, signal, precision=precise)
    first_im = jnp.einsum("kn,gnm->gkm", sin_first, signal, precision=precise)
    mid_re = first_re * cos_twist - first_im * sin_twist
    mid_im = first_re * sin_twist + first_im * cos_twist
    out_re = jnp.einsum("gkn,nm->gkm", mid_re, cos_second, precision=precise) - jnp.einsum(
        "gkn,nm->gkm", mid_im, sin_second, precision=precise
    )
    out_im = jnp.einsum("gkn,nm->gkm", mid_re, sin_second, precision=precise) + jnp.einsum(
        "gkn,nm->gkm", mid_im, cos_second, precision=precise
    )
    return (out_re, out_im)


def inverse(spec_re, spec_im, tables):
    cos_first, sin_first, cos_second, sin_second, cos_twist, sin_twist = tables
    full_len = cos_first.shape[0] * cos_second.shape[0]
    mid_re = jnp.einsum("gkn,nm->gkm", spec_re, cos_second, precision=precise) + jnp.einsum(
        "gkn,nm->gkm", spec_im, sin_second, precision=precise
    )
    mid_im = jnp.einsum("gkn,nm->gkm", spec_im, cos_second, precision=precise) - jnp.einsum(
        "gkn,nm->gkm", spec_re, sin_second, precision=precise
    )
    turn_re = mid_re * cos_twist + mid_im * sin_twist
    turn_im = mid_im * cos_twist - mid_re * sin_twist
    result = jnp.einsum("kn,gkm->gnm", cos_first, turn_re, precision=precise) + jnp.einsum(
        "kn,gkm->gnm", sin_first, turn_im, precision=precise
    )
    return result * (1.0 / full_len)


def causal_taps(series, preceding, tap_weights):
    tok_rows = series.shape[0]
    span = tap_weights.shape[0]
    joined = jnp.concatenate([preceding, series], axis=0).astype(jnp.float32)
    running = jnp.zeros(series.shape, jnp.float32)
    for offset in range(span):
        first_row = span - 1 - offset
        running = running + tap_weights[offset][None, :] * joined[first_row : first_row + tok_rows]
    return running


def reverse_taps(series, following, tap_weights):
    tok_rows = series.shape[0]
    span = tap_weights.shape[0]
    joined = jnp.concatenate([series, following], axis=0).astype(jnp.float32)
    running = jnp.zeros(series.shape, jnp.float32)
    for offset in range(span):
        running = running + tap_weights[offset][None, :] * joined[offset : offset + tok_rows]
    return running


def general_shards(query_proj, key_proj, value_proj, short_taps, long_filter, grad_mixed):
    tok_rows, channels = query_proj.shape
    blocks = lax.axis_size("context")
    halo_rows = short_taps.shape[1] - 1
    per_device = channels // blocks
    seq_len = tok_rows * blocks
    tables = build_tables(blocks, tok_rows)
    preceding = from_behind(
        (
            query_proj[tok_rows - halo_rows :],
            key_proj[tok_rows - halo_rows :],
            value_proj[tok_rows - halo_rows :],
        ),
        "context",
        1,
    )
    query_f = causal_taps(query_proj, preceding[0], short_taps[0])
    key_f = causal_taps(key_proj, preceding[1], short_taps[1])
    value_f = causal_taps(value_proj, preceding[2], short_taps[2])
    gated_prod = (key_f * value_f).astype(jnp.bfloat16)
    grad_f = grad_mixed.astype(jnp.float32)
    grad_long = (grad_f * query_f).astype(jnp.bfloat16)

    def to_spectrum(series):
        arranged = series.T.reshape(blocks, per_device, tok_rows)
        received = lax.all_to_all(arranged, "context", split_axis=0, concat_axis=2, tiled=True)
        item_count = received.shape[1]
        signal = received.reshape(item_count, blocks, tok_rows).astype(jnp.float32)
        return transform(signal, tables)

    def to_token_rows(spatial):
        arrived = lax.all_to_all(spatial, "context", split_axis=1, concat_axis=0, tiled=True)
        return arrived.reshape(channels, tok_rows).T

    gate_re, gate_im = to_spectrum(gated_prod)
    filter_re, filter_im = transform(long_filter.reshape(per_device, blocks, tok_rows), tables)
    long_spatial = inverse(
        gate_re * filter_re - gate_im * filter_im, gate_re * filter_im + gate_im * filter_re, tables
    ).astype(jnp.bfloat16)
    long_conv = to_token_rows(long_spatial)
    long_f = long_conv.astype(jnp.float32)
    mixed_out = (query_f * long_f).astype(jnp.bfloat16)
    grad_query_f = (grad_f * long_f).astype(jnp.bfloat16)
    grad_after = lax.optimization_barrier((grad_long, long_conv))[0]
    grad_re, grad_im = to_spectrum(grad_after)
    back_spatial = inverse(
        filter_re * grad_re + filter_im * grad_im, filter_re * grad_im - filter_im * grad_re, tables
    ).astype(jnp.bfloat16)
    corr_spatial = inverse(
        gate_re * grad_re + gate_im * grad_im, gate_re * grad_im - gate_im * grad_re, tables
    )
    grad_gated = to_token_rows(back_spatial).astype(jnp.float32)
    grad_key_f = (grad_gated * value_f).astype(jnp.bfloat16)
    grad_value_f = (grad_gated * key_f).astype(jnp.bfloat16)
    following = from_behind(
        (grad_query_f[:halo_rows], grad_key_f[:halo_rows], grad_value_f[:halo_rows]), "context", -1
    )
    input_grads = jnp.stack(
        [
            reverse_taps(grad_query_f, following[0], short_taps[0]),
            reverse_taps(grad_key_f, following[1], short_taps[1]),
            reverse_taps(grad_value_f, following[2], short_taps[2]),
        ]
    ).astype(jnp.bfloat16)
    filter_grad = (corr_spatial * (1.0 / math.sqrt(seq_len))).reshape(1, per_device, seq_len)
    return (mixed_out, input_grads, filter_grad)


LANES = 128
VMEM_BYTES = 48 * 1024 * 1024


def split_bf16(table):
    high = table.astype(jnp.bfloat16)
    low = (table - high.astype(np.float64)).astype(jnp.bfloat16)
    return (high, low)


@functools.cache
def block_tables(rows):
    bins = np.pi * (np.arange(rows) + 0.5)[:, None] / rows
    lag = np.arange(-rows, rows)[None, :]
    window = np.concatenate([np.cos(bins * lag), -np.sin(bins * lag)], axis=0)
    window_hi, window_lo = split_bf16(window)
    doubled = np.concatenate([window_hi[:, rows:], window_lo[:, rows:]], axis=1)
    inv_hi, inv_lo = split_bf16(window[:, rows:].T / rows)
    return (window_hi, window_lo, doubled, inv_hi, inv_lo)


def round_up(count, unit):
    return (count + unit - 1) // unit * unit


def head_rows(fresh, whole, halo):
    row = lax.broadcasted_iota(jnp.int32, fresh.shape, 0)
    return jnp.concatenate([jnp.where(row < halo, fresh, whole[:8]), whole[8:]], axis=0)


def tap_rows(taps_ref, which, lanes):
    return [taps_ref[which, pl.ds(offset, 1), lanes] for offset in range(taps_ref.shape[1])]


def short_filter(padded, rows, weights):
    running = weights[0] * padded[pl.ds(8, rows), :]
    for offset in range(1, len(weights)):
        running = running + weights[offset] * padded[pl.ds(8 - offset, rows), :]
    return running


def send_kernel(q_ref, k_ref, v_ref, g_ref, taps_ref, out_ref, padded, extra):
    rows = q_ref.shape[0]
    halo = taps_ref.shape[1] - 1
    groups = out_ref.shape[0]
    padded[:, pl.ds(0, 8), :] = jnp.zeros((3, 8, LANES), jnp.float32)
    extra[...] = jnp.zeros(extra.shape, jnp.float32)

    def body(group, carry):
        lanes = pl.ds(pl.multiple_of(group * LANES, LANES), LANES)
        filtered = []
        for which, ref in enumerate((q_ref, k_ref, v_ref)):
            padded[which, pl.ds(8, rows), :] = ref[:, lanes].astype(jnp.float32)
            filtered.append(short_filter(padded.at[which], rows, tap_rows(taps_ref, which, lanes)))
        query_f, key_f, value_f = filtered
        cotangent = g_ref[:, lanes].astype(jnp.float32)
        gated = head_rows(padded[1, pl.ds(8, 8), :], key_f * value_f, halo)
        grad_long = head_rows(cotangent[:8], cotangent * query_f, halo)
        out_ref[group, pl.ds(0, rows), :] = gated.astype(jnp.bfloat16)
        out_ref[group, pl.ds(rows, rows), :] = grad_long.astype(jnp.bfloat16)
        pieces = ((1, rows - halo), (2, 0), (2, rows - halo), (0, 0), (0, rows - halo))
        for place, (which, first) in enumerate(pieces):
            extra[pl.ds(place * halo, halo), :] = padded[which, pl.ds(8 + first, halo), :]
        out_ref[group, pl.ds(2 * rows, extra.shape[0]), :] = extra[...].astype(jnp.bfloat16)
        return carry

    lax.fori_loop(0, groups, body, 0)


def repair_heads(in_ref, taps_ref, edges, joined, rows):
    blocks = in_ref.shape[0]
    span = taps_ref.shape[1]
    halo = span - 1
    joined[...] = jnp.zeros(joined.shape, jnp.float32)
    for block in range(blocks):
        edges[block] = in_ref[block, pl.ds(2 * rows, edges.shape[1]), :].astype(jnp.float32)
    heads = []
    for block in range(blocks):
        key_head = in_ref[block, pl.ds(0, 16), :].astype(jnp.float32)
        grad_head = in_ref[block, pl.ds(rows, 16), :].astype(jnp.float32)[:8]
        joined[1, block, pl.ds(halo, 8), :] = key_head[:8]
        joined[2, block, pl.ds(halo, halo), :] = edges[block, pl.ds(halo, halo), :]
        joined[0, block, pl.ds(halo, halo), :] = edges[block, pl.ds(3 * halo, halo), :]
        if block > 0:
            for which, place in ((1, 0), (2, 2), (0, 4)):
                joined[which, block, pl.ds(0, halo), :] = edges[block - 1, pl.ds(place * halo, halo), :]
        filtered = []
        for which in range(3):
            running = jnp.zeros((8, LANES), jnp.float32)
            for offset in range(span):
                weight = taps_ref[which, pl.ds(offset, 1), :]
                running = running + weight * joined[which, block, pl.ds(halo - offset, 8), :]
            filtered.append(running)
        heads.append((filtered[0], filtered[1], filtered[2], grad_head))
    return heads


def to_spectra(in_ref, heads, doubled, spec_x, spec_g, rows, halo):
    for block, (query_f, key_f, value_f, cotangent) in enumerate(heads):
        parts = []
        for first, fresh in ((0, key_f * value_f), (rows, cotangent * query_f)):
            head = in_ref[block, pl.ds(first, 16), :].astype(jnp.float32)
            head = head_rows(fresh, head, halo).astype(jnp.bfloat16)
            parts.append(
                jnp.concatenate([head, in_ref[block, pl.ds(first + 16, rows - 16), :]], axis=0)
            )
        pair = jnp.concatenate(parts, axis=1)
        spectrum = jnp.dot(
            doubled, jnp.concatenate([pair, pair], axis=0), preferred_element_type=jnp.float32
        )
        spec_x[block] = spectrum[:, :LANES]
        spec_g[block] = spectrum[:, LANES:]


def filter_kernel(h_ref, window_hi, window_lo, out_ref):
    blocks, two_rows, _ = out_ref.shape
    rows = two_rows // 2
    for block in range(blocks):
        here = h_ref[:, pl.ds(block * rows, rows)]
        if block > 0:
            before = h_ref[:, pl.ds((block - 1) * rows, rows)]
        else:
            before = jnp.zeros_like(here)
        signal = jnp.concatenate([before, here], axis=1)
        high = signal.astype(jnp.bfloat16)
        low = (signal - high.astype(jnp.float32)).astype(jnp.bfloat16)

        def product(table, values):
            return lax.dot_general(
                table, values, (((1,), (1,)), ((), ())), preferred_element_type=jnp.float32
            )

        out_ref[block] = (
            product(window_hi[...], high) + product(window_lo[...], high) + product(window_hi[...], low)
        )


def load_tile(ref, count, tile, bins):
    real = [ref[index, pl.ds(pl.multiple_of(tile * 8, 8), 8), :] for index in range(count)]
    imag = [ref[index, pl.ds(pl.multiple_of(bins + tile * 8, 8), 8), :] for index in range(count)]
    return (real, imag)


def mixed_products(left, right, sums, conjugate):
    (left_re, left_im), (right_re, right_im) = left, right
    results = []
    for pairs in sums:
        total_re, total_im = None, None
        for one, two in pairs:
            a, b, c, d = left_re[one], left_im[one], right_re[two], right_im[two]
            if conjugate:
                real, imag = a * c + b * d, a * d - b * c
            else:
                real, imag = a * c - b * d, a * d + b * c
            total_re = real if total_re is None else total_re + real
            total_im = imag if total_im is None else total_im + imag
        results.append((total_re, total_im))
    return results


def back_to_rows(spectrum, inv_hi, inv_lo):
    high = spectrum.astype(jnp.bfloat16)
    low = (spectrum - high.astype(jnp.float32)).astype(jnp.bfloat16)
    return (
        jnp.dot(inv_hi, high, preferred_element_type=jnp.float32)
        + jnp.dot(inv_lo, high, preferred_element_type=jnp.float32)
        + jnp.dot(inv_hi, low, preferred_element_type=jnp.float32)
    )


def store_tile(ref, first_lane, results, tile, bins):
    lanes = pl.ds(first_lane, LANES)
    for index, (real, imag) in enumerate(results):
        ref[index, pl.ds(pl.multiple_of(tile * 8, 8), 8), lanes] = real
        ref[index, pl.ds(pl.multiple_of(bins + tile * 8, 8), 8), lanes] = imag


def convolve_kernel(
    in_ref, taps_ref, spec_h, doubled, inv_hi, inv_lo, out_ref,
    edges, joined, spec_x, spec_g, spec_y, extra,
):
    blocks = in_ref.shape[0]
    rows = inv_hi.shape[0]
    halo = taps_ref.shape[1] - 1
    heads = repair_heads(in_ref, taps_ref, edges, joined, rows)
    to_spectra(in_ref, heads, doubled[...], spec_x, spec_g, rows, halo)

    def body(tile, carry):
        filt = load_tile(spec_h, blocks, tile, rows)
        sums = [[(i - j, j) for j in range(i + 1)] for i in range(blocks)]
        store_tile(spec_y, 0, mixed_products(filt, load_tile(spec_x, blocks, tile, rows), sums, False), tile, rows)
        sums = [[(j - i, j) for j in range(i, blocks)] for i in range(blocks)]
        store_tile(spec_y, LANES, mixed_products(filt, load_tile(spec_g, blocks, tile, rows), sums, True), tile, rows)
        return carry

    lax.fori_loop(0, rows // 8, body, 0)
    extra[...] = jnp.zeros(extra.shape, jnp.float32)
    for block, (query_f, key_f, value_f, cotangent) in enumerate(heads):
        both = back_to_rows(spec_y[block], inv_hi[...], inv_lo[...])
        both = both.astype(jnp.bfloat16)
        out_ref[block, pl.ds(0, rows), :] = both[:, :LANES]
        head = both[:16].astype(jnp.float32)
        long_head, back_head = head[:8, :LANES], head[:8, LANES:]
        grad_key = back_head * value_f
        back = jnp.concatenate([head_rows(grad_key, head[:, LANES:], halo).astype(jnp.bfloat16), both[16:, LANES:]], axis=0)
        out_ref[block, pl.ds(rows, rows), :] = back
        grad_value = back_head * key_f
        own = (query_f * long_head, grad_value)
        following = (cotangent * long_head, grad_key, grad_value)
        for place, value in enumerate(own):
            extra[block, pl.ds(place * halo, halo), :] = value[:halo]
        if block > 0:
            for place, value in enumerate(following):
                extra[block - 1, pl.ds((2 + place) * halo, halo), :] = value[:halo]
    for block in range(blocks):
        out_ref[block, pl.ds(2 * rows, extra.shape[1]), :] = extra[block].astype(jnp.bfloat16)


def correlate_kernel(
    scale, in_ref, taps_ref, doubled, inv_hi, inv_lo, out_ref, edges, joined, spec_x, spec_g, spec_y
):
    blocks = in_ref.shape[0]
    rows = inv_hi.shape[0]
    halo = taps_ref.shape[1] - 1
    heads = repair_heads(in_ref, taps_ref, edges, joined, rows)
    to_spectra(in_ref, heads, doubled[...], spec_x, spec_g, rows, halo)

    def body(tile, carry):
        real, imag = load_tile(spec_x, blocks, tile, rows)
        row = lax.broadcasted_iota(jnp.int32, (8, LANES), 0)
        sign = jnp.where(row % 2 == 0, 1.0, -1.0)
        window_re = [real[0]] + [real[i] - sign * imag[i - 1] for i in range(1, blocks)]
        window_im = [imag[0]] + [imag[i] + sign * real[i - 1] for i in range(1, blocks)]
        sums = [[(j - lag, j) for j in range(lag, blocks)] for lag in range(blocks)]
        results = mixed_products((window_re, window_im), load_tile(spec_g, blocks, tile, rows), sums, True)
        store_tile(spec_y, 0, results, tile, rows)
        return carry

    lax.fori_loop(0, rows // 8, body, 0)
    for block in range(blocks):
        result = back_to_rows(spec_y[block], inv_hi[...], inv_lo[...])
        out_ref[0, :, pl.ds(block * rows, rows)] = result.T * scale


def receive_kernel(q_ref, k_ref, v_ref, g_ref, taps_ref, in_ref, mixed_ref, grads_ref, padded, extra):
    rows = q_ref.shape[0]
    span = taps_ref.shape[1]
    halo = span - 1
    groups = in_ref.shape[0]
    for which in range(3):
        padded[which, pl.ds(0, 8), :] = jnp.zeros((8, LANES), jnp.float32)
        padded[which, pl.ds(rows, 16), :] = jnp.zeros((16, LANES), jnp.float32)

    def body(group, carry):
        lanes = pl.ds(pl.multiple_of(group * LANES, LANES), LANES)
        filtered = []
        for which, ref in enumerate((q_ref, k_ref, v_ref)):
            padded[which, pl.ds(0, 8), :] = jnp.zeros((8, LANES), jnp.float32)
            padded[which, pl.ds(8, rows), :] = ref[:, lanes].astype(jnp.float32)
            filtered.append(short_filter(padded.at[which], rows, tap_rows(taps_ref, which, lanes)))
        query_f, key_f, value_f = filtered
        cotangent = g_ref[:, lanes].astype(jnp.float32)
        long_conv = in_ref[group, pl.ds(0, rows), :].astype(jnp.float32)
        back = in_ref[group, pl.ds(rows, rows), :].astype(jnp.float32)
        extra[pl.ds(0, in_ref.shape[1] - 2 * rows), :] = in_ref[group, pl.ds(2 * rows, in_ref.shape[1] - 2 * rows), :].astype(jnp.float32)
        mixed = head_rows(extra[pl.ds(0, 8), :], query_f * long_conv, halo)
        mixed_ref[:, lanes] = mixed.astype(jnp.bfloat16)
        grads = (
            cotangent * long_conv,
            head_rows(back[:8], back * value_f, halo),
            head_rows(extra[pl.ds(halo, 8), :], back * key_f, halo),
        )
        for which, grad in enumerate(grads):
            padded[which, pl.ds(0, rows), :] = grad.astype(jnp.bfloat16).astype(jnp.float32)
            padded[which, pl.ds(rows, halo), :] = extra[pl.ds((2 + which) * halo, halo), :]
            weights = tap_rows(taps_ref, which, lanes)
            running = weights[0] * padded[which, pl.ds(0, rows), :]
            for offset in range(1, span):
                running = running + weights[offset] * padded[which, pl.ds(offset, rows), :]
            grads_ref[which, :, lanes] = running.astype(jnp.bfloat16)
        return carry

    lax.fori_loop(0, groups, body, 0)


def in_vmem(kernel, out_shape, scratch, args):
    whole = pl.BlockSpec(memory_space=pltpu.VMEM)
    single = not isinstance(out_shape, tuple)
    return pl.pallas_call(
        kernel,
        out_shape=out_shape,
        in_specs=[whole] * len(args),
        out_specs=whole if single else (whole,) * len(out_shape),
        scratch_shapes=[pltpu.VMEM(shape, jnp.float32) for shape in scratch],
        compiler_params=pltpu.CompilerParams(vmem_limit_bytes=VMEM_BYTES),
    )(*args)


def block_shards(query_proj, key_proj, value_proj, short_taps, long_filter, grad_mixed):
    rows, channels = query_proj.shape
    blocks = lax.axis_size("context")
    halo = short_taps.shape[1] - 1
    seq_len = rows * blocks
    window_hi, window_lo, doubled, inv_hi, inv_lo = [jnp.asarray(t) for t in block_tables(rows)]
    edge_rows = round_up(5 * halo, 16)
    parcel = jax.ShapeDtypeStruct((blocks, 2 * rows + edge_rows, LANES), jnp.bfloat16)
    spectra = (blocks, 2 * rows, LANES)
    own = lax.dynamic_slice_in_dim(short_taps, lax.axis_index("context") * LANES, LANES, axis=2)

    sent = in_vmem(
        send_kernel,
        parcel,
        [(3, rows + 8, LANES), (edge_rows, LANES)],
        (query_proj, key_proj, value_proj, grad_mixed, short_taps),
    )
    arrived = lax.all_to_all(sent, "context", split_axis=0, concat_axis=0, tiled=True)
    spec_h = in_vmem(
        filter_kernel,
        jax.ShapeDtypeStruct(spectra, jnp.float32),
        [],
        (long_filter[0], window_hi, window_lo),
    )
    repair = [(blocks, edge_rows, LANES), (3, blocks, 24, LANES)]
    results = in_vmem(
        convolve_kernel,
        parcel,
        repair + [spectra, spectra, (blocks, 2 * rows, 2 * LANES), (blocks, edge_rows, LANES)],
        (arrived, own, spec_h, doubled, inv_hi, inv_lo),
    )
    returned = lax.all_to_all(results, "context", split_axis=0, concat_axis=0, tiled=True)
    filter_grad = in_vmem(
        functools.partial(correlate_kernel, 1.0 / math.sqrt(seq_len)),
        jax.ShapeDtypeStruct(long_filter.shape, jnp.float32),
        repair + [spectra, spectra, spectra],
        (arrived, own, doubled, inv_hi, inv_lo),
    )
    mixed_out, input_grads = in_vmem(
        receive_kernel,
        (
            jax.ShapeDtypeStruct((rows, channels), jnp.bfloat16),
            jax.ShapeDtypeStruct((3, rows, channels), jnp.bfloat16),
        ),
        [(3, rows + 16, LANES), (edge_rows + 8, LANES)],
        (query_proj, key_proj, value_proj, grad_mixed, short_taps, returned),
    )
    return (mixed_out, input_grads, filter_grad)


def shards(query_proj, key_proj, value_proj, short_taps, long_filter, grad_mixed):
    rows, channels = query_proj.shape
    halo = short_taps.shape[1] - 1
    fits = channels == lax.axis_size("context") * LANES and rows % 128 == 0 and halo <= 8
    chosen = block_shards if fits else general_shards
    return chosen(query_proj, key_proj, value_proj, short_taps, long_filter, grad_mixed)


def solution(mesh):
    return jax.shard_map(
        shards,
        mesh=mesh,
        in_specs=(
            P("context", "tensor"),
            P("context", "tensor"),
            P("context", "tensor"),
            P(None, None, "tensor"),
            P("tensor", "context", None),
            P("context", "tensor"),
        ),
        out_specs=(
            P("context", "tensor"),
            P(None, "context", "tensor"),
            P("tensor", "context", None),
        ),
        check_vma=False,
    )
```

```python
import functools
import math

import jax
import jax.numpy as jnp
import numpy as np
from jax import lax
from jax.experimental import pallas as pl
from jax.experimental.pallas import tpu as pltpu
from jax.sharding import PartitionSpec as P

precise = lax.Precision.HIGHEST


def from_behind(value, axis, steps):
    count = lax.axis_size(axis)
    first, last = (max(0, -steps), min(count, count - steps))
    return lax.ppermute(value, axis, [(source, source + steps) for source in range(first, last)])


def build_tables(blocks, tok_rows):
    outer_len = 2 * blocks
    full_len = outer_len * tok_rows
    k_one = jnp.arange(outer_len, dtype=jnp.int32)
    n_one = jnp.arange(blocks, dtype=jnp.int32)
    position = jnp.arange(tok_rows, dtype=jnp.int32)
    first_idx = k_one[:, None] * n_one[None, :] % outer_len
    first_angle = -2.0 * math.pi / outer_len * first_idx.astype(jnp.float32)
    second = position[:, None] * position[None, :] % tok_rows
    second_angle = -2.0 * math.pi / tok_rows * second.astype(jnp.float32)
    twist_idx = k_one[:, None] * position[None, :] % full_len
    twist_angle = -2.0 * math.pi / full_len * twist_idx.astype(jnp.float32)
    return (
        jnp.cos(first_angle),
        jnp.sin(first_angle),
        jnp.cos(second_angle),
        jnp.sin(second_angle),
        jnp.cos(twist_angle),
        jnp.sin(twist_angle),
    )


def transform(signal, tables):
    cos_first, sin_first, cos_second, sin_second, cos_twist, sin_twist = tables
    first_re = jnp.einsum("kn,gnm->gkm", cos_first, signal, precision=precise)
    first_im = jnp.einsum("kn,gnm->gkm", sin_first, signal, precision=precise)
    mid_re = first_re * cos_twist - first_im * sin_twist
    mid_im = first_re * sin_twist + first_im * cos_twist
    out_re = jnp.einsum("gkn,nm->gkm", mid_re, cos_second, precision=precise) - jnp.einsum(
        "gkn,nm->gkm", mid_im, sin_second, precision=precise
    )
    out_im = jnp.einsum("gkn,nm->gkm", mid_re, sin_second, precision=precise) + jnp.einsum(
        "gkn,nm->gkm", mid_im, cos_second, precision=precise
    )
    return (out_re, out_im)


def inverse(spec_re, spec_im, tables):
    cos_first, sin_first, cos_second, sin_second, cos_twist, sin_twist = tables
    full_len = cos_first.shape[0] * cos_second.shape[0]
    mid_re = jnp.einsum("gkn,nm->gkm", spec_re, cos_second, precision=precise) + jnp.einsum(
        "gkn,nm->gkm", spec_im, sin_second, precision=precise
    )
    mid_im = jnp.einsum("gkn,nm->gkm", spec_im, cos_second, precision=precise) - jnp.einsum(
        "gkn,nm->gkm", spec_re, sin_second, precision=precise
    )
    turn_re = mid_re * cos_twist + mid_im * sin_twist
    turn_im = mid_im * cos_twist - mid_re * sin_twist
    result = jnp.einsum("kn,gkm->gnm", cos_first, turn_re, precision=precise) + jnp.einsum(
        "kn,gkm->gnm", sin_first, turn_im, precision=precise
    )
    return result * (1.0 / full_len)


def causal_taps(series, preceding, tap_weights):
    tok_rows = series.shape[0]
    span = tap_weights.shape[0]
    joined = jnp.concatenate([preceding, series], axis=0).astype(jnp.float32)
    running = jnp.zeros(series.shape, jnp.float32)
    for offset in range(span):
        first_row = span - 1 - offset
        running = running + tap_weights[offset][None, :] * joined[first_row : first_row + tok_rows]
    return running


def reverse_taps(series, following, tap_weights):
    tok_rows = series.shape[0]
    span = tap_weights.shape[0]
    joined = jnp.concatenate([series, following], axis=0).astype(jnp.float32)
    running = jnp.zeros(series.shape, jnp.float32)
    for offset in range(span):
        running = running + tap_weights[offset][None, :] * joined[offset : offset + tok_rows]
    return running


def general_shards(query_proj, key_proj, value_proj, short_taps, long_filter, grad_mixed):
    tok_rows, channels = query_proj.shape
    blocks = lax.axis_size("context")
    halo_rows = short_taps.shape[1] - 1
    per_device = channels // blocks
    seq_len = tok_rows * blocks
    tables = build_tables(blocks, tok_rows)
    preceding = from_behind(
        (
            query_proj[tok_rows - halo_rows :],
            key_proj[tok_rows - halo_rows :],
            value_proj[tok_rows - halo_rows :],
        ),
        "context",
        1,
    )
    query_f = causal_taps(query_proj, preceding[0], short_taps[0])
    key_f = causal_taps(key_proj, preceding[1], short_taps[1])
    value_f = causal_taps(value_proj, preceding[2], short_taps[2])
    gated_prod = (key_f * value_f).astype(jnp.bfloat16)
    grad_f = grad_mixed.astype(jnp.float32)
    grad_long = (grad_f * query_f).astype(jnp.bfloat16)

    def to_spectrum(series):
        arranged = series.T.reshape(blocks, per_device, tok_rows)
        received = lax.all_to_all(arranged, "context", split_axis=0, concat_axis=2, tiled=True)
        item_count = received.shape[1]
        signal = received.reshape(item_count, blocks, tok_rows).astype(jnp.float32)
        return transform(signal, tables)

    def to_token_rows(spatial):
        arrived = lax.all_to_all(spatial, "context", split_axis=1, concat_axis=0, tiled=True)
        return arrived.reshape(channels, tok_rows).T

    gate_re, gate_im = to_spectrum(gated_prod)
    filter_re, filter_im = transform(long_filter.reshape(per_device, blocks, tok_rows), tables)
    long_spatial = inverse(
        gate_re * filter_re - gate_im * filter_im, gate_re * filter_im + gate_im * filter_re, tables
    ).astype(jnp.bfloat16)
    long_conv = to_token_rows(long_spatial)
    long_f = long_conv.astype(jnp.float32)
    mixed_out = (query_f * long_f).astype(jnp.bfloat16)
    grad_query_f = (grad_f * long_f).astype(jnp.bfloat16)
    grad_after = lax.optimization_barrier((grad_long, long_conv))[0]
    grad_re, grad_im = to_spectrum(grad_after)
    back_spatial = inverse(
        filter_re * grad_re + filter_im * grad_im, filter_re * grad_im - filter_im * grad_re, tables
    ).astype(jnp.bfloat16)
    corr_spatial = inverse(
        gate_re * grad_re + gate_im * grad_im, gate_re * grad_im - gate_im * grad_re, tables
    )
    grad_gated = to_token_rows(back_spatial).astype(jnp.float32)
    grad_key_f = (grad_gated * value_f).astype(jnp.bfloat16)
    grad_value_f = (grad_gated * key_f).astype(jnp.bfloat16)
    following = from_behind(
        (grad_query_f[:halo_rows], grad_key_f[:halo_rows], grad_value_f[:halo_rows]), "context", -1
    )
    input_grads = jnp.stack(
        [
            reverse_taps(grad_query_f, following[0], short_taps[0]),
            reverse_taps(grad_key_f, following[1], short_taps[1]),
            reverse_taps(grad_value_f, following[2], short_taps[2]),
        ]
    ).astype(jnp.bfloat16)
    filter_grad = (corr_spatial * (1.0 / math.sqrt(seq_len))).reshape(1, per_device, seq_len)
    return (mixed_out, input_grads, filter_grad)


LANES = 128
VMEM_BYTES = 48 * 1024 * 1024


def split_bf16(table):
    high = table.astype(jnp.bfloat16)
    low = (table - high.astype(np.float64)).astype(jnp.bfloat16)
    return (high, low)


@functools.cache
def block_tables(rows):
    bins = np.pi * (np.arange(rows) + 0.5)[:, None] / rows
    lag = np.arange(-rows, rows)[None, :]
    window = np.concatenate([np.cos(bins * lag), -np.sin(bins * lag)], axis=0)
    window_hi, window_lo = split_bf16(window)
    doubled = np.concatenate([window_hi[:, rows:], window_lo[:, rows:]], axis=1)
    inv_hi, inv_lo = split_bf16(window[:, rows:].T / rows)
    return (window_hi, window_lo, doubled, inv_hi, inv_lo)


def round_up(count, unit):
    return (count + unit - 1) // unit * unit


def head_rows(fresh, whole, halo):
    row = lax.broadcasted_iota(jnp.int32, fresh.shape, 0)
    return jnp.concatenate([jnp.where(row < halo, fresh, whole[:8]), whole[8:]], axis=0)


def tap_rows(taps_ref, which, lanes):
    return [taps_ref[which, pl.ds(offset, 1), lanes] for offset in range(taps_ref.shape[1])]


def short_filter(padded, rows, weights):
    running = weights[0] * padded[pl.ds(8, rows), :]
    for offset in range(1, len(weights)):
        running = running + weights[offset] * padded[pl.ds(8 - offset, rows), :]
    return running


def send_kernel(order, q_ref, k_ref, v_ref, g_ref, taps_ref, h_ref, hi_ref, lo_ref, *refs):
    count = len(order)
    outs = refs[:count]
    filtered_ref, own_ref, h_here, hi_here, lo_here = refs[count : count + 5]
    landed, taps, padded, extra, arrivals, kept = refs[count + 5 :]
    me = lax.axis_index("context")
    rows = q_ref.shape[0]
    halo = taps_ref.shape[1] - 1

    def lanes_of(place):
        return pl.ds(pl.multiple_of((me ^ order[place]) * LANES, LANES), LANES)

    def fetches(place):
        lanes = lanes_of(place)
        copies = [
            pltpu.make_async_copy(
                taps_ref.at[:, :, lanes], taps.at[place], arrivals.at[place, 4]
            )
        ]
        for which, ref in enumerate((q_ref, k_ref, v_ref, g_ref)):
            copies.append(
                pltpu.make_async_copy(
                    ref.at[:, lanes], landed.at[place, which], arrivals.at[place, which]
                )
            )
        return copies

    keeps = [
        pltpu.make_async_copy(source, target, kept.at[index])
        for index, (source, target) in enumerate(
            ((h_ref, h_here), (hi_ref, hi_here), (lo_ref, lo_here))
        )
    ]
    for place in range(count):
        for copy in fetches(place):
            copy.start()
    for copy in keeps:
        copy.start()
    for place in range(count):
        slot = place % padded.shape[0]
        out_ref = outs[place]
        padded[slot, :, pl.ds(0, 8), :] = jnp.zeros((3, 8, LANES), jnp.float32)
        extra[slot, pl.ds(5 * halo, extra.shape[1] - 5 * halo), :] = jnp.zeros(
            (extra.shape[1] - 5 * halo, LANES), jnp.float32
        )
        for copy in fetches(place):
            copy.wait()
        filtered = []
        for which in range(3):
            padded[slot, which, pl.ds(8, rows), :] = landed[place, which].astype(jnp.float32)
            weights = tap_rows(taps.at[place], which, pl.ds(0, LANES))
            result = short_filter(padded.at[slot, which], rows, weights)
            filtered_ref[which, place] = result
            filtered.append(result)
        query_f, key_f, value_f = filtered
        cotangent = landed[place, 3].astype(jnp.float32)
        gated = head_rows(padded[slot, 1, pl.ds(8, 8), :], key_f * value_f, halo)
        grad_long = head_rows(cotangent[:8], cotangent * query_f, halo)
        out_ref[pl.ds(0, rows), :] = gated.astype(jnp.bfloat16)
        out_ref[pl.ds(rows, rows), :] = grad_long.astype(jnp.bfloat16)
        pieces = ((1, rows - halo), (2, 0), (2, rows - halo), (0, 0), (0, rows - halo))
        for position, (which, first) in enumerate(pieces):
            extra[slot, pl.ds(position * halo, halo), :] = padded[slot, which, pl.ds(8 + first, halo), :]
        out_ref[pl.ds(2 * rows, extra.shape[1]), :] = extra[slot].astype(jnp.bfloat16)
    own_ref[...] = taps[order.index(0)]
    for copy in keeps:
        copy.wait()


def gather_heads(order, in_refs, edges, firsts, rows):
    me = lax.axis_index("context")
    for mask, in_ref in zip(order, in_refs):
        block = me ^ mask
        edges[block] = in_ref[pl.ds(2 * rows, edges.shape[1]), :].astype(jnp.float32)
        firsts[block, 0] = in_ref[pl.ds(0, 16), :].astype(jnp.float32)[:8]
        firsts[block, 1] = in_ref[pl.ds(rows, 16), :].astype(jnp.float32)[:8]


def repair_heads(taps_ref, edges, firsts, joined, heads):
    blocks = edges.shape[0]
    span = taps_ref.shape[1]
    halo = span - 1
    joined[...] = jnp.zeros(joined.shape, jnp.float32)
    for block in range(blocks):
        joined[1, block, pl.ds(halo, 8), :] = firsts[block, 0]
        joined[2, block, pl.ds(halo, halo), :] = edges[block, pl.ds(halo, halo), :]
        joined[0, block, pl.ds(halo, halo), :] = edges[block, pl.ds(3 * halo, halo), :]
        if block > 0:
            for which, place in ((1, 0), (2, 2), (0, 4)):
                joined[which, block, pl.ds(0, halo), :] = edges[block - 1, pl.ds(place * halo, halo), :]
        filtered = []
        for which in range(3):
            running = jnp.zeros((8, LANES), jnp.float32)
            for offset in range(span):
                weight = taps_ref[which, pl.ds(offset, 1), :]
                running = running + weight * joined[which, block, pl.ds(halo - offset, 8), :]
            filtered.append(running)
            heads[block, which] = running
        cotangent = firsts[block, 1]
        heads[block, 3] = cotangent
        heads[block, 4] = filtered[1] * filtered[2]
        heads[block, 5] = cotangent * filtered[0]


def to_spectra(order, in_refs, heads, doubled, spec_x, spec_g, rows, halo):
    me = lax.axis_index("context")
    for mask, in_ref in zip(order, in_refs):
        block = me ^ mask
        parts = []
        for first, place in ((0, 4), (rows, 5)):
            head = in_ref[pl.ds(first, 16), :].astype(jnp.float32)
            head = head_rows(heads[block, place], head, halo).astype(jnp.bfloat16)
            parts.append(jnp.concatenate([head, in_ref[pl.ds(first + 16, rows - 16), :]], axis=0))
        pair = jnp.concatenate(parts, axis=1)
        spectrum = jnp.dot(
            doubled, jnp.concatenate([pair, pair], axis=0), preferred_element_type=jnp.float32
        )
        spec_x[block] = spectrum[:, :LANES]
        spec_g[block] = spectrum[:, LANES:]


def filter_kernel(parcel_ref, h_ref, window_hi, window_lo, out_ref):
    del parcel_ref
    blocks, two_rows, _ = out_ref.shape
    rows = two_rows // 2
    for block in range(blocks):
        here = h_ref[:, pl.ds(block * rows, rows)]
        if block > 0:
            before = h_ref[:, pl.ds((block - 1) * rows, rows)]
        else:
            before = jnp.zeros_like(here)
        signal = jnp.concatenate([before, here], axis=1)
        high = signal.astype(jnp.bfloat16)
        low = (signal - high.astype(jnp.float32)).astype(jnp.bfloat16)

        def product(table, values):
            return lax.dot_general(
                table, values, (((1,), (1,)), ((), ())), preferred_element_type=jnp.float32
            )

        out_ref[block] = (
            product(window_hi[...], high) + product(window_lo[...], high) + product(window_hi[...], low)
        )


def load_tile(ref, count, tile, bins):
    real = [ref[index, pl.ds(pl.multiple_of(tile * 8, 8), 8), :] for index in range(count)]
    imag = [ref[index, pl.ds(pl.multiple_of(bins + tile * 8, 8), 8), :] for index in range(count)]
    return (real, imag)


def mixed_products(left, right, sums, conjugate):
    (left_re, left_im), (right_re, right_im) = left, right
    results = []
    for pairs in sums:
        total_re, total_im = None, None
        for one, two in pairs:
            a, b, c, d = left_re[one], left_im[one], right_re[two], right_im[two]
            if conjugate:
                real, imag = a * c + b * d, a * d - b * c
            else:
                real, imag = a * c - b * d, a * d + b * c
            total_re = real if total_re is None else total_re + real
            total_im = imag if total_im is None else total_im + imag
        results.append((total_re, total_im))
    return results


def back_to_rows(spectrum, inv_hi, inv_lo):
    high = spectrum.astype(jnp.bfloat16)
    low = (spectrum - high.astype(jnp.float32)).astype(jnp.bfloat16)
    return (
        jnp.dot(inv_hi, high, preferred_element_type=jnp.float32)
        + jnp.dot(inv_lo, high, preferred_element_type=jnp.float32)
        + jnp.dot(inv_hi, low, preferred_element_type=jnp.float32)
    )


def store_tile(ref, first_lane, results, tile, bins):
    lanes = pl.ds(first_lane, LANES)
    for index, (real, imag) in enumerate(results):
        ref[index, pl.ds(pl.multiple_of(tile * 8, 8), 8), lanes] = real
        ref[index, pl.ds(pl.multiple_of(bins + tile * 8, 8), 8), lanes] = imag


def convolve_kernel(order, taps_ref, spec_h, doubled, inv_hi, inv_lo, *refs):
    count = len(order)
    in_refs, out_refs = refs[:count], refs[count : 2 * count]
    spec_x, spec_g, edges, firsts, joined, heads, spec_y, extra = refs[2 * count :]
    me = lax.axis_index("context")
    rows = inv_hi.shape[0]
    halo = taps_ref.shape[1] - 1
    gather_heads(order, in_refs, edges, firsts, rows)
    repair_heads(taps_ref, edges, firsts, joined, heads)
    to_spectra(order, in_refs, heads, doubled[...], spec_x, spec_g, rows, halo)

    def body(tile, carry):
        filt = load_tile(spec_h, count, tile, rows)
        sums = [[(i - j, j) for j in range(i + 1)] for i in range(count)]
        results = mixed_products(filt, load_tile(spec_x, count, tile, rows), sums, False)
        store_tile(spec_y, 0, results, tile, rows)
        sums = [[(j - i, j) for j in range(i, count)] for i in range(count)]
        results = mixed_products(filt, load_tile(spec_g, count, tile, rows), sums, True)
        store_tile(spec_y, LANES, results, tile, rows)
        return carry

    lax.fori_loop(0, rows // 8, body, 0)
    extra[...] = jnp.zeros(extra.shape, jnp.float32)
    for mask, out_ref in zip(order, out_refs):
        block = me ^ mask
        query_f, key_f, value_f, cotangent = [heads[block, which] for which in range(4)]
        both = back_to_rows(spec_y[block], inv_hi[...], inv_lo[...]).astype(jnp.bfloat16)
        out_ref[pl.ds(0, rows), :] = both[:, :LANES]
        head = both[:16].astype(jnp.float32)
        long_head, back_head = head[:8, :LANES], head[:8, LANES:]
        grad_key, grad_value = back_head * value_f, back_head * key_f
        back = head_rows(grad_key, head[:, LANES:], halo).astype(jnp.bfloat16)
        out_ref[pl.ds(rows, rows), :] = jnp.concatenate([back, both[16:, LANES:]], axis=0)
        own = (query_f * long_head, grad_value)
        following = (cotangent * long_head, grad_key, grad_value)
        for place, value in enumerate(own):
            extra[block + 1, pl.ds(place * halo, halo), :] = value[:halo]
        for place, value in enumerate(following):
            extra[block, pl.ds((2 + place) * halo, halo), :] = value[:halo]
    for mask, out_ref in zip(order, out_refs):
        block = me ^ mask
        out_ref[pl.ds(2 * rows, extra.shape[1]), :] = extra[block + 1].astype(jnp.bfloat16)


def correlate_kernel(scale, spec_x, spec_g, inv_hi, inv_lo, out_ref, spec_y):
    count = spec_x.shape[0]
    rows = inv_hi.shape[0]

    def body(tile, carry):
        real, imag = load_tile(spec_x, count, tile, rows)
        row = lax.broadcasted_iota(jnp.int32, (8, LANES), 0)
        sign = jnp.where(row % 2 == 0, 1.0, -1.0)
        window_re = [real[0]] + [real[i] - sign * imag[i - 1] for i in range(1, count)]
        window_im = [imag[0]] + [imag[i] + sign * real[i - 1] for i in range(1, count)]
        sums = [[(j - lag, j) for j in range(lag, count)] for lag in range(count)]
        results = mixed_products((window_re, window_im), load_tile(spec_g, count, tile, rows), sums, True)
        store_tile(spec_y, 0, results, tile, rows)
        return carry

    lax.fori_loop(0, rows // 8, body, 0)
    for block in range(count):
        result = back_to_rows(spec_y[block], inv_hi[...], inv_lo[...])
        out_ref[0, :, pl.ds(block * rows, rows)] = result.T * scale


def receive_kernel(places, order, g_ref, taps_ref, filtered_ref, *refs):
    count = len(places)
    in_refs = refs[:count]
    mixed_ref, grads_ref, padded, extra, leaving, departures = refs[-6:]
    me = lax.axis_index("context")
    rows = g_ref.shape[0]
    span = taps_ref.shape[1]
    halo = span - 1
    copies = []
    for index, (place, in_ref) in enumerate(zip(places, in_refs)):
        lanes = pl.ds(pl.multiple_of((me ^ order[place]) * LANES, LANES), LANES)
        slot = index % padded.shape[0]
        edge_rows = in_ref.shape[0] - 2 * rows
        query_f, key_f, value_f = [filtered_ref[which, place] for which in range(3)]
        cotangent = g_ref[:, lanes].astype(jnp.float32)
        long_conv = in_ref[pl.ds(0, rows), :].astype(jnp.float32)
        back = in_ref[pl.ds(rows, rows), :].astype(jnp.float32)
        extra[slot, pl.ds(0, edge_rows), :] = in_ref[pl.ds(2 * rows, edge_rows), :].astype(jnp.float32)
        mixed = head_rows(extra[slot, pl.ds(0, 8), :], query_f * long_conv, halo)
        leaving[index, 3] = mixed.astype(jnp.bfloat16)
        copies.append(
            pltpu.make_async_copy(leaving.at[index, 3], mixed_ref.at[:, lanes], departures.at[index, 3])
        )
        copies[-1].start()
        grads = (
            cotangent * long_conv,
            head_rows(back[:8], back * value_f, halo),
            head_rows(extra[slot, pl.ds(halo, 8), :], back * key_f, halo),
        )
        for which, grad in enumerate(grads):
            padded[slot, which, pl.ds(0, rows), :] = grad.astype(jnp.bfloat16).astype(jnp.float32)
            padded[slot, which, pl.ds(rows, halo), :] = extra[slot, pl.ds((2 + which) * halo, halo), :]
            weights = tap_rows(taps_ref, which, lanes)
            running = weights[0] * padded[slot, which, pl.ds(0, rows), :]
            for offset in range(1, span):
                running = running + weights[offset] * padded[slot, which, pl.ds(offset, rows), :]
            leaving[index, which] = running.astype(jnp.bfloat16)
            copies.append(
                pltpu.make_async_copy(
                    leaving.at[index, which], grads_ref.at[which, :, lanes], departures.at[index, which]
                )
            )
            copies[-1].start()
    for copy in copies:
        copy.wait()


def on_device(kernel, out_shape, scratch, args, in_hbm=0, pin=True, updated=0):
    whole = pl.BlockSpec(memory_space=pltpu.VMEM)
    outside = pl.BlockSpec(memory_space=pltpu.HBM if pin else pl.ANY)
    last = len(args) - updated
    args = [
        pltpu.with_memory_space_constraint(arg, pltpu.HBM) if pin and place < in_hbm else arg
        for place, arg in enumerate(args)
    ]
    return pl.pallas_call(
        kernel,
        out_shape=out_shape,
        in_specs=[outside if place < in_hbm or place >= last else whole for place in range(len(args))],
        out_specs=jax.tree.map(
            lambda out: whole if isinstance(out, jax.ShapeDtypeStruct) else outside, out_shape
        ),
        input_output_aliases={last + place: place for place in range(updated)},
        scratch_shapes=[
            pltpu.VMEM(shape, jnp.float32) if isinstance(shape, tuple) else shape for shape in scratch
        ],
        compiler_params=pltpu.CompilerParams(vmem_limit_bytes=VMEM_BYTES),
    )(*args)


def exchange(order, parcels):
    count = lax.axis_size("context")
    return [
        parcel if mask == 0 else lax.ppermute(parcel, "context", [(i, i ^ mask) for i in range(count)])
        for mask, parcel in zip(order, parcels)
    ]


def block_shards(query_proj, key_proj, value_proj, short_taps, long_filter, grad_mixed):
    rows, channels = query_proj.shape
    blocks = lax.axis_size("context")
    halo = short_taps.shape[1] - 1
    seq_len = rows * blocks
    window_hi, window_lo, doubled, inv_hi, inv_lo = [jnp.asarray(t) for t in block_tables(rows)]
    edge_rows = round_up(5 * halo, 16)
    order = sorted(range(blocks), key=lambda mask: (mask == 0, -(mask >> 1).bit_count()))
    parcels = [jax.ShapeDtypeStruct((2 * rows + edge_rows, LANES), jnp.bfloat16)] * blocks
    spectra = (blocks, 2 * rows, LANES)
    own_taps = (*short_taps.shape[:2], LANES)
    kept = (long_filter[0], window_hi, window_lo)

    *sent, filtered, own, filter_here, hi_here, lo_here = on_device(
        functools.partial(send_kernel, order),
        parcels
        + [
            jax.ShapeDtypeStruct((3, blocks, rows, LANES), jnp.float32),
            jax.ShapeDtypeStruct(own_taps, jnp.float32),
        ]
        + [jax.ShapeDtypeStruct(value.shape, value.dtype) for value in kept],
        [
            pltpu.VMEM((blocks, 4, rows, LANES), jnp.bfloat16),
            (blocks, *own_taps),
            (2, 3, rows + 8, LANES),
            (2, edge_rows, LANES),
            pltpu.SemaphoreType.DMA((blocks, 5)),
            pltpu.SemaphoreType.DMA((len(kept),)),
        ],
        (query_proj, key_proj, value_proj, grad_mixed, short_taps, *kept),
        in_hbm=8,
    )
    arrived = exchange(order, sent)
    spec_h = on_device(
        filter_kernel,
        jax.ShapeDtypeStruct(spectra, jnp.float32),
        [],
        (arrived[2], filter_here, hi_here, lo_here),
        in_hbm=1,
        pin=False,
    )
    *results, spec_x, spec_g = on_device(
        functools.partial(convolve_kernel, order),
        parcels + [jax.ShapeDtypeStruct(spectra, jnp.float32)] * 2,
        [
            (blocks, edge_rows, LANES),
            (blocks, 2, 8, LANES),
            (3, blocks, 24, LANES),
            (blocks, 6, 8, LANES),
            (blocks, 2 * rows, 2 * LANES),
            (blocks + 1, edge_rows, LANES),
        ],
        (own, spec_h, doubled, inv_hi, inv_lo, *arrived),
    )
    returned = exchange(order, results)
    filter_grad = on_device(
        functools.partial(correlate_kernel, 1.0 / math.sqrt(seq_len)),
        jax.ShapeDtypeStruct(long_filter.shape, jnp.float32),
        [spectra],
        (spec_x, spec_g, inv_hi, inv_lo),
    )
    finished = ()
    halves = (range(blocks // 2), range(blocks // 2, blocks))
    for places in halves:
        finished = on_device(
            functools.partial(receive_kernel, places, order),
            (
                pltpu.HBM((rows, channels), jnp.bfloat16),
                pltpu.HBM((3, rows, channels), jnp.bfloat16),
            ),
            [
                (2, 3, rows + 16, LANES),
                (2, edge_rows + 8, LANES),
                pltpu.VMEM((len(places), 4, rows, LANES), jnp.bfloat16),
                pltpu.SemaphoreType.DMA((len(places), 4)),
            ],
            (grad_mixed, short_taps, filtered, *(returned[place] for place in places), *finished),
            updated=len(finished),
        )
    mixed_out, input_grads = finished
    return (mixed_out, input_grads, filter_grad)


def shards(query_proj, key_proj, value_proj, short_taps, long_filter, grad_mixed):
    rows, channels = query_proj.shape
    halo = short_taps.shape[1] - 1
    blocks = lax.axis_size("context")
    power_of_two = blocks & (blocks - 1) == 0
    fits = power_of_two and channels == blocks * LANES and rows % 128 == 0 and halo <= 8
    chosen = block_shards if fits else general_shards
    return chosen(query_proj, key_proj, value_proj, short_taps, long_filter, grad_mixed)


def solution(mesh):
    return jax.shard_map(
        shards,
        mesh=mesh,
        in_specs=(
            P("context", "tensor"),
            P("context", "tensor"),
            P("context", "tensor"),
            P(None, None, "tensor"),
            P("tensor", "context", None),
            P("context", "tensor"),
        ),
        out_specs=(
            P("context", "tensor"),
            P(None, "context", "tensor"),
            P("tensor", "context", None),
        ),
        check_vma=False,
    )
```

```python
import functools
import math

import jax
import jax.numpy as jnp
import numpy as np
from jax import lax
from jax.experimental import pallas as pl
from jax.experimental.pallas import tpu as pltpu
from jax.sharding import PartitionSpec as P

precise = lax.Precision.HIGHEST


def from_behind(value, axis, steps):
    count = lax.axis_size(axis)
    first, last = (max(0, -steps), min(count, count - steps))
    return lax.ppermute(value, axis, [(source, source + steps) for source in range(first, last)])


def build_tables(blocks, tok_rows):
    outer_len = 2 * blocks
    full_len = outer_len * tok_rows
    k_one = jnp.arange(outer_len, dtype=jnp.int32)
    n_one = jnp.arange(blocks, dtype=jnp.int32)
    position = jnp.arange(tok_rows, dtype=jnp.int32)
    first_idx = k_one[:, None] * n_one[None, :] % outer_len
    first_angle = -2.0 * math.pi / outer_len * first_idx.astype(jnp.float32)
    second = position[:, None] * position[None, :] % tok_rows
    second_angle = -2.0 * math.pi / tok_rows * second.astype(jnp.float32)
    twist_idx = k_one[:, None] * position[None, :] % full_len
    twist_angle = -2.0 * math.pi / full_len * twist_idx.astype(jnp.float32)
    return (
        jnp.cos(first_angle),
        jnp.sin(first_angle),
        jnp.cos(second_angle),
        jnp.sin(second_angle),
        jnp.cos(twist_angle),
        jnp.sin(twist_angle),
    )


def transform(signal, tables):
    cos_first, sin_first, cos_second, sin_second, cos_twist, sin_twist = tables
    first_re = jnp.einsum("kn,gnm->gkm", cos_first, signal, precision=precise)
    first_im = jnp.einsum("kn,gnm->gkm", sin_first, signal, precision=precise)
    mid_re = first_re * cos_twist - first_im * sin_twist
    mid_im = first_re * sin_twist + first_im * cos_twist
    out_re = jnp.einsum("gkn,nm->gkm", mid_re, cos_second, precision=precise) - jnp.einsum(
        "gkn,nm->gkm", mid_im, sin_second, precision=precise
    )
    out_im = jnp.einsum("gkn,nm->gkm", mid_re, sin_second, precision=precise) + jnp.einsum(
        "gkn,nm->gkm", mid_im, cos_second, precision=precise
    )
    return (out_re, out_im)


def inverse(spec_re, spec_im, tables):
    cos_first, sin_first, cos_second, sin_second, cos_twist, sin_twist = tables
    full_len = cos_first.shape[0] * cos_second.shape[0]
    mid_re = jnp.einsum("gkn,nm->gkm", spec_re, cos_second, precision=precise) + jnp.einsum(
        "gkn,nm->gkm", spec_im, sin_second, precision=precise
    )
    mid_im = jnp.einsum("gkn,nm->gkm", spec_im, cos_second, precision=precise) - jnp.einsum(
        "gkn,nm->gkm", spec_re, sin_second, precision=precise
    )
    turn_re = mid_re * cos_twist + mid_im * sin_twist
    turn_im = mid_im * cos_twist - mid_re * sin_twist
    result = jnp.einsum("kn,gkm->gnm", cos_first, turn_re, precision=precise) + jnp.einsum(
        "kn,gkm->gnm", sin_first, turn_im, precision=precise
    )
    return result * (1.0 / full_len)


def causal_taps(series, preceding, tap_weights):
    tok_rows = series.shape[0]
    span = tap_weights.shape[0]
    joined = jnp.concatenate([preceding, series], axis=0).astype(jnp.float32)
    running = jnp.zeros(series.shape, jnp.float32)
    for offset in range(span):
        first_row = span - 1 - offset
        running = running + tap_weights[offset][None, :] * joined[first_row : first_row + tok_rows]
    return running


def reverse_taps(series, following, tap_weights):
    tok_rows = series.shape[0]
    span = tap_weights.shape[0]
    joined = jnp.concatenate([series, following], axis=0).astype(jnp.float32)
    running = jnp.zeros(series.shape, jnp.float32)
    for offset in range(span):
        running = running + tap_weights[offset][None, :] * joined[offset : offset + tok_rows]
    return running


def general_shards(query_proj, key_proj, value_proj, short_taps, long_filter, grad_mixed):
    tok_rows, channels = query_proj.shape
    blocks = lax.axis_size("context")
    halo_rows = short_taps.shape[1] - 1
    per_device = channels // blocks
    seq_len = tok_rows * blocks
    tables = build_tables(blocks, tok_rows)
    preceding = from_behind(
        (
            query_proj[tok_rows - halo_rows :],
            key_proj[tok_rows - halo_rows :],
            value_proj[tok_rows - halo_rows :],
        ),
        "context",
        1,
    )
    query_f = causal_taps(query_proj, preceding[0], short_taps[0])
    key_f = causal_taps(key_proj, preceding[1], short_taps[1])
    value_f = causal_taps(value_proj, preceding[2], short_taps[2])
    gated_prod = (key_f * value_f).astype(jnp.bfloat16)
    grad_f = grad_mixed.astype(jnp.float32)
    grad_long = (grad_f * query_f).astype(jnp.bfloat16)

    def to_spectrum(series):
        arranged = series.T.reshape(blocks, per_device, tok_rows)
        received = lax.all_to_all(arranged, "context", split_axis=0, concat_axis=2, tiled=True)
        item_count = received.shape[1]
        signal = received.reshape(item_count, blocks, tok_rows).astype(jnp.float32)
        return transform(signal, tables)

    def to_token_rows(spatial):
        arrived = lax.all_to_all(spatial, "context", split_axis=1, concat_axis=0, tiled=True)
        return arrived.reshape(channels, tok_rows).T

    gate_re, gate_im = to_spectrum(gated_prod)
    filter_re, filter_im = transform(long_filter.reshape(per_device, blocks, tok_rows), tables)
    long_spatial = inverse(
        gate_re * filter_re - gate_im * filter_im, gate_re * filter_im + gate_im * filter_re, tables
    ).astype(jnp.bfloat16)
    long_conv = to_token_rows(long_spatial)
    long_f = long_conv.astype(jnp.float32)
    mixed_out = (query_f * long_f).astype(jnp.bfloat16)
    grad_query_f = (grad_f * long_f).astype(jnp.bfloat16)
    grad_after = lax.optimization_barrier((grad_long, long_conv))[0]
    grad_re, grad_im = to_spectrum(grad_after)
    back_spatial = inverse(
        filter_re * grad_re + filter_im * grad_im, filter_re * grad_im - filter_im * grad_re, tables
    ).astype(jnp.bfloat16)
    corr_spatial = inverse(
        gate_re * grad_re + gate_im * grad_im, gate_re * grad_im - gate_im * grad_re, tables
    )
    grad_gated = to_token_rows(back_spatial).astype(jnp.float32)
    grad_key_f = (grad_gated * value_f).astype(jnp.bfloat16)
    grad_value_f = (grad_gated * key_f).astype(jnp.bfloat16)
    following = from_behind(
        (grad_query_f[:halo_rows], grad_key_f[:halo_rows], grad_value_f[:halo_rows]), "context", -1
    )
    input_grads = jnp.stack(
        [
            reverse_taps(grad_query_f, following[0], short_taps[0]),
            reverse_taps(grad_key_f, following[1], short_taps[1]),
            reverse_taps(grad_value_f, following[2], short_taps[2]),
        ]
    ).astype(jnp.bfloat16)
    filter_grad = (corr_spatial * (1.0 / math.sqrt(seq_len))).reshape(1, per_device, seq_len)
    return (mixed_out, input_grads, filter_grad)


LANES = 128
VMEM_BYTES = 48 * 1024 * 1024


def split_bf16(table):
    high = table.astype(jnp.bfloat16)
    low = (table - high.astype(np.float64)).astype(jnp.bfloat16)
    return (high, low)


@functools.cache
def block_tables(rows):
    bins = np.pi * (np.arange(rows) + 0.5)[:, None] / rows
    lag = np.arange(-rows, rows)[None, :]
    window = np.concatenate([np.cos(bins * lag), -np.sin(bins * lag)], axis=0)
    window_hi, window_lo = split_bf16(window)
    doubled = np.concatenate([window_hi[:, rows:], window_lo[:, rows:]], axis=1)
    inv_hi, inv_lo = split_bf16(window[:, rows:].T / rows)
    return (window_hi, window_lo, doubled, inv_hi, inv_lo)


def round_up(count, unit):
    return (count + unit - 1) // unit * unit


def head_rows(fresh, whole, halo):
    row = lax.broadcasted_iota(jnp.int32, fresh.shape, 0)
    return jnp.concatenate([jnp.where(row < halo, fresh, whole[:8]), whole[8:]], axis=0)


def tap_rows(taps_ref, which, lanes):
    return [taps_ref[which, pl.ds(offset, 1), lanes] for offset in range(taps_ref.shape[1])]


def short_filter(padded, rows, weights):
    running = weights[0] * padded[pl.ds(8, rows), :]
    for offset in range(1, len(weights)):
        running = running + weights[offset] * padded[pl.ds(8 - offset, rows), :]
    return running


def send_kernel(order, q_ref, k_ref, v_ref, g_ref, taps_ref, h_ref, hi_ref, lo_ref, *refs):
    count = len(order)
    outs = refs[:count]
    filtered_ref, own_ref, h_here, hi_here, lo_here = refs[count : count + 5]
    landed, taps, padded, extra, arrivals, kept = refs[count + 5 :]
    me = lax.axis_index("context")
    rows = q_ref.shape[0]
    halo = taps_ref.shape[1] - 1

    def lanes_of(place):
        return pl.ds(pl.multiple_of((me ^ order[place]) * LANES, LANES), LANES)

    def fetches(place):
        lanes = lanes_of(place)
        copies = [
            pltpu.make_async_copy(
                taps_ref.at[:, :, lanes], taps.at[place], arrivals.at[place, 4]
            )
        ]
        for which, ref in enumerate((q_ref, k_ref, v_ref, g_ref)):
            copies.append(
                pltpu.make_async_copy(
                    ref.at[:, lanes], landed.at[place, which], arrivals.at[place, which]
                )
            )
        return copies

    keeps = [
        pltpu.make_async_copy(source, target, kept.at[index])
        for index, (source, target) in enumerate(
            ((h_ref, h_here), (hi_ref, hi_here), (lo_ref, lo_here))
        )
    ]
    for place in range(count):
        for copy in fetches(place):
            copy.start()
    for copy in keeps:
        copy.start()
    for place in range(count):
        slot = place % padded.shape[0]
        out_ref = outs[place]
        padded[slot, :, pl.ds(0, 8), :] = jnp.zeros((3, 8, LANES), jnp.float32)
        extra[slot, pl.ds(5 * halo, extra.shape[1] - 5 * halo), :] = jnp.zeros(
            (extra.shape[1] - 5 * halo, LANES), jnp.float32
        )
        for copy in fetches(place):
            copy.wait()
        filtered = []
        for which in range(3):
            padded[slot, which, pl.ds(8, rows), :] = landed[place, which].astype(jnp.float32)
            weights = tap_rows(taps.at[place], which, pl.ds(0, LANES))
            result = short_filter(padded.at[slot, which], rows, weights)
            filtered_ref[which, place] = result
            filtered.append(result)
        query_f, key_f, value_f = filtered
        cotangent = landed[place, 3].astype(jnp.float32)
        gated = head_rows(padded[slot, 1, pl.ds(8, 8), :], key_f * value_f, halo)
        grad_long = head_rows(cotangent[:8], cotangent * query_f, halo)
        out_ref[pl.ds(0, rows), :] = gated.astype(jnp.bfloat16)
        out_ref[pl.ds(rows, rows), :] = grad_long.astype(jnp.bfloat16)
        pieces = ((1, rows - halo), (2, 0), (2, rows - halo), (0, 0), (0, rows - halo))
        for position, (which, first) in enumerate(pieces):
            extra[slot, pl.ds(position * halo, halo), :] = padded[slot, which, pl.ds(8 + first, halo), :]
        out_ref[pl.ds(2 * rows, extra.shape[1]), :] = extra[slot].astype(jnp.bfloat16)
    own_ref[...] = taps[order.index(0)]
    for copy in keeps:
        copy.wait()


def gather_heads(order, in_refs, edges, firsts, rows):
    me = lax.axis_index("context")
    for mask, in_ref in zip(order, in_refs):
        block = me ^ mask
        edges[block] = in_ref[pl.ds(2 * rows, edges.shape[1]), :].astype(jnp.float32)
        firsts[block, 0] = in_ref[pl.ds(0, 16), :].astype(jnp.float32)[:8]
        firsts[block, 1] = in_ref[pl.ds(rows, 16), :].astype(jnp.float32)[:8]


def repair_heads(taps_ref, edges, firsts, joined, heads):
    blocks = edges.shape[0]
    span = taps_ref.shape[1]
    halo = span - 1
    joined[...] = jnp.zeros(joined.shape, jnp.float32)
    for block in range(blocks):
        joined[1, block, pl.ds(halo, 8), :] = firsts[block, 0]
        joined[2, block, pl.ds(halo, halo), :] = edges[block, pl.ds(halo, halo), :]
        joined[0, block, pl.ds(halo, halo), :] = edges[block, pl.ds(3 * halo, halo), :]
        if block > 0:
            for which, place in ((1, 0), (2, 2), (0, 4)):
                joined[which, block, pl.ds(0, halo), :] = edges[block - 1, pl.ds(place * halo, halo), :]
        filtered = []
        for which in range(3):
            running = jnp.zeros((8, LANES), jnp.float32)
            for offset in range(span):
                weight = taps_ref[which, pl.ds(offset, 1), :]
                running = running + weight * joined[which, block, pl.ds(halo - offset, 8), :]
            filtered.append(running)
            heads[block, which] = running
        cotangent = firsts[block, 1]
        heads[block, 3] = cotangent
        heads[block, 4] = filtered[1] * filtered[2]
        heads[block, 5] = cotangent * filtered[0]


def to_spectra(order, in_refs, heads, doubled, spec_x, spec_g, rows, halo):
    me = lax.axis_index("context")
    for mask, in_ref in zip(order, in_refs):
        block = me ^ mask
        parts = []
        for first, place in ((0, 4), (rows, 5)):
            head = in_ref[pl.ds(first, 16), :].astype(jnp.float32)
            head = head_rows(heads[block, place], head, halo).astype(jnp.bfloat16)
            parts.append(jnp.concatenate([head, in_ref[pl.ds(first + 16, rows - 16), :]], axis=0))
        pair = jnp.concatenate(parts, axis=1)
        spectrum = jnp.dot(
            doubled, jnp.concatenate([pair, pair], axis=0), preferred_element_type=jnp.float32
        )
        spec_x[block] = spectrum[:, :LANES]
        spec_g[block] = spectrum[:, LANES:]


def filter_kernel(parcel_ref, h_ref, window_hi, window_lo, out_ref):
    del parcel_ref
    blocks, two_rows, _ = out_ref.shape
    rows = two_rows // 2
    for block in range(blocks):
        here = h_ref[:, pl.ds(block * rows, rows)]
        if block > 0:
            before = h_ref[:, pl.ds((block - 1) * rows, rows)]
        else:
            before = jnp.zeros_like(here)
        signal = jnp.concatenate([before, here], axis=1)
        high = signal.astype(jnp.bfloat16)
        low = (signal - high.astype(jnp.float32)).astype(jnp.bfloat16)

        def product(table, values):
            return lax.dot_general(
                table, values, (((1,), (1,)), ((), ())), preferred_element_type=jnp.float32
            )

        out_ref[block] = (
            product(window_hi[...], high) + product(window_lo[...], high) + product(window_hi[...], low)
        )


def load_tile(ref, count, tile, bins):
    real = [ref[index, pl.ds(pl.multiple_of(tile * 8, 8), 8), :] for index in range(count)]
    imag = [ref[index, pl.ds(pl.multiple_of(bins + tile * 8, 8), 8), :] for index in range(count)]
    return (real, imag)


def mixed_products(left, right, sums, conjugate):
    (left_re, left_im), (right_re, right_im) = left, right
    results = []
    for pairs in sums:
        total_re, total_im = None, None
        for one, two in pairs:
            a, b, c, d = left_re[one], left_im[one], right_re[two], right_im[two]
            if conjugate:
                real, imag = a * c + b * d, a * d - b * c
            else:
                real, imag = a * c - b * d, a * d + b * c
            total_re = real if total_re is None else total_re + real
            total_im = imag if total_im is None else total_im + imag
        results.append((total_re, total_im))
    return results


def back_to_rows(spectrum, inv_hi, inv_lo):
    return jnp.dot(inv_hi, spectrum, preferred_element_type=jnp.float32) + jnp.dot(
        inv_lo, spectrum, preferred_element_type=jnp.float32
    )


def store_tiles(ref, first_lane, tiles, pair, bins):
    lanes = pl.ds(first_lane, LANES)
    for index, parts in enumerate(zip(*tiles)):
        for first, values in zip((0, bins), zip(*parts)):
            rows = pl.ds(pl.multiple_of(first + pair * 16, 16), 16)
            ref[index, rows, lanes] = jnp.concatenate(values, axis=0).astype(ref.dtype)


def convolve_kernel(order, taps_ref, spec_h, doubled, inv_hi, inv_lo, *refs):
    count = len(order)
    in_refs, out_refs = refs[:count], refs[count : 2 * count]
    spec_x, spec_g, edges, firsts, joined, heads, spec_y, extra = refs[2 * count :]
    me = lax.axis_index("context")
    rows = inv_hi.shape[0]
    halo = taps_ref.shape[1] - 1
    gather_heads(order, in_refs, edges, firsts, rows)
    repair_heads(taps_ref, edges, firsts, joined, heads)
    to_spectra(order, in_refs, heads, doubled[...], spec_x, spec_g, rows, halo)

    def body(pair, carry):
        longs, backs = [], []
        for tile in (2 * pair, 2 * pair + 1):
            filt = load_tile(spec_h, count, tile, rows)
            sums = [[(i - j, j) for j in range(i + 1)] for i in range(count)]
            longs.append(mixed_products(filt, load_tile(spec_x, count, tile, rows), sums, False))
            sums = [[(j - i, j) for j in range(i, count)] for i in range(count)]
            backs.append(mixed_products(filt, load_tile(spec_g, count, tile, rows), sums, True))
        store_tiles(spec_y, 0, longs, pair, rows)
        store_tiles(spec_y, LANES, backs, pair, rows)
        return carry

    lax.fori_loop(0, rows // 16, body, 0)
    extra[...] = jnp.zeros(extra.shape, jnp.float32)
    for mask, out_ref in zip(order, out_refs):
        block = me ^ mask
        query_f, key_f, value_f, cotangent = [heads[block, which] for which in range(4)]
        both = back_to_rows(spec_y[block], inv_hi[...], inv_lo[...]).astype(jnp.bfloat16)
        out_ref[pl.ds(0, rows), :] = both[:, :LANES]
        head = both[:16].astype(jnp.float32)
        long_head, back_head = head[:8, :LANES], head[:8, LANES:]
        grad_key, grad_value = back_head * value_f, back_head * key_f
        back = head_rows(grad_key, head[:, LANES:], halo).astype(jnp.bfloat16)
        out_ref[pl.ds(rows, rows), :] = jnp.concatenate([back, both[16:, LANES:]], axis=0)
        own = (query_f * long_head, grad_value)
        following = (cotangent * long_head, grad_key, grad_value)
        for place, value in enumerate(own):
            extra[block + 1, pl.ds(place * halo, halo), :] = value[:halo]
        for place, value in enumerate(following):
            extra[block, pl.ds((2 + place) * halo, halo), :] = value[:halo]
    for mask, out_ref in zip(order, out_refs):
        block = me ^ mask
        out_ref[pl.ds(2 * rows, extra.shape[1]), :] = extra[block + 1].astype(jnp.bfloat16)


def correlate_kernel(scale, spec_x, spec_g, inv_hi, inv_lo, out_ref, spec_y):
    count = spec_x.shape[0]
    rows = inv_hi.shape[0]

    def body(pair, carry):
        row = lax.broadcasted_iota(jnp.int32, (8, LANES), 0)
        sign = jnp.where(row % 2 == 0, 1.0, -1.0)
        tiles = []
        for tile in (2 * pair, 2 * pair + 1):
            real, imag = load_tile(spec_x, count, tile, rows)
            window_re = [real[0]] + [real[i] - sign * imag[i - 1] for i in range(1, count)]
            window_im = [imag[0]] + [imag[i] + sign * real[i - 1] for i in range(1, count)]
            sums = [[(j - lag, j) for j in range(lag, count)] for lag in range(count)]
            grad = load_tile(spec_g, count, tile, rows)
            tiles.append(mixed_products((window_re, window_im), grad, sums, True))
        store_tiles(spec_y, 0, tiles, pair, rows)
        return carry

    lax.fori_loop(0, rows // 16, body, 0)
    for block in range(count):
        result = back_to_rows(spec_y[block], inv_hi[...], inv_lo[...])
        out_ref[:, pl.ds(block * rows, rows)] = result.T * scale


def finish_channels(order, places, in_refs, g_ref, taps_ref, filtered_ref, padded, extra, results, leave):
    me = lax.axis_index("context")
    rows = g_ref.shape[0]
    span = taps_ref.shape[1]
    halo = span - 1
    for index, (place, in_ref) in enumerate(zip(places, in_refs)):
        lanes = pl.ds(pl.multiple_of((me ^ order[place]) * LANES, LANES), LANES)
        slot = index % padded.shape[0]
        edge_rows = in_ref.shape[0] - 2 * rows
        query_f, key_f, value_f = [filtered_ref[which, place] for which in range(3)]
        cotangent = g_ref[:, lanes].astype(jnp.float32)
        long_conv = in_ref[pl.ds(0, rows), :].astype(jnp.float32)
        back = in_ref[pl.ds(rows, rows), :].astype(jnp.float32)
        extra[slot, pl.ds(0, edge_rows), :] = in_ref[pl.ds(2 * rows, edge_rows), :].astype(jnp.float32)
        mixed = head_rows(extra[slot, pl.ds(0, 8), :], query_f * long_conv, halo)
        results[index, 3] = mixed.astype(jnp.bfloat16)
        leave(index, 3)
        grads = (
            cotangent * long_conv,
            head_rows(back[:8], back * value_f, halo),
            head_rows(extra[slot, pl.ds(halo, 8), :], back * key_f, halo),
        )
        for which, grad in enumerate(grads):
            padded[slot, which, pl.ds(0, rows), :] = grad.astype(jnp.bfloat16).astype(jnp.float32)
            padded[slot, which, pl.ds(rows, halo), :] = extra[slot, pl.ds((2 + which) * halo, halo), :]
            weights = tap_rows(taps_ref, which, lanes)
            running = weights[0] * padded[slot, which, pl.ds(0, rows), :]
            for offset in range(1, span):
                running = running + weights[offset] * padded[slot, which, pl.ds(offset, rows), :]
            results[index, which] = running.astype(jnp.bfloat16)
            leave(index, which)


def early_kernel(order, places, g_ref, taps_ref, filtered_ref, *refs):
    *in_refs, results, padded, extra = refs
    finish_channels(
        order, places, in_refs, g_ref, taps_ref, filtered_ref, padded, extra, results, lambda *_: None
    )


def last_kernel(order, early, places, g_ref, taps_ref, filtered_ref, early_ref, filter_ref, *refs):
    in_refs = refs[: len(places)]
    mixed_ref, grads_ref, filter_out, padded, extra, results, early_sems, sems, filter_sem = refs[
        len(places) :
    ]
    me = lax.axis_index("context")
    copies = [pltpu.make_async_copy(filter_ref, filter_out.at[0], filter_sem)]
    copies[0].start()

    def leave_from(source, members, semaphores):
        def leave(index, which):
            lanes = pl.ds(pl.multiple_of((me ^ order[members[index]]) * LANES, LANES), LANES)
            target = mixed_ref.at[:, lanes] if which == 3 else grads_ref.at[which, :, lanes]
            copies.append(
                pltpu.make_async_copy(source.at[index, which], target, semaphores.at[index, which])
            )
            copies[-1].start()

        return leave

    leave = leave_from(early_ref, early, early_sems)
    for index in range(len(early)):
        for which in range(4):
            leave(index, which)
    finish_channels(
        order, places, in_refs, g_ref, taps_ref, filtered_ref, padded, extra, results,
        leave_from(results, places, sems),
    )
    for copy in copies:
        copy.wait()


def on_device(kernel, out_shape, scratch, args, in_hbm=0, pin=True):
    whole = pl.BlockSpec(memory_space=pltpu.VMEM)
    outside = pl.BlockSpec(memory_space=pltpu.HBM if pin else pl.ANY)
    args = [
        pltpu.with_memory_space_constraint(arg, pltpu.HBM) if pin and place < in_hbm else arg
        for place, arg in enumerate(args)
    ]
    return pl.pallas_call(
        kernel,
        out_shape=out_shape,
        in_specs=[outside if place < in_hbm else whole for place in range(len(args))],
        out_specs=jax.tree.map(
            lambda out: whole if isinstance(out, jax.ShapeDtypeStruct) else outside, out_shape
        ),
        scratch_shapes=[
            pltpu.VMEM(shape, jnp.float32) if isinstance(shape, tuple) else shape for shape in scratch
        ],
        compiler_params=pltpu.CompilerParams(vmem_limit_bytes=VMEM_BYTES),
    )(*args)


def exchange_order(count):
    return sorted(
        range(count),
        key=lambda mask: (mask == 0, -(mask >> 1).bit_count(), mask % 2, mask if mask % 2 else -mask),
    )


def exchange(order, parcels):
    count = lax.axis_size("context")
    return [
        parcel if mask == 0 else lax.ppermute(parcel, "context", [(i, i ^ mask) for i in range(count)])
        for mask, parcel in zip(order, parcels)
    ]


def block_shards(query_proj, key_proj, value_proj, short_taps, long_filter, grad_mixed):
    rows, channels = query_proj.shape
    blocks = lax.axis_size("context")
    halo = short_taps.shape[1] - 1
    seq_len = rows * blocks
    window_hi, window_lo, doubled, inv_hi, inv_lo = [jnp.asarray(t) for t in block_tables(rows)]
    edge_rows = round_up(5 * halo, 16)
    order = exchange_order(blocks)
    parcels = [jax.ShapeDtypeStruct((2 * rows + edge_rows, LANES), jnp.bfloat16)] * blocks
    spectra = (blocks, 2 * rows, LANES)
    own_taps = (*short_taps.shape[:2], LANES)
    kept = (long_filter[0], window_hi, window_lo)

    *sent, filtered, own, filter_here, hi_here, lo_here = on_device(
        functools.partial(send_kernel, order),
        parcels
        + [
            jax.ShapeDtypeStruct((3, blocks, rows, LANES), jnp.float32),
            jax.ShapeDtypeStruct(own_taps, jnp.float32),
        ]
        + [jax.ShapeDtypeStruct(value.shape, value.dtype) for value in kept],
        [
            pltpu.VMEM((blocks, 4, rows, LANES), jnp.bfloat16),
            (blocks, *own_taps),
            (2, 3, rows + 8, LANES),
            (2, edge_rows, LANES),
            pltpu.SemaphoreType.DMA((blocks, 5)),
            pltpu.SemaphoreType.DMA((len(kept),)),
        ],
        (query_proj, key_proj, value_proj, grad_mixed, short_taps, *kept),
        in_hbm=8,
    )
    arrived = exchange(order, sent)
    spec_h = on_device(
        filter_kernel,
        jax.ShapeDtypeStruct(spectra, jnp.float32),
        [],
        (arrived[0], filter_here, hi_here, lo_here),
        in_hbm=1,
        pin=False,
    )
    *results, spec_x, spec_g = on_device(
        functools.partial(convolve_kernel, order),
        parcels + [jax.ShapeDtypeStruct(spectra, jnp.float32)] * 2,
        [
            (blocks, edge_rows, LANES),
            (blocks, 2, 8, LANES),
            (3, blocks, 24, LANES),
            (blocks, 6, 8, LANES),
            pltpu.VMEM((blocks, 2 * rows, 2 * LANES), jnp.bfloat16),
            (blocks + 1, edge_rows, LANES),
        ],
        (own, spec_h, doubled, inv_hi, inv_lo, *arrived),
    )
    returned = exchange(order, results)
    filter_grad = on_device(
        functools.partial(correlate_kernel, 1.0 / math.sqrt(seq_len)),
        jax.ShapeDtypeStruct(long_filter.shape[1:], jnp.float32),
        [pltpu.VMEM(spectra, jnp.bfloat16)],
        (spec_x, spec_g, inv_hi, inv_lo),
    )
    late = list(range(blocks // 2 - 1, blocks - 1))
    early = [place for place in range(blocks) if place not in late]
    padded = [(2, 3, rows + 16, LANES), (2, edge_rows + 8, LANES)]
    common = (grad_mixed, short_taps, filtered)
    early_results = on_device(
        functools.partial(early_kernel, order, early),
        jax.ShapeDtypeStruct((len(early), 4, rows, LANES), jnp.bfloat16),
        padded,
        (*common, *(returned[place] for place in early)),
    )
    mixed_out, input_grads, filter_grad = on_device(
        functools.partial(last_kernel, order, early, late),
        (
            pltpu.HBM((rows, channels), jnp.bfloat16),
            pltpu.HBM((3, rows, channels), jnp.bfloat16),
            pltpu.HBM(long_filter.shape, jnp.float32),
        ),
        padded
        + [
            pltpu.VMEM((len(late), 4, rows, LANES), jnp.bfloat16),
            pltpu.SemaphoreType.DMA((len(early), 4)),
            pltpu.SemaphoreType.DMA((len(late), 4)),
            pltpu.SemaphoreType.DMA(()),
        ],
        (*common, early_results, filter_grad, *(returned[place] for place in late)),
    )
    return (mixed_out, input_grads, filter_grad)


def shards(query_proj, key_proj, value_proj, short_taps, long_filter, grad_mixed):
    rows, channels = query_proj.shape
    halo = short_taps.shape[1] - 1
    blocks = lax.axis_size("context")
    power_of_two = blocks & (blocks - 1) == 0
    fits = power_of_two and channels == blocks * LANES and rows % 128 == 0 and halo <= 8
    chosen = block_shards if fits else general_shards
    return chosen(query_proj, key_proj, value_proj, short_taps, long_filter, grad_mixed)


def solution(mesh):
    return jax.shard_map(
        shards,
        mesh=mesh,
        in_specs=(
            P("context", "tensor"),
            P("context", "tensor"),
            P("context", "tensor"),
            P(None, None, "tensor"),
            P("tensor", "context", None),
            P("context", "tensor"),
        ),
        out_specs=(
            P("context", "tensor"),
            P(None, "context", "tensor"),
            P("tensor", "context", None),
        ),
        check_vma=False,
    )
```

```python
import functools
import math

import jax
import jax.numpy as jnp
import numpy as np
from jax import lax
from jax.experimental import pallas as pl
from jax.experimental.pallas import tpu as pltpu
from jax.sharding import PartitionSpec as P

precise = lax.Precision.HIGHEST


def from_behind(value, axis, steps):
    count = lax.axis_size(axis)
    first, last = (max(0, -steps), min(count, count - steps))
    return lax.ppermute(value, axis, [(source, source + steps) for source in range(first, last)])


def build_tables(blocks, tok_rows):
    outer_len = 2 * blocks
    full_len = outer_len * tok_rows
    k_one = jnp.arange(outer_len, dtype=jnp.int32)
    n_one = jnp.arange(blocks, dtype=jnp.int32)
    position = jnp.arange(tok_rows, dtype=jnp.int32)
    first_idx = k_one[:, None] * n_one[None, :] % outer_len
    first_angle = -2.0 * math.pi / outer_len * first_idx.astype(jnp.float32)
    second = position[:, None] * position[None, :] % tok_rows
    second_angle = -2.0 * math.pi / tok_rows * second.astype(jnp.float32)
    twist_idx = k_one[:, None] * position[None, :] % full_len
    twist_angle = -2.0 * math.pi / full_len * twist_idx.astype(jnp.float32)
    return (
        jnp.cos(first_angle),
        jnp.sin(first_angle),
        jnp.cos(second_angle),
        jnp.sin(second_angle),
        jnp.cos(twist_angle),
        jnp.sin(twist_angle),
    )


def transform(signal, tables):
    cos_first, sin_first, cos_second, sin_second, cos_twist, sin_twist = tables
    first_re = jnp.einsum("kn,gnm->gkm", cos_first, signal, precision=precise)
    first_im = jnp.einsum("kn,gnm->gkm", sin_first, signal, precision=precise)
    mid_re = first_re * cos_twist - first_im * sin_twist
    mid_im = first_re * sin_twist + first_im * cos_twist
    out_re = jnp.einsum("gkn,nm->gkm", mid_re, cos_second, precision=precise) - jnp.einsum(
        "gkn,nm->gkm", mid_im, sin_second, precision=precise
    )
    out_im = jnp.einsum("gkn,nm->gkm", mid_re, sin_second, precision=precise) + jnp.einsum(
        "gkn,nm->gkm", mid_im, cos_second, precision=precise
    )
    return (out_re, out_im)


def inverse(spec_re, spec_im, tables):
    cos_first, sin_first, cos_second, sin_second, cos_twist, sin_twist = tables
    full_len = cos_first.shape[0] * cos_second.shape[0]
    mid_re = jnp.einsum("gkn,nm->gkm", spec_re, cos_second, precision=precise) + jnp.einsum(
        "gkn,nm->gkm", spec_im, sin_second, precision=precise
    )
    mid_im = jnp.einsum("gkn,nm->gkm", spec_im, cos_second, precision=precise) - jnp.einsum(
        "gkn,nm->gkm", spec_re, sin_second, precision=precise
    )
    turn_re = mid_re * cos_twist + mid_im * sin_twist
    turn_im = mid_im * cos_twist - mid_re * sin_twist
    result = jnp.einsum("kn,gkm->gnm", cos_first, turn_re, precision=precise) + jnp.einsum(
        "kn,gkm->gnm", sin_first, turn_im, precision=precise
    )
    return result * (1.0 / full_len)


def causal_taps(series, preceding, tap_weights):
    tok_rows = series.shape[0]
    span = tap_weights.shape[0]
    joined = jnp.concatenate([preceding, series], axis=0).astype(jnp.float32)
    running = jnp.zeros(series.shape, jnp.float32)
    for offset in range(span):
        first_row = span - 1 - offset
        running = running + tap_weights[offset][None, :] * joined[first_row : first_row + tok_rows]
    return running


def reverse_taps(series, following, tap_weights):
    tok_rows = series.shape[0]
    span = tap_weights.shape[0]
    joined = jnp.concatenate([series, following], axis=0).astype(jnp.float32)
    running = jnp.zeros(series.shape, jnp.float32)
    for offset in range(span):
        running = running + tap_weights[offset][None, :] * joined[offset : offset + tok_rows]
    return running


def general_shards(query_proj, key_proj, value_proj, short_taps, long_filter, grad_mixed):
    tok_rows, channels = query_proj.shape
    blocks = lax.axis_size("context")
    halo_rows = short_taps.shape[1] - 1
    per_device = channels // blocks
    seq_len = tok_rows * blocks
    tables = build_tables(blocks, tok_rows)
    preceding = from_behind(
        (
            query_proj[tok_rows - halo_rows :],
            key_proj[tok_rows - halo_rows :],
            value_proj[tok_rows - halo_rows :],
        ),
        "context",
        1,
    )
    query_f = causal_taps(query_proj, preceding[0], short_taps[0])
    key_f = causal_taps(key_proj, preceding[1], short_taps[1])
    value_f = causal_taps(value_proj, preceding[2], short_taps[2])
    gated_prod = (key_f * value_f).astype(jnp.bfloat16)
    grad_f = grad_mixed.astype(jnp.float32)
    grad_long = (grad_f * query_f).astype(jnp.bfloat16)

    def to_spectrum(series):
        arranged = series.T.reshape(blocks, per_device, tok_rows)
        received = lax.all_to_all(arranged, "context", split_axis=0, concat_axis=2, tiled=True)
        item_count = received.shape[1]
        signal = received.reshape(item_count, blocks, tok_rows).astype(jnp.float32)
        return transform(signal, tables)

    def to_token_rows(spatial):
        arrived = lax.all_to_all(spatial, "context", split_axis=1, concat_axis=0, tiled=True)
        return arrived.reshape(channels, tok_rows).T

    gate_re, gate_im = to_spectrum(gated_prod)
    filter_re, filter_im = transform(long_filter.reshape(per_device, blocks, tok_rows), tables)
    long_spatial = inverse(
        gate_re * filter_re - gate_im * filter_im, gate_re * filter_im + gate_im * filter_re, tables
    ).astype(jnp.bfloat16)
    long_conv = to_token_rows(long_spatial)
    long_f = long_conv.astype(jnp.float32)
    mixed_out = (query_f * long_f).astype(jnp.bfloat16)
    grad_query_f = (grad_f * long_f).astype(jnp.bfloat16)
    grad_after = lax.optimization_barrier((grad_long, long_conv))[0]
    grad_re, grad_im = to_spectrum(grad_after)
    back_spatial = inverse(
        filter_re * grad_re + filter_im * grad_im, filter_re * grad_im - filter_im * grad_re, tables
    ).astype(jnp.bfloat16)
    corr_spatial = inverse(
        gate_re * grad_re + gate_im * grad_im, gate_re * grad_im - gate_im * grad_re, tables
    )
    grad_gated = to_token_rows(back_spatial).astype(jnp.float32)
    grad_key_f = (grad_gated * value_f).astype(jnp.bfloat16)
    grad_value_f = (grad_gated * key_f).astype(jnp.bfloat16)
    following = from_behind(
        (grad_query_f[:halo_rows], grad_key_f[:halo_rows], grad_value_f[:halo_rows]), "context", -1
    )
    input_grads = jnp.stack(
        [
            reverse_taps(grad_query_f, following[0], short_taps[0]),
            reverse_taps(grad_key_f, following[1], short_taps[1]),
            reverse_taps(grad_value_f, following[2], short_taps[2]),
        ]
    ).astype(jnp.bfloat16)
    filter_grad = (corr_spatial * (1.0 / math.sqrt(seq_len))).reshape(1, per_device, seq_len)
    return (mixed_out, input_grads, filter_grad)


LANES = 128
VMEM_BYTES = 48 * 1024 * 1024


def split_bf16(table):
    high = table.astype(jnp.bfloat16)
    low = (table - high.astype(np.float64)).astype(jnp.bfloat16)
    return (high, low)


@functools.cache
def block_tables(rows):
    bins = np.pi * (np.arange(rows) + 0.5)[:, None] / rows
    lag = np.arange(rows)[None, :]
    forward = np.concatenate([np.cos(bins * lag), -np.sin(bins * lag)], axis=0)
    forward_hi, forward_lo = split_bf16(forward)
    return (forward_hi, forward_lo, split_bf16(forward.T / rows)[0])


def round_up(count, unit):
    return (count + unit - 1) // unit * unit


def head_rows(fresh, whole, halo):
    row = lax.broadcasted_iota(jnp.int32, fresh.shape, 0)
    return jnp.concatenate([jnp.where(row < halo, fresh, whole[:8]), whole[8:]], axis=0)


def tap_rows(taps_ref, which, lanes):
    return [taps_ref[which, pl.ds(offset, 1), lanes] for offset in range(taps_ref.shape[1])]


def short_filter(padded, rows, weights):
    running = weights[0] * padded[pl.ds(8, rows), :]
    for offset in range(1, len(weights)):
        running = running + weights[offset] * padded[pl.ds(8 - offset, rows), :]
    return running


def send_kernel(order, q_ref, k_ref, v_ref, g_ref, taps_ref, h_ref, hi_ref, lo_ref, *refs):
    count = len(order)
    outs = refs[:count]
    filtered_ref, own_ref, h_here, hi_here, lo_here = refs[count : count + 5]
    landed, taps, padded, extra, arrivals, kept = refs[count + 5 :]
    me = lax.axis_index("context")
    rows = q_ref.shape[0]
    halo = taps_ref.shape[1] - 1

    def lanes_of(place):
        return pl.ds(pl.multiple_of((me ^ order[place]) * LANES, LANES), LANES)

    def fetches(place):
        lanes = lanes_of(place)
        copies = [
            pltpu.make_async_copy(
                taps_ref.at[:, :, lanes], taps.at[place], arrivals.at[place, 4]
            )
        ]
        for which, ref in enumerate((q_ref, k_ref, v_ref, g_ref)):
            copies.append(
                pltpu.make_async_copy(
                    ref.at[:, lanes], landed.at[place, which], arrivals.at[place, which]
                )
            )
        return copies

    keeps = [
        pltpu.make_async_copy(source, target, kept.at[index])
        for index, (source, target) in enumerate(
            ((h_ref, h_here), (hi_ref, hi_here), (lo_ref, lo_here))
        )
    ]
    for place in range(count):
        for copy in fetches(place):
            copy.start()
    for copy in keeps:
        copy.start()
    for place in range(count):
        slot = place % padded.shape[0]
        out_ref = outs[place]
        padded[slot, :, pl.ds(0, 8), :] = jnp.zeros((3, 8, LANES), jnp.float32)
        extra[slot, pl.ds(5 * halo, extra.shape[1] - 5 * halo), :] = jnp.zeros(
            (extra.shape[1] - 5 * halo, LANES), jnp.float32
        )
        for copy in fetches(place):
            copy.wait()
        filtered = []
        for which in range(3):
            padded[slot, which, pl.ds(8, rows), :] = landed[place, which].astype(jnp.float32)
            weights = tap_rows(taps.at[place], which, pl.ds(0, LANES))
            result = short_filter(padded.at[slot, which], rows, weights)
            filtered_ref[which, place] = result
            filtered.append(result)
        query_f, key_f, value_f = filtered
        cotangent = landed[place, 3].astype(jnp.float32)
        gated = head_rows(padded[slot, 1, pl.ds(8, 8), :], key_f * value_f, halo)
        grad_long = head_rows(cotangent[:8], cotangent * query_f, halo)
        out_ref[pl.ds(0, rows), :] = gated.astype(jnp.bfloat16)
        out_ref[pl.ds(rows, rows), :] = grad_long.astype(jnp.bfloat16)
        pieces = ((1, rows - halo), (2, 0), (2, rows - halo), (0, 0), (0, rows - halo))
        for position, (which, first) in enumerate(pieces):
            extra[slot, pl.ds(position * halo, halo), :] = padded[slot, which, pl.ds(8 + first, halo), :]
        out_ref[pl.ds(2 * rows, extra.shape[1]), :] = extra[slot].astype(jnp.bfloat16)
    own_ref[...] = taps[order.index(0)]
    for copy in keeps:
        copy.wait()


def gather(order, in_refs, edges, firsts, pairs, rows):
    me = lax.axis_index("context")
    for mask, in_ref in zip(order, in_refs):
        block = me ^ mask
        edges[block] = in_ref[pl.ds(2 * rows, edges.shape[1]), :].astype(jnp.float32)
        for which in range(2):
            values = in_ref[pl.ds(which * rows, rows), :]
            firsts[block, which] = values[:16].astype(jnp.float32)[:8]
            pairs[block, :, pl.ds(which * LANES, LANES)] = values


def repair_heads(taps_ref, edges, firsts, joined, heads):
    blocks = edges.shape[0]
    span = taps_ref.shape[1]
    halo = span - 1
    joined[...] = jnp.zeros(joined.shape, jnp.float32)
    for block in range(blocks):
        joined[1, block, pl.ds(halo, 8), :] = firsts[block, 0]
        joined[2, block, pl.ds(halo, halo), :] = edges[block, pl.ds(halo, halo), :]
        joined[0, block, pl.ds(halo, halo), :] = edges[block, pl.ds(3 * halo, halo), :]
        if block > 0:
            for which, place in ((1, 0), (2, 2), (0, 4)):
                joined[which, block, pl.ds(0, halo), :] = edges[block - 1, pl.ds(place * halo, halo), :]
        filtered = []
        for which in range(3):
            running = jnp.zeros((8, LANES), jnp.float32)
            for offset in range(span):
                weight = taps_ref[which, pl.ds(offset, 1), :]
                running = running + weight * joined[which, block, pl.ds(halo - offset, 8), :]
            filtered.append(running)
            heads[block, which] = running
        cotangent = firsts[block, 1]
        heads[block, 3] = cotangent
        heads[block, 4] = filtered[1] * filtered[2]
        heads[block, 5] = cotangent * filtered[0]


def to_spectra(heads, pairs, forward, spec_x, spec_g, halo):
    blocks, rows, width = pairs.shape
    merged = blocks // spec_x.shape[0]
    for block in range(blocks):
        fresh = jnp.concatenate([heads[block, 4], heads[block, 5]], axis=1)
        head = head_rows(fresh, pairs[block, pl.ds(0, 16), :].astype(jnp.float32), halo)
        pairs[block, pl.ds(0, 16), :] = head.astype(jnp.bfloat16)
    for index in range(spec_x.shape[0]):
        signals = pairs[pl.ds(index * merged, merged)].reshape(merged * rows, width)
        spectrum = jnp.dot(forward, signals, preferred_element_type=jnp.float32)
        spec_x[index] = spectrum[:, :LANES]
        spec_g[index] = spectrum[:, LANES:]


def filter_kernel(parcel_ref, h_ref, forward_hi, forward_lo, out_ref):
    del parcel_ref
    blocks, two_rows, _ = out_ref.shape
    rows = two_rows // 2
    sign = jnp.where(lax.broadcasted_iota(jnp.int32, (rows, LANES), 0) % 2 == 0, 1.0, -1.0)

    def product(table, values):
        return lax.dot_general(
            table, values, (((1,), (1,)), ((), ())), preferred_element_type=jnp.float32
        )

    before = None
    for block in range(blocks):
        signal = h_ref[:, pl.ds(block * rows, rows)]
        high = signal.astype(jnp.bfloat16)
        low = (signal - high.astype(jnp.float32)).astype(jnp.bfloat16)
        spectrum = (
            product(forward_hi[...], high)
            + product(forward_lo[...], high)
            + product(forward_hi[...], low)
        )
        real, imag = spectrum[:rows], spectrum[rows:]
        if before is None:
            out_ref[block] = spectrum
        else:
            out_ref[block, pl.ds(0, rows), :] = real - sign * before[1]
            out_ref[block, pl.ds(rows, rows), :] = imag + sign * before[0]
        before = (real, imag)


def load_tile(ref, count, tile, bins):
    real = [ref[index, pl.ds(pl.multiple_of(tile * 8, 8), 8), :] for index in range(count)]
    imag = [ref[index, pl.ds(pl.multiple_of(bins + tile * 8, 8), 8), :] for index in range(count)]
    return (real, imag)


def mixed_products(left, right, sums, conjugate):
    (left_re, left_im), (right_re, right_im) = left, right
    results = []
    for pairs in sums:
        total_re, total_im = None, None
        for one, two in pairs:
            a, b, c, d = left_re[one], left_im[one], right_re[two], right_im[two]
            if conjugate:
                real, imag = a * c + b * d, a * d - b * c
            else:
                real, imag = a * c - b * d, a * d + b * c
            total_re = real if total_re is None else total_re + real
            total_im = imag if total_im is None else total_im + imag
        results.append((total_re, total_im))
    return results


def store_tiles(ref, first_lane, tiles, pair, bins):
    lanes = pl.ds(first_lane, LANES)
    for index, parts in enumerate(zip(*tiles)):
        for first, values in zip((0, bins), zip(*parts)):
            rows = pl.ds(pl.multiple_of(first + pair * 16, 16), 16)
            ref[index, rows, lanes] = jnp.concatenate(values, axis=0).astype(ref.dtype)


def convolve_kernel(order, taps_ref, spec_h, forward, inverse, *refs):
    count = len(order)
    in_refs, out_refs = refs[:count], refs[count : 2 * count]
    spec_x, spec_g, edges, firsts, joined, heads, pairs, spec_y, extra = refs[2 * count :]
    me = lax.axis_index("context")
    rows = pairs.shape[1]
    halo = taps_ref.shape[1] - 1
    bins = inverse.shape[0]
    wide = spec_h.shape[0]
    gather(order, in_refs, edges, firsts, pairs, rows)
    repair_heads(taps_ref, edges, firsts, joined, heads)
    to_spectra(heads, pairs, forward[...], spec_x, spec_g, halo)

    def body(pair, carry):
        longs, backs = [], []
        for tile in (2 * pair, 2 * pair + 1):
            filt = load_tile(spec_h, wide, tile, bins)
            sums = [[(i - j, j) for j in range(i + 1)] for i in range(wide)]
            longs.append(mixed_products(filt, load_tile(spec_x, wide, tile, bins), sums, False))
            sums = [[(j - i, j) for j in range(i, wide)] for i in range(wide)]
            backs.append(mixed_products(filt, load_tile(spec_g, wide, tile, bins), sums, True))
        store_tiles(spec_y, 0, longs, pair, bins)
        store_tiles(spec_y, LANES, backs, pair, bins)
        return carry

    lax.fori_loop(0, bins // 16, body, 0)
    extra[...] = jnp.zeros(extra.shape, jnp.float32)
    for index in range(wide):
        both = jnp.dot(inverse[...], spec_y[index], preferred_element_type=jnp.float32).astype(jnp.bfloat16)
        for part in range(count // wide):
            block = index * (count // wide) + part
            here = both[part * rows : (part + 1) * rows]
            query_f, key_f, value_f, cotangent = [heads[block, which] for which in range(4)]
            head = here[:16].astype(jnp.float32)
            long_head, back_head = head[:8, :LANES], head[:8, LANES:]
            grad_key, grad_value = back_head * value_f, back_head * key_f
            back = head_rows(grad_key, head[:, LANES:], halo).astype(jnp.bfloat16)
            pairs[block, :, pl.ds(0, LANES)] = here[:, :LANES]
            pairs[block, :, pl.ds(LANES, LANES)] = jnp.concatenate([back, here[16:, LANES:]], axis=0)
            own = (query_f * long_head, grad_value)
            following = (cotangent * long_head, grad_key, grad_value)
            for place, value in enumerate(own):
                extra[block + 1, pl.ds(place * halo, halo), :] = value[:halo]
            for place, value in enumerate(following):
                extra[block, pl.ds((2 + place) * halo, halo), :] = value[:halo]
    for mask, out_ref in zip(order, out_refs):
        block = me ^ mask
        for which in range(2):
            out_ref[pl.ds(which * rows, rows), :] = pairs[block, :, pl.ds(which * LANES, LANES)]
        out_ref[pl.ds(2 * rows, extra.shape[1]), :] = extra[block + 1].astype(jnp.bfloat16)


def correlate_kernel(scale, spec_x, spec_g, inverse, out_ref, spec_y):
    wide = spec_x.shape[0]
    bins = inverse.shape[0]

    def body(pair, carry):
        row = lax.broadcasted_iota(jnp.int32, (8, LANES), 0)
        sign = jnp.where(row % 2 == 0, 1.0, -1.0)
        tiles = []
        for tile in (2 * pair, 2 * pair + 1):
            real, imag = load_tile(spec_x, wide, tile, bins)
            window_re = [real[0]] + [real[i] - sign * imag[i - 1] for i in range(1, wide)]
            window_im = [imag[0]] + [imag[i] + sign * real[i - 1] for i in range(1, wide)]
            sums = [[(j - lag, j) for j in range(lag, wide)] for lag in range(wide)]
            grad = load_tile(spec_g, wide, tile, bins)
            tiles.append(mixed_products((window_re, window_im), grad, sums, True))
        store_tiles(spec_y, 0, tiles, pair, bins)
        return carry

    lax.fori_loop(0, bins // 16, body, 0)
    for index in range(wide):
        result = jnp.dot(inverse[...], spec_y[index], preferred_element_type=jnp.float32)
        out_ref[:, pl.ds(index * bins, bins)] = result.T * scale


def finish_channels(order, places, in_refs, g_ref, taps_ref, filtered_ref, padded, extra, results, leave):
    me = lax.axis_index("context")
    rows = g_ref.shape[0]
    span = taps_ref.shape[1]
    halo = span - 1
    for index, (place, in_ref) in enumerate(zip(places, in_refs)):
        lanes = pl.ds(pl.multiple_of((me ^ order[place]) * LANES, LANES), LANES)
        slot = index % padded.shape[0]
        edge_rows = in_ref.shape[0] - 2 * rows
        query_f, key_f, value_f = [filtered_ref[which, place] for which in range(3)]
        cotangent = g_ref[:, lanes].astype(jnp.float32)
        long_conv = in_ref[pl.ds(0, rows), :].astype(jnp.float32)
        back = in_ref[pl.ds(rows, rows), :].astype(jnp.float32)
        extra[slot, pl.ds(0, edge_rows), :] = in_ref[pl.ds(2 * rows, edge_rows), :].astype(jnp.float32)
        mixed = head_rows(extra[slot, pl.ds(0, 8), :], query_f * long_conv, halo)
        results[index, 3] = mixed.astype(jnp.bfloat16)
        leave(index, 3)
        grads = (
            cotangent * long_conv,
            head_rows(back[:8], back * value_f, halo),
            head_rows(extra[slot, pl.ds(halo, 8), :], back * key_f, halo),
        )
        for which, grad in enumerate(grads):
            padded[slot, which, pl.ds(0, rows), :] = grad.astype(jnp.bfloat16).astype(jnp.float32)
            padded[slot, which, pl.ds(rows, halo), :] = extra[slot, pl.ds((2 + which) * halo, halo), :]
            weights = tap_rows(taps_ref, which, lanes)
            running = weights[0] * padded[slot, which, pl.ds(0, rows), :]
            for offset in range(1, span):
                running = running + weights[offset] * padded[slot, which, pl.ds(offset, rows), :]
            results[index, which] = running.astype(jnp.bfloat16)
            leave(index, which)


def receive_kernel(order, places, g_ref, taps_ref, filtered_ref, filter_ref, *refs):
    in_refs = refs[: len(places)]
    mixed_ref, grads_ref, filter_out, padded, extra, results, sems, filter_sem = refs[-8:]
    me = lax.axis_index("context")
    copies = []
    if filter_ref is not None:
        copies.append(pltpu.make_async_copy(filter_ref, filter_out.at[0], filter_sem))
        copies[-1].start()

    def leave(index, which):
        lanes = pl.ds(pl.multiple_of((me ^ order[places[index]]) * LANES, LANES), LANES)
        target = mixed_ref.at[:, lanes] if which == 3 else grads_ref.at[which, :, lanes]
        copies.append(pltpu.make_async_copy(results.at[index, which], target, sems.at[index, which]))
        copies[-1].start()

    finish_channels(
        order, places, in_refs, g_ref, taps_ref, filtered_ref, padded, extra, results, leave
    )
    for copy in copies:
        copy.wait()


def last_kernel(order, places, g_ref, taps_ref, filtered_ref, *refs):
    in_refs, refs = refs[: len(places)], refs[len(places) + 2 :]
    mixed_ref, grads_ref, padded, extra, results, sems = refs
    receive_kernel(
        order, places, g_ref, taps_ref, filtered_ref, None, *in_refs,
        mixed_ref, grads_ref, None, padded, extra, results, sems, None,
    )


def on_device(kernel, out_shape, scratch, args, in_hbm=0, pin=True, updated=0):
    whole = pl.BlockSpec(memory_space=pltpu.VMEM)
    outside = pl.BlockSpec(memory_space=pltpu.HBM if pin else pl.ANY)
    last = len(args) - updated
    args = [
        pltpu.with_memory_space_constraint(arg, pltpu.HBM) if pin and place < in_hbm else arg
        for place, arg in enumerate(args)
    ]
    return pl.pallas_call(
        kernel,
        out_shape=out_shape,
        in_specs=[outside if place < in_hbm or place >= last else whole for place in range(len(args))],
        out_specs=jax.tree.map(
            lambda out: whole if isinstance(out, jax.ShapeDtypeStruct) else outside, out_shape
        ),
        input_output_aliases={last + place: place for place in range(updated)},
        scratch_shapes=[
            pltpu.VMEM(shape, jnp.float32) if isinstance(shape, tuple) else shape for shape in scratch
        ],
        compiler_params=pltpu.CompilerParams(vmem_limit_bytes=VMEM_BYTES),
    )(*args)


def exchange_order(count):
    return sorted(
        range(count),
        key=lambda mask: (mask == 0, -(mask >> 1).bit_count(), mask % 2, mask if mask % 2 else -mask),
    )


def exchange(order, parcels):
    count = lax.axis_size("context")
    return [
        parcel if mask == 0 else lax.ppermute(parcel, "context", [(i, i ^ mask) for i in range(count)])
        for mask, parcel in zip(order, parcels)
    ]


def block_shards(query_proj, key_proj, value_proj, short_taps, long_filter, grad_mixed):
    rows, channels = query_proj.shape
    blocks = lax.axis_size("context")
    halo = short_taps.shape[1] - 1
    seq_len = rows * blocks
    merged = 2
    wide = merged * rows
    forward_hi, forward_lo, inverse = [jnp.asarray(table) for table in block_tables(wide)]
    edge_rows = round_up(5 * halo, 16)
    order = exchange_order(blocks)
    parcels = [jax.ShapeDtypeStruct((2 * rows + edge_rows, LANES), jnp.bfloat16)] * blocks
    spectra = (blocks // merged, 2 * wide, LANES)
    own_taps = (*short_taps.shape[:2], LANES)
    kept = (long_filter[0], forward_hi, forward_lo)

    *sent, filtered, own, filter_here, hi_here, lo_here = on_device(
        functools.partial(send_kernel, order),
        parcels
        + [
            jax.ShapeDtypeStruct((3, blocks, rows, LANES), jnp.float32),
            jax.ShapeDtypeStruct(own_taps, jnp.float32),
        ]
        + [jax.ShapeDtypeStruct(value.shape, value.dtype) for value in kept],
        [
            pltpu.VMEM((blocks, 4, rows, LANES), jnp.bfloat16),
            (blocks, *own_taps),
            (2, 3, rows + 8, LANES),
            (2, edge_rows, LANES),
            pltpu.SemaphoreType.DMA((blocks, 5)),
            pltpu.SemaphoreType.DMA((len(kept),)),
        ],
        (query_proj, key_proj, value_proj, grad_mixed, short_taps, *kept),
        in_hbm=8,
    )
    arrived = exchange(order, sent)
    spec_h = on_device(
        filter_kernel,
        jax.ShapeDtypeStruct(spectra, jnp.float32),
        [],
        (arrived[0], filter_here, hi_here, lo_here),
        in_hbm=1,
        pin=False,
    )
    *results, spec_x, spec_g = on_device(
        functools.partial(convolve_kernel, order),
        parcels + [jax.ShapeDtypeStruct(spectra, jnp.float32)] * 2,
        [
            (blocks, edge_rows, LANES),
            (blocks, 2, 8, LANES),
            (3, blocks, 24, LANES),
            (blocks, 6, 8, LANES),
            pltpu.VMEM((blocks, rows, 2 * LANES), jnp.bfloat16),
            pltpu.VMEM((*spectra[:2], 2 * LANES), jnp.bfloat16),
            (blocks + 1, edge_rows, LANES),
        ],
        (own, spec_h, hi_here, inverse, *arrived),
    )
    returned = exchange(order, results)
    filter_grad = on_device(
        functools.partial(correlate_kernel, 1.0 / math.sqrt(seq_len)),
        jax.ShapeDtypeStruct(long_filter.shape[1:], jnp.float32),
        [pltpu.VMEM(spectra, jnp.bfloat16)],
        (spec_x, spec_g, inverse),
    )
    late = list(range(blocks // 2 - 1, blocks - 1))
    early = [place for place in range(blocks) if place not in late]
    outputs = (
        pltpu.HBM((rows, channels), jnp.bfloat16),
        pltpu.HBM((3, rows, channels), jnp.bfloat16),
        pltpu.HBM(long_filter.shape, jnp.float32),
    )

    def working(places):
        return [
            (2, 3, rows + 16, LANES),
            (2, edge_rows + 8, LANES),
            pltpu.VMEM((len(places), 4, rows, LANES), jnp.bfloat16),
            pltpu.SemaphoreType.DMA((len(places), 4)),
        ]

    common = (grad_mixed, short_taps, filtered)
    *begun, filter_grad = on_device(
        functools.partial(receive_kernel, order, early),
        outputs,
        [*working(early), pltpu.SemaphoreType.DMA(())],
        (*common, filter_grad, *(returned[place] for place in early)),
    )
    mixed_out, input_grads = on_device(
        functools.partial(last_kernel, order, late),
        outputs[:2],
        working(late),
        (*common, *(returned[place] for place in late), *begun),
        updated=2,
    )
    return (mixed_out, input_grads, filter_grad)


def shards(query_proj, key_proj, value_proj, short_taps, long_filter, grad_mixed):
    rows, channels = query_proj.shape
    halo = short_taps.shape[1] - 1
    blocks = lax.axis_size("context")
    power_of_two = blocks & (blocks - 1) == 0
    fits = power_of_two and blocks > 1 and channels == blocks * LANES and rows % 128 == 0 and halo <= 8
    chosen = block_shards if fits else general_shards
    return chosen(query_proj, key_proj, value_proj, short_taps, long_filter, grad_mixed)


def solution(mesh):
    return jax.shard_map(
        shards,
        mesh=mesh,
        in_specs=(
            P("context", "tensor"),
            P("context", "tensor"),
            P("context", "tensor"),
            P(None, None, "tensor"),
            P("tensor", "context", None),
            P("context", "tensor"),
        ),
        out_specs=(
            P("context", "tensor"),
            P(None, "context", "tensor"),
            P("tensor", "context", None),
        ),
        check_vma=False,
    )
```

```python
import functools
import math

import jax
import jax.numpy as jnp
import numpy as np
from jax import lax
from jax.experimental import pallas as pl
from jax.experimental.pallas import tpu as pltpu
from jax.sharding import PartitionSpec as P

precise = lax.Precision.HIGHEST


def from_behind(value, axis, steps):
    count = lax.axis_size(axis)
    first, last = (max(0, -steps), min(count, count - steps))
    return lax.ppermute(value, axis, [(source, source + steps) for source in range(first, last)])


def build_tables(blocks, tok_rows):
    outer_len = 2 * blocks
    full_len = outer_len * tok_rows
    k_one = jnp.arange(outer_len, dtype=jnp.int32)
    n_one = jnp.arange(blocks, dtype=jnp.int32)
    position = jnp.arange(tok_rows, dtype=jnp.int32)
    first_idx = k_one[:, None] * n_one[None, :] % outer_len
    first_angle = -2.0 * math.pi / outer_len * first_idx.astype(jnp.float32)
    second = position[:, None] * position[None, :] % tok_rows
    second_angle = -2.0 * math.pi / tok_rows * second.astype(jnp.float32)
    twist_idx = k_one[:, None] * position[None, :] % full_len
    twist_angle = -2.0 * math.pi / full_len * twist_idx.astype(jnp.float32)
    return (
        jnp.cos(first_angle),
        jnp.sin(first_angle),
        jnp.cos(second_angle),
        jnp.sin(second_angle),
        jnp.cos(twist_angle),
        jnp.sin(twist_angle),
    )


def transform(signal, tables):
    cos_first, sin_first, cos_second, sin_second, cos_twist, sin_twist = tables
    first_re = jnp.einsum("kn,gnm->gkm", cos_first, signal, precision=precise)
    first_im = jnp.einsum("kn,gnm->gkm", sin_first, signal, precision=precise)
    mid_re = first_re * cos_twist - first_im * sin_twist
    mid_im = first_re * sin_twist + first_im * cos_twist
    out_re = jnp.einsum("gkn,nm->gkm", mid_re, cos_second, precision=precise) - jnp.einsum(
        "gkn,nm->gkm", mid_im, sin_second, precision=precise
    )
    out_im = jnp.einsum("gkn,nm->gkm", mid_re, sin_second, precision=precise) + jnp.einsum(
        "gkn,nm->gkm", mid_im, cos_second, precision=precise
    )
    return (out_re, out_im)


def inverse(spec_re, spec_im, tables):
    cos_first, sin_first, cos_second, sin_second, cos_twist, sin_twist = tables
    full_len = cos_first.shape[0] * cos_second.shape[0]
    mid_re = jnp.einsum("gkn,nm->gkm", spec_re, cos_second, precision=precise) + jnp.einsum(
        "gkn,nm->gkm", spec_im, sin_second, precision=precise
    )
    mid_im = jnp.einsum("gkn,nm->gkm", spec_im, cos_second, precision=precise) - jnp.einsum(
        "gkn,nm->gkm", spec_re, sin_second, precision=precise
    )
    turn_re = mid_re * cos_twist + mid_im * sin_twist
    turn_im = mid_im * cos_twist - mid_re * sin_twist
    result = jnp.einsum("kn,gkm->gnm", cos_first, turn_re, precision=precise) + jnp.einsum(
        "kn,gkm->gnm", sin_first, turn_im, precision=precise
    )
    return result * (1.0 / full_len)


def causal_taps(series, preceding, tap_weights):
    tok_rows = series.shape[0]
    span = tap_weights.shape[0]
    joined = jnp.concatenate([preceding, series], axis=0).astype(jnp.float32)
    running = jnp.zeros(series.shape, jnp.float32)
    for offset in range(span):
        first_row = span - 1 - offset
        running = running + tap_weights[offset][None, :] * joined[first_row : first_row + tok_rows]
    return running


def reverse_taps(series, following, tap_weights):
    tok_rows = series.shape[0]
    span = tap_weights.shape[0]
    joined = jnp.concatenate([series, following], axis=0).astype(jnp.float32)
    running = jnp.zeros(series.shape, jnp.float32)
    for offset in range(span):
        running = running + tap_weights[offset][None, :] * joined[offset : offset + tok_rows]
    return running


def general_shards(query_proj, key_proj, value_proj, short_taps, long_filter, grad_mixed):
    tok_rows, channels = query_proj.shape
    blocks = lax.axis_size("context")
    halo_rows = short_taps.shape[1] - 1
    per_device = channels // blocks
    seq_len = tok_rows * blocks
    tables = build_tables(blocks, tok_rows)
    preceding = from_behind(
        (
            query_proj[tok_rows - halo_rows :],
            key_proj[tok_rows - halo_rows :],
            value_proj[tok_rows - halo_rows :],
        ),
        "context",
        1,
    )
    query_f = causal_taps(query_proj, preceding[0], short_taps[0])
    key_f = causal_taps(key_proj, preceding[1], short_taps[1])
    value_f = causal_taps(value_proj, preceding[2], short_taps[2])
    gated_prod = (key_f * value_f).astype(jnp.bfloat16)
    grad_f = grad_mixed.astype(jnp.float32)
    grad_long = (grad_f * query_f).astype(jnp.bfloat16)

    def to_spectrum(series):
        arranged = series.T.reshape(blocks, per_device, tok_rows)
        received = lax.all_to_all(arranged, "context", split_axis=0, concat_axis=2, tiled=True)
        item_count = received.shape[1]
        signal = received.reshape(item_count, blocks, tok_rows).astype(jnp.float32)
        return transform(signal, tables)

    def to_token_rows(spatial):
        arrived = lax.all_to_all(spatial, "context", split_axis=1, concat_axis=0, tiled=True)
        return arrived.reshape(channels, tok_rows).T

    gate_re, gate_im = to_spectrum(gated_prod)
    filter_re, filter_im = transform(long_filter.reshape(per_device, blocks, tok_rows), tables)
    long_spatial = inverse(
        gate_re * filter_re - gate_im * filter_im, gate_re * filter_im + gate_im * filter_re, tables
    ).astype(jnp.bfloat16)
    long_conv = to_token_rows(long_spatial)
    long_f = long_conv.astype(jnp.float32)
    mixed_out = (query_f * long_f).astype(jnp.bfloat16)
    grad_query_f = (grad_f * long_f).astype(jnp.bfloat16)
    grad_after = lax.optimization_barrier((grad_long, long_conv))[0]
    grad_re, grad_im = to_spectrum(grad_after)
    back_spatial = inverse(
        filter_re * grad_re + filter_im * grad_im, filter_re * grad_im - filter_im * grad_re, tables
    ).astype(jnp.bfloat16)
    corr_spatial = inverse(
        gate_re * grad_re + gate_im * grad_im, gate_re * grad_im - gate_im * grad_re, tables
    )
    grad_gated = to_token_rows(back_spatial).astype(jnp.float32)
    grad_key_f = (grad_gated * value_f).astype(jnp.bfloat16)
    grad_value_f = (grad_gated * key_f).astype(jnp.bfloat16)
    following = from_behind(
        (grad_query_f[:halo_rows], grad_key_f[:halo_rows], grad_value_f[:halo_rows]), "context", -1
    )
    input_grads = jnp.stack(
        [
            reverse_taps(grad_query_f, following[0], short_taps[0]),
            reverse_taps(grad_key_f, following[1], short_taps[1]),
            reverse_taps(grad_value_f, following[2], short_taps[2]),
        ]
    ).astype(jnp.bfloat16)
    filter_grad = (corr_spatial * (1.0 / math.sqrt(seq_len))).reshape(1, per_device, seq_len)
    return (mixed_out, input_grads, filter_grad)


LANES = 128
VMEM_BYTES = 48 * 1024 * 1024


def split_bf16(table):
    high = table.astype(jnp.bfloat16)
    low = (table - high.astype(np.float64)).astype(jnp.bfloat16)
    return (high, low)


@functools.cache
def block_tables(rows):
    bins = np.pi * (np.arange(rows) + 0.5)[:, None] / rows
    lag = np.arange(rows)[None, :]
    forward = np.concatenate([np.cos(bins * lag), -np.sin(bins * lag)], axis=0)
    forward_hi, forward_lo = split_bf16(forward)
    return (forward_hi, forward_lo, split_bf16(forward.T / rows)[0])


def round_up(count, unit):
    return (count + unit - 1) // unit * unit


def head_rows(fresh, whole, halo):
    row = lax.broadcasted_iota(jnp.int32, fresh.shape, 0)
    return jnp.concatenate([jnp.where(row < halo, fresh, whole[:8]), whole[8:]], axis=0)


def tap_rows(taps_ref, which, lanes):
    return [taps_ref[which, pl.ds(offset, 1), lanes] for offset in range(taps_ref.shape[1])]


def short_filter(padded, rows, weights):
    running = weights[0] * padded[pl.ds(8, rows), :]
    for offset in range(1, len(weights)):
        running = running + weights[offset] * padded[pl.ds(8 - offset, rows), :]
    return running


def send_kernel(order, places, extras, q_ref, k_ref, v_ref, g_ref, taps_ref, *refs):
    sources, refs = refs[:extras], refs[extras:]
    outs, refs = refs[: len(places)], refs[len(places) :]
    landed, taps, padded, extra, arrivals, kept = refs[-6:]
    filtered_ref, *brought = refs[:-6]
    me = lax.axis_index("context")
    rows = q_ref.shape[0]
    halo = taps_ref.shape[1] - 1

    def fetches(index):
        lanes = pl.ds(pl.multiple_of((me ^ order[places[index]]) * LANES, LANES), LANES)
        copies = [
            pltpu.make_async_copy(taps_ref.at[:, :, lanes], taps.at[index], arrivals.at[index, 4])
        ]
        for which, ref in enumerate((q_ref, k_ref, v_ref, g_ref)):
            copies.append(
                pltpu.make_async_copy(
                    ref.at[:, lanes], landed.at[index, which], arrivals.at[index, which]
                )
            )
        return copies

    keeps = [
        pltpu.make_async_copy(source, target, kept.at[index])
        for index, (source, target) in enumerate(zip(sources, brought))
    ]
    for index in range(len(places)):
        for copy in fetches(index):
            copy.start()
    for copy in keeps:
        copy.start()
    for index in range(len(places)):
        slot = index % padded.shape[0]
        out_ref = outs[index]
        padded[slot, :, pl.ds(0, 8), :] = jnp.zeros((3, 8, LANES), jnp.float32)
        extra[slot, pl.ds(5 * halo, extra.shape[1] - 5 * halo), :] = jnp.zeros(
            (extra.shape[1] - 5 * halo, LANES), jnp.float32
        )
        for copy in fetches(index):
            copy.wait()
        filtered = []
        for which in range(3):
            padded[slot, which, pl.ds(8, rows), :] = landed[index, which].astype(jnp.float32)
            weights = tap_rows(taps.at[index], which, pl.ds(0, LANES))
            result = short_filter(padded.at[slot, which], rows, weights)
            filtered_ref[which, index] = result
            filtered.append(result)
        query_f, key_f, value_f = filtered
        cotangent = landed[index, 3].astype(jnp.float32)
        gated = head_rows(padded[slot, 1, pl.ds(8, 8), :], key_f * value_f, halo)
        grad_long = head_rows(cotangent[:8], cotangent * query_f, halo)
        out_ref[pl.ds(0, rows), :] = gated.astype(jnp.bfloat16)
        out_ref[pl.ds(rows, rows), :] = grad_long.astype(jnp.bfloat16)
        pieces = ((1, rows - halo), (2, 0), (2, rows - halo), (0, 0), (0, rows - halo))
        for position, (which, first) in enumerate(pieces):
            extra[slot, pl.ds(position * halo, halo), :] = padded[slot, which, pl.ds(8 + first, halo), :]
        out_ref[pl.ds(2 * rows, extra.shape[1]), :] = extra[slot].astype(jnp.bfloat16)
    if order[places[-1]] == 0:
        brought[-1][...] = taps[len(places) - 1]
    for copy in keeps:
        copy.wait()


def gather(order, in_refs, edges, firsts, pairs, rows):
    me = lax.axis_index("context")
    for mask, in_ref in zip(order, in_refs):
        block = me ^ mask
        edges[block] = in_ref[pl.ds(2 * rows, edges.shape[1]), :].astype(jnp.float32)
        for which in range(2):
            values = in_ref[pl.ds(which * rows, rows), :]
            firsts[block, which] = values[:16].astype(jnp.float32)[:8]
            pairs[block, :, pl.ds(which * LANES, LANES)] = values


def repair_heads(taps_ref, edges, firsts, joined, heads):
    blocks = edges.shape[0]
    span = taps_ref.shape[1]
    halo = span - 1
    joined[...] = jnp.zeros(joined.shape, jnp.float32)
    for block in range(blocks):
        joined[1, block, pl.ds(halo, 8), :] = firsts[block, 0]
        joined[2, block, pl.ds(halo, halo), :] = edges[block, pl.ds(halo, halo), :]
        joined[0, block, pl.ds(halo, halo), :] = edges[block, pl.ds(3 * halo, halo), :]
        if block > 0:
            for which, place in ((1, 0), (2, 2), (0, 4)):
                joined[which, block, pl.ds(0, halo), :] = edges[block - 1, pl.ds(place * halo, halo), :]
        filtered = []
        for which in range(3):
            running = jnp.zeros((8, LANES), jnp.float32)
            for offset in range(span):
                weight = taps_ref[which, pl.ds(offset, 1), :]
                running = running + weight * joined[which, block, pl.ds(halo - offset, 8), :]
            filtered.append(running)
            heads[block, which] = running
        cotangent = firsts[block, 1]
        heads[block, 3] = cotangent
        heads[block, 4] = filtered[1] * filtered[2]
        heads[block, 5] = cotangent * filtered[0]


def to_spectra(heads, pairs, forward, spec_x, spec_g, halo):
    blocks, rows, width = pairs.shape
    merged = blocks // spec_x.shape[0]
    for block in range(blocks):
        fresh = jnp.concatenate([heads[block, 4], heads[block, 5]], axis=1)
        head = head_rows(fresh, pairs[block, pl.ds(0, 16), :].astype(jnp.float32), halo)
        pairs[block, pl.ds(0, 16), :] = head.astype(jnp.bfloat16)
    for index in range(spec_x.shape[0]):
        signals = pairs[pl.ds(index * merged, merged)].reshape(merged * rows, width)
        spectrum = jnp.dot(forward, signals, preferred_element_type=jnp.float32)
        spec_x[index] = spectrum[:, :LANES]
        spec_g[index] = spectrum[:, LANES:]


def filter_kernel(h_ref, forward_hi, forward_lo, out_ref):
    blocks, two_rows, _ = out_ref.shape
    rows = two_rows // 2
    sign = jnp.where(lax.broadcasted_iota(jnp.int32, (rows, LANES), 0) % 2 == 0, 1.0, -1.0)

    def product(table, values):
        return lax.dot_general(
            table, values, (((1,), (1,)), ((), ())), preferred_element_type=jnp.float32
        )

    before = None
    for block in range(blocks):
        signal = h_ref[:, pl.ds(block * rows, rows)]
        high = signal.astype(jnp.bfloat16)
        low = (signal - high.astype(jnp.float32)).astype(jnp.bfloat16)
        spectrum = (
            product(forward_hi[...], high)
            + product(forward_lo[...], high)
            + product(forward_hi[...], low)
        )
        real, imag = spectrum[:rows], spectrum[rows:]
        if before is None:
            out_ref[block] = spectrum
        else:
            out_ref[block, pl.ds(0, rows), :] = real - sign * before[1]
            out_ref[block, pl.ds(rows, rows), :] = imag + sign * before[0]
        before = (real, imag)


def load_tile(ref, count, tile, bins):
    real = [ref[index, pl.ds(pl.multiple_of(tile * 8, 8), 8), :] for index in range(count)]
    imag = [ref[index, pl.ds(pl.multiple_of(bins + tile * 8, 8), 8), :] for index in range(count)]
    return (real, imag)


def mixed_products(left, right, sums, conjugate):
    (left_re, left_im), (right_re, right_im) = left, right
    results = []
    for pairs in sums:
        total_re, total_im = None, None
        for one, two in pairs:
            a, b, c, d = left_re[one], left_im[one], right_re[two], right_im[two]
            if conjugate:
                real, imag = a * c + b * d, a * d - b * c
            else:
                real, imag = a * c - b * d, a * d + b * c
            total_re = real if total_re is None else total_re + real
            total_im = imag if total_im is None else total_im + imag
        results.append((total_re, total_im))
    return results


def store_tiles(ref, first_lane, tiles, pair, bins):
    lanes = pl.ds(first_lane, LANES)
    for index, parts in enumerate(zip(*tiles)):
        for first, values in zip((0, bins), zip(*parts)):
            rows = pl.ds(pl.multiple_of(first + pair * 16, 16), 16)
            ref[index, rows, lanes] = jnp.concatenate(values, axis=0).astype(ref.dtype)


def convolve_kernel(order, taps_ref, spec_h, forward, inverse, *refs):
    count = len(order)
    in_refs, out_refs = refs[:count], refs[count : 2 * count]
    spec_x, spec_g, edges, firsts, joined, heads, pairs, spec_y, extra = refs[2 * count :]
    me = lax.axis_index("context")
    rows = pairs.shape[1]
    halo = taps_ref.shape[1] - 1
    bins = inverse.shape[0]
    wide = spec_h.shape[0]
    gather(order, in_refs, edges, firsts, pairs, rows)
    repair_heads(taps_ref, edges, firsts, joined, heads)
    to_spectra(heads, pairs, forward[...], spec_x, spec_g, halo)

    def body(pair, carry):
        longs, backs = [], []
        for tile in (2 * pair, 2 * pair + 1):
            filt = load_tile(spec_h, wide, tile, bins)
            sums = [[(i - j, j) for j in range(i + 1)] for i in range(wide)]
            longs.append(mixed_products(filt, load_tile(spec_x, wide, tile, bins), sums, False))
            sums = [[(j - i, j) for j in range(i, wide)] for i in range(wide)]
            backs.append(mixed_products(filt, load_tile(spec_g, wide, tile, bins), sums, True))
        store_tiles(spec_y, 0, longs, pair, bins)
        store_tiles(spec_y, LANES, backs, pair, bins)
        return carry

    lax.fori_loop(0, bins // 16, body, 0)
    extra[...] = jnp.zeros(extra.shape, jnp.float32)
    for index in range(wide):
        both = jnp.dot(inverse[...], spec_y[index], preferred_element_type=jnp.float32).astype(jnp.bfloat16)
        for part in range(count // wide):
            block = index * (count // wide) + part
            here = both[part * rows : (part + 1) * rows]
            query_f, key_f, value_f, cotangent = [heads[block, which] for which in range(4)]
            head = here[:16].astype(jnp.float32)
            long_head, back_head = head[:8, :LANES], head[:8, LANES:]
            grad_key, grad_value = back_head * value_f, back_head * key_f
            back = head_rows(grad_key, head[:, LANES:], halo).astype(jnp.bfloat16)
            pairs[block, :, pl.ds(0, LANES)] = here[:, :LANES]
            pairs[block, :, pl.ds(LANES, LANES)] = jnp.concatenate([back, here[16:, LANES:]], axis=0)
            own = (query_f * long_head, grad_value)
            following = (cotangent * long_head, grad_key, grad_value)
            for place, value in enumerate(own):
                extra[block + 1, pl.ds(place * halo, halo), :] = value[:halo]
            for place, value in enumerate(following):
                extra[block, pl.ds((2 + place) * halo, halo), :] = value[:halo]
    for mask, out_ref in zip(order, out_refs):
        block = me ^ mask
        for which in range(2):
            out_ref[pl.ds(which * rows, rows), :] = pairs[block, :, pl.ds(which * LANES, LANES)]
        out_ref[pl.ds(2 * rows, extra.shape[1]), :] = extra[block + 1].astype(jnp.bfloat16)


def correlate_kernel(scale, spec_x, spec_g, inverse, out_ref, spec_y):
    wide = spec_x.shape[0]
    bins = inverse.shape[0]

    def body(pair, carry):
        row = lax.broadcasted_iota(jnp.int32, (8, LANES), 0)
        sign = jnp.where(row % 2 == 0, 1.0, -1.0)
        tiles = []
        for tile in (2 * pair, 2 * pair + 1):
            real, imag = load_tile(spec_x, wide, tile, bins)
            window_re = [real[0]] + [real[i] - sign * imag[i - 1] for i in range(1, wide)]
            window_im = [imag[0]] + [imag[i] + sign * real[i - 1] for i in range(1, wide)]
            sums = [[(j - lag, j) for j in range(lag, wide)] for lag in range(wide)]
            grad = load_tile(spec_g, wide, tile, bins)
            tiles.append(mixed_products((window_re, window_im), grad, sums, True))
        store_tiles(spec_y, 0, tiles, pair, bins)
        return carry

    lax.fori_loop(0, bins // 16, body, 0)
    for index in range(wide):
        result = jnp.dot(inverse[...], spec_y[index], preferred_element_type=jnp.float32)
        out_ref[:, pl.ds(index * bins, bins)] = result.T * scale


def finish_channels(
    order, places, in_refs, g_ref, taps_ref, far_ref, near_ref, padded, extra, results, leave
):
    me = lax.axis_index("context")
    rows = g_ref.shape[0]
    span = taps_ref.shape[1]
    halo = span - 1
    for index, (place, in_ref) in enumerate(zip(places, in_refs)):
        lanes = pl.ds(pl.multiple_of((me ^ order[place]) * LANES, LANES), LANES)
        slot = index % padded.shape[0]
        edge_rows = in_ref.shape[0] - 2 * rows
        far_count = far_ref.shape[1]
        held, spot = (far_ref, place) if place < far_count else (near_ref, place - far_count)
        query_f, key_f, value_f = [held[which, spot] for which in range(3)]
        cotangent = g_ref[:, lanes].astype(jnp.float32)
        long_conv = in_ref[pl.ds(0, rows), :].astype(jnp.float32)
        back = in_ref[pl.ds(rows, rows), :].astype(jnp.float32)
        extra[slot, pl.ds(0, edge_rows), :] = in_ref[pl.ds(2 * rows, edge_rows), :].astype(jnp.float32)
        mixed = head_rows(extra[slot, pl.ds(0, 8), :], query_f * long_conv, halo)
        results[index, 3] = mixed.astype(jnp.bfloat16)
        leave(index, 3)
        grads = (
            cotangent * long_conv,
            head_rows(back[:8], back * value_f, halo),
            head_rows(extra[slot, pl.ds(halo, 8), :], back * key_f, halo),
        )
        for which, grad in enumerate(grads):
            padded[slot, which, pl.ds(0, rows), :] = grad.astype(jnp.bfloat16).astype(jnp.float32)
            padded[slot, which, pl.ds(rows, halo), :] = extra[slot, pl.ds((2 + which) * halo, halo), :]
            weights = tap_rows(taps_ref, which, lanes)
            running = weights[0] * padded[slot, which, pl.ds(0, rows), :]
            for offset in range(1, span):
                running = running + weights[offset] * padded[slot, which, pl.ds(offset, rows), :]
            results[index, which] = running.astype(jnp.bfloat16)
            leave(index, which)


def receive_kernel(order, places, g_ref, taps_ref, far_ref, near_ref, filter_ref, *refs):
    in_refs = refs[: len(places)]
    mixed_ref, grads_ref, filter_out, padded, extra, results, sems, filter_sem = refs[-8:]
    me = lax.axis_index("context")
    copies = []
    if filter_ref is not None:
        copies.append(pltpu.make_async_copy(filter_ref, filter_out.at[0], filter_sem))
        copies[-1].start()

    def leave(index, which):
        lanes = pl.ds(pl.multiple_of((me ^ order[places[index]]) * LANES, LANES), LANES)
        target = mixed_ref.at[:, lanes] if which == 3 else grads_ref.at[which, :, lanes]
        copies.append(pltpu.make_async_copy(results.at[index, which], target, sems.at[index, which]))
        copies[-1].start()

    finish_channels(
        order, places, in_refs, g_ref, taps_ref, far_ref, near_ref, padded, extra, results, leave
    )
    for copy in copies:
        copy.wait()


def last_kernel(order, places, g_ref, taps_ref, far_ref, near_ref, *refs):
    in_refs, refs = refs[: len(places)], refs[len(places) + 2 :]
    mixed_ref, grads_ref, padded, extra, results, sems = refs
    receive_kernel(
        order, places, g_ref, taps_ref, far_ref, near_ref, None, *in_refs,
        mixed_ref, grads_ref, None, padded, extra, results, sems, None,
    )


def on_device(kernel, out_shape, scratch, args, in_hbm=(), unread=None, updates=()):
    whole = pl.BlockSpec(memory_space=pltpu.VMEM)
    hbm = pl.BlockSpec(memory_space=pltpu.HBM)
    anywhere = pl.BlockSpec(memory_space=pl.ANY)
    fixed = [pltpu.with_memory_space_constraint(arg, pltpu.HBM) for arg in in_hbm]
    before = [] if unread is None else [unread]
    first_update = len(before) + len(fixed) + len(args)
    return pl.pallas_call(
        kernel if unread is None else lambda _, *refs: kernel(*refs),
        out_shape=out_shape,
        in_specs=[anywhere] * len(before) + [hbm] * len(fixed) + [whole] * len(args) + [hbm] * len(updates),
        out_specs=jax.tree.map(
            lambda out: whole if isinstance(out, jax.ShapeDtypeStruct) else hbm, out_shape
        ),
        input_output_aliases={first_update + place: place for place in range(len(updates))},
        scratch_shapes=[
            pltpu.VMEM(shape, jnp.float32) if isinstance(shape, tuple) else shape for shape in scratch
        ],
        compiler_params=pltpu.CompilerParams(vmem_limit_bytes=VMEM_BYTES),
    )(*before, *fixed, *args, *updates)


def exchange_order(count):
    return sorted(
        range(count),
        key=lambda mask: (mask == 0, -(mask >> 1).bit_count(), mask % 2, mask if mask % 2 else -mask),
    )


def exchange(parcel, mask):
    count = lax.axis_size("context")
    return lax.ppermute(parcel, "context", [(i, i ^ mask) for i in range(count)])


def block_shards(query_proj, key_proj, value_proj, short_taps, long_filter, grad_mixed):
    rows, channels = query_proj.shape
    blocks = lax.axis_size("context")
    halo = short_taps.shape[1] - 1
    seq_len = rows * blocks
    merged = 2
    wide = merged * rows
    forward_hi, forward_lo, inverse = [jnp.asarray(table) for table in block_tables(wide)]
    edge_rows = round_up(5 * halo, 16)
    order = exchange_order(blocks)
    parcels = [jax.ShapeDtypeStruct((2 * rows + edge_rows, LANES), jnp.bfloat16)] * blocks
    spectra = (blocks // merged, 2 * wide, LANES)
    own_taps = (*short_taps.shape[:2], LANES)
    far = [place for place in range(blocks) if order[place] > 1]
    near = [place for place in range(blocks) if order[place] <= 1]

    def send(places, sources=(), unread=None):
        return on_device(
            functools.partial(send_kernel, order, places, len(sources)),
            [parcels[place] for place in places]
            + [
                jax.ShapeDtypeStruct((3, len(places), rows, LANES), jnp.float32),
            ]
            + [jax.ShapeDtypeStruct(value.shape, value.dtype) for value in sources]
            + [jax.ShapeDtypeStruct(own_taps, jnp.float32)] * (order[places[-1]] == 0),
            [
                pltpu.VMEM((len(places), 4, rows, LANES), jnp.bfloat16),
                (len(places), *own_taps),
                (2, 3, rows + 8, LANES),
                (2, edge_rows, LANES),
                pltpu.SemaphoreType.DMA((len(places), 5)),
                pltpu.SemaphoreType.DMA((max(1, len(sources)),)),
            ],
            (),
            in_hbm=(query_proj, key_proj, value_proj, grad_mixed, short_taps, *sources),
            unread=unread,
        )

    *sent, far_filtered = send(far)
    arrived = [exchange(parcel, order[place]) for place, parcel in zip(far, sent)]
    *sent, near_filtered, filter_here, hi_here, lo_here, own = send(
        near, (long_filter[0], forward_hi, forward_lo), arrived[0]
    )
    arrived += [exchange(sent[0], order[near[0]]), sent[1]]
    spec_h = on_device(
        filter_kernel,
        jax.ShapeDtypeStruct(spectra, jnp.float32),
        [],
        (filter_here, hi_here, lo_here),
    )
    *results, spec_x, spec_g = on_device(
        functools.partial(convolve_kernel, order),
        parcels + [jax.ShapeDtypeStruct(spectra, jnp.float32)] * 2,
        [
            (blocks, edge_rows, LANES),
            (blocks, 2, 8, LANES),
            (3, blocks, 24, LANES),
            (blocks, 6, 8, LANES),
            pltpu.VMEM((blocks, rows, 2 * LANES), jnp.bfloat16),
            pltpu.VMEM((*spectra[:2], 2 * LANES), jnp.bfloat16),
            (blocks + 1, edge_rows, LANES),
        ],
        (own, spec_h, hi_here, inverse, *arrived),
    )
    returned = [exchange(parcel, mask) if mask else parcel for mask, parcel in zip(order, results)]
    filter_grad = on_device(
        functools.partial(correlate_kernel, 1.0 / math.sqrt(seq_len)),
        jax.ShapeDtypeStruct(long_filter.shape[1:], jnp.float32),
        [pltpu.VMEM(spectra, jnp.bfloat16)],
        (spec_x, spec_g, inverse),
    )
    late = far[len(far) // 2 :] + near[:-1]
    early = [place for place in range(blocks) if place not in late]
    outputs = (
        pltpu.HBM((rows, channels), jnp.bfloat16),
        pltpu.HBM((3, rows, channels), jnp.bfloat16),
        pltpu.HBM(long_filter.shape, jnp.float32),
    )

    def working(places):
        return [
            (2, 3, rows + 16, LANES),
            (2, edge_rows + 8, LANES),
            pltpu.VMEM((len(places), 4, rows, LANES), jnp.bfloat16),
            pltpu.SemaphoreType.DMA((len(places), 4)),
        ]

    common = (grad_mixed, short_taps, far_filtered, near_filtered)
    *begun, filter_grad = on_device(
        functools.partial(receive_kernel, order, early),
        outputs,
        [*working(early), pltpu.SemaphoreType.DMA(())],
        (*common, filter_grad, *(returned[place] for place in early)),
    )
    mixed_out, input_grads = on_device(
        functools.partial(last_kernel, order, late),
        outputs[:2],
        working(late),
        (*common, *(returned[place] for place in late)),
        updates=begun,
    )
    return (mixed_out, input_grads, filter_grad)


def shards(query_proj, key_proj, value_proj, short_taps, long_filter, grad_mixed):
    rows, channels = query_proj.shape
    halo = short_taps.shape[1] - 1
    blocks = lax.axis_size("context")
    power_of_two = blocks & (blocks - 1) == 0
    fits = power_of_two and blocks > 1 and channels == blocks * LANES and rows % 128 == 0 and halo <= 8
    chosen = block_shards if fits else general_shards
    return chosen(query_proj, key_proj, value_proj, short_taps, long_filter, grad_mixed)


def solution(mesh):
    return jax.shard_map(
        shards,
        mesh=mesh,
        in_specs=(
            P("context", "tensor"),
            P("context", "tensor"),
            P("context", "tensor"),
            P(None, None, "tensor"),
            P("tensor", "context", None),
            P("context", "tensor"),
        ),
        out_specs=(
            P("context", "tensor"),
            P(None, "context", "tensor"),
            P("tensor", "context", None),
        ),
        check_vma=False,
    )
```

```python
import functools
import math

import jax
import jax.numpy as jnp
import numpy as np
from jax import lax
from jax.experimental import pallas as pl
from jax.experimental.pallas import tpu as pltpu
from jax.sharding import PartitionSpec as P

precise = lax.Precision.HIGHEST


def from_behind(value, axis, steps):
    count = lax.axis_size(axis)
    first, last = (max(0, -steps), min(count, count - steps))
    return lax.ppermute(value, axis, [(source, source + steps) for source in range(first, last)])


def build_tables(blocks, tok_rows):
    outer_len = 2 * blocks
    full_len = outer_len * tok_rows
    k_one = jnp.arange(outer_len, dtype=jnp.int32)
    n_one = jnp.arange(blocks, dtype=jnp.int32)
    position = jnp.arange(tok_rows, dtype=jnp.int32)
    first_idx = k_one[:, None] * n_one[None, :] % outer_len
    first_angle = -2.0 * math.pi / outer_len * first_idx.astype(jnp.float32)
    second = position[:, None] * position[None, :] % tok_rows
    second_angle = -2.0 * math.pi / tok_rows * second.astype(jnp.float32)
    twist_idx = k_one[:, None] * position[None, :] % full_len
    twist_angle = -2.0 * math.pi / full_len * twist_idx.astype(jnp.float32)
    return (
        jnp.cos(first_angle),
        jnp.sin(first_angle),
        jnp.cos(second_angle),
        jnp.sin(second_angle),
        jnp.cos(twist_angle),
        jnp.sin(twist_angle),
    )


def transform(signal, tables):
    cos_first, sin_first, cos_second, sin_second, cos_twist, sin_twist = tables
    first_re = jnp.einsum("kn,gnm->gkm", cos_first, signal, precision=precise)
    first_im = jnp.einsum("kn,gnm->gkm", sin_first, signal, precision=precise)
    mid_re = first_re * cos_twist - first_im * sin_twist
    mid_im = first_re * sin_twist + first_im * cos_twist
    out_re = jnp.einsum("gkn,nm->gkm", mid_re, cos_second, precision=precise) - jnp.einsum(
        "gkn,nm->gkm", mid_im, sin_second, precision=precise
    )
    out_im = jnp.einsum("gkn,nm->gkm", mid_re, sin_second, precision=precise) + jnp.einsum(
        "gkn,nm->gkm", mid_im, cos_second, precision=precise
    )
    return (out_re, out_im)


def inverse(spec_re, spec_im, tables):
    cos_first, sin_first, cos_second, sin_second, cos_twist, sin_twist = tables
    full_len = cos_first.shape[0] * cos_second.shape[0]
    mid_re = jnp.einsum("gkn,nm->gkm", spec_re, cos_second, precision=precise) + jnp.einsum(
        "gkn,nm->gkm", spec_im, sin_second, precision=precise
    )
    mid_im = jnp.einsum("gkn,nm->gkm", spec_im, cos_second, precision=precise) - jnp.einsum(
        "gkn,nm->gkm", spec_re, sin_second, precision=precise
    )
    turn_re = mid_re * cos_twist + mid_im * sin_twist
    turn_im = mid_im * cos_twist - mid_re * sin_twist
    result = jnp.einsum("kn,gkm->gnm", cos_first, turn_re, precision=precise) + jnp.einsum(
        "kn,gkm->gnm", sin_first, turn_im, precision=precise
    )
    return result * (1.0 / full_len)


def causal_taps(series, preceding, tap_weights):
    tok_rows = series.shape[0]
    span = tap_weights.shape[0]
    joined = jnp.concatenate([preceding, series], axis=0).astype(jnp.float32)
    running = jnp.zeros(series.shape, jnp.float32)
    for offset in range(span):
        first_row = span - 1 - offset
        running = running + tap_weights[offset][None, :] * joined[first_row : first_row + tok_rows]
    return running


def reverse_taps(series, following, tap_weights):
    tok_rows = series.shape[0]
    span = tap_weights.shape[0]
    joined = jnp.concatenate([series, following], axis=0).astype(jnp.float32)
    running = jnp.zeros(series.shape, jnp.float32)
    for offset in range(span):
        running = running + tap_weights[offset][None, :] * joined[offset : offset + tok_rows]
    return running


def general_shards(query_proj, key_proj, value_proj, short_taps, long_filter, grad_mixed):
    tok_rows, channels = query_proj.shape
    blocks = lax.axis_size("context")
    halo_rows = short_taps.shape[1] - 1
    per_device = channels // blocks
    seq_len = tok_rows * blocks
    tables = build_tables(blocks, tok_rows)
    preceding = from_behind(
        (
            query_proj[tok_rows - halo_rows :],
            key_proj[tok_rows - halo_rows :],
            value_proj[tok_rows - halo_rows :],
        ),
        "context",
        1,
    )
    query_f = causal_taps(query_proj, preceding[0], short_taps[0])
    key_f = causal_taps(key_proj, preceding[1], short_taps[1])
    value_f = causal_taps(value_proj, preceding[2], short_taps[2])
    gated_prod = (key_f * value_f).astype(jnp.bfloat16)
    grad_f = grad_mixed.astype(jnp.float32)
    grad_long = (grad_f * query_f).astype(jnp.bfloat16)

    def to_spectrum(series):
        arranged = series.T.reshape(blocks, per_device, tok_rows)
        received = lax.all_to_all(arranged, "context", split_axis=0, concat_axis=2, tiled=True)
        item_count = received.shape[1]
        signal = received.reshape(item_count, blocks, tok_rows).astype(jnp.float32)
        return transform(signal, tables)

    def to_token_rows(spatial):
        arrived = lax.all_to_all(spatial, "context", split_axis=1, concat_axis=0, tiled=True)
        return arrived.reshape(channels, tok_rows).T

    gate_re, gate_im = to_spectrum(gated_prod)
    filter_re, filter_im = transform(long_filter.reshape(per_device, blocks, tok_rows), tables)
    long_spatial = inverse(
        gate_re * filter_re - gate_im * filter_im, gate_re * filter_im + gate_im * filter_re, tables
    ).astype(jnp.bfloat16)
    long_conv = to_token_rows(long_spatial)
    long_f = long_conv.astype(jnp.float32)
    mixed_out = (query_f * long_f).astype(jnp.bfloat16)
    grad_query_f = (grad_f * long_f).astype(jnp.bfloat16)
    grad_after = lax.optimization_barrier((grad_long, long_conv))[0]
    grad_re, grad_im = to_spectrum(grad_after)
    back_spatial = inverse(
        filter_re * grad_re + filter_im * grad_im, filter_re * grad_im - filter_im * grad_re, tables
    ).astype(jnp.bfloat16)
    corr_spatial = inverse(
        gate_re * grad_re + gate_im * grad_im, gate_re * grad_im - gate_im * grad_re, tables
    )
    grad_gated = to_token_rows(back_spatial).astype(jnp.float32)
    grad_key_f = (grad_gated * value_f).astype(jnp.bfloat16)
    grad_value_f = (grad_gated * key_f).astype(jnp.bfloat16)
    following = from_behind(
        (grad_query_f[:halo_rows], grad_key_f[:halo_rows], grad_value_f[:halo_rows]), "context", -1
    )
    input_grads = jnp.stack(
        [
            reverse_taps(grad_query_f, following[0], short_taps[0]),
            reverse_taps(grad_key_f, following[1], short_taps[1]),
            reverse_taps(grad_value_f, following[2], short_taps[2]),
        ]
    ).astype(jnp.bfloat16)
    filter_grad = (corr_spatial * (1.0 / math.sqrt(seq_len))).reshape(1, per_device, seq_len)
    return (mixed_out, input_grads, filter_grad)


LANES = 128
VMEM_BYTES = 48 * 1024 * 1024
COVER = pl.CostEstimate(flops=10**10, bytes_accessed=10**8, transcendentals=0)


def split_bf16(table):
    high = table.astype(jnp.bfloat16)
    low = (table - high.astype(np.float64)).astype(jnp.bfloat16)
    return (high, low)


@functools.cache
def block_tables(rows):
    bins = np.pi * (np.arange(rows) + 0.5)[:, None] / rows
    lag = np.arange(rows)[None, :]
    forward = np.concatenate([np.cos(bins * lag), -np.sin(bins * lag)], axis=0)
    forward_hi, forward_lo = split_bf16(forward)
    return (forward_hi, forward_lo, split_bf16(forward.T / rows)[0])


def round_up(count, unit):
    return (count + unit - 1) // unit * unit


def head_rows(fresh, whole, halo):
    row = lax.broadcasted_iota(jnp.int32, fresh.shape, 0)
    return jnp.concatenate([jnp.where(row < halo, fresh, whole[:8]), whole[8:]], axis=0)


def tap_rows(taps_ref, which, lanes):
    return [taps_ref[which, pl.ds(offset, 1), lanes] for offset in range(taps_ref.shape[1])]


def short_filter(padded, rows, weights):
    running = weights[0] * padded[pl.ds(8, rows), :]
    for offset in range(1, len(weights)):
        running = running + weights[offset] * padded[pl.ds(8 - offset, rows), :]
    return running


def make_parcel(slot, source, taps, padded, extra, filtered_ref, out_ref):
    rows = source.shape[1]
    halo = taps.shape[1] - 1
    padded[slot, :, pl.ds(0, 8), :] = jnp.zeros((3, 8, LANES), jnp.float32)
    extra[slot, pl.ds(5 * halo, extra.shape[1] - 5 * halo), :] = jnp.zeros(
        (extra.shape[1] - 5 * halo, LANES), jnp.float32
    )
    filtered = []
    for which in range(3):
        padded[slot, which, pl.ds(8, rows), :] = source[which].astype(jnp.float32)
        weights = tap_rows(taps, which, pl.ds(0, LANES))
        result = short_filter(padded.at[slot, which], rows, weights)
        filtered_ref[which] = result
        filtered.append(result)
    query_f, key_f, value_f = filtered
    cotangent = source[3].astype(jnp.float32)
    gated = head_rows(padded[slot, 1, pl.ds(8, 8), :], key_f * value_f, halo)
    grad_long = head_rows(cotangent[:8], cotangent * query_f, halo)
    out_ref[pl.ds(0, rows), :] = gated.astype(jnp.bfloat16)
    out_ref[pl.ds(rows, rows), :] = grad_long.astype(jnp.bfloat16)
    pieces = ((1, rows - halo), (2, 0), (2, rows - halo), (0, 0), (0, rows - halo))
    for position, (which, first) in enumerate(pieces):
        extra[slot, pl.ds(position * halo, halo), :] = padded[slot, which, pl.ds(8 + first, halo), :]
    out_ref[pl.ds(2 * rows, extra.shape[1]), :] = extra[slot].astype(jnp.bfloat16)


def fetches(order, places, inputs, taps_ref, landed, taps, arrivals):
    me = lax.axis_index("context")
    result = []
    for index, place in enumerate(places):
        lanes = pl.ds(pl.multiple_of((me ^ order[place]) * LANES, LANES), LANES)
        sources = [taps_ref.at[:, :, lanes]] + [ref.at[:, lanes] for ref in inputs]
        targets = [taps.at[index]] + [landed.at[index, which] for which in range(len(inputs))]
        result.append(
            [
                pltpu.make_async_copy(source, target, arrivals.at[index, number])
                for number, (source, target) in enumerate(zip(sources, targets))
            ]
        )
    return result


def send_kernel(order, places, ahead, extras, q_ref, k_ref, v_ref, g_ref, taps_ref, *refs):
    inputs = (q_ref, k_ref, v_ref, g_ref)
    sources, refs = refs[:extras], refs[extras:]
    first_ref, *outs = refs[: len(places) - 1]
    size = first_ref.shape[0] // 2
    outs = [first_ref.at[pl.ds(0, size)], first_ref.at[pl.ds(size, size)], *outs]
    filtered_ref, *brought = refs[len(places) - 1 : -7]
    landed, taps, padded, extra, arrivals, later, kept = refs[-7:]
    own = fetches(order, places, inputs, taps_ref, landed, taps, arrivals)
    others = [
        pltpu.make_async_copy(source, target, kept.at[index])
        for index, (source, target) in enumerate(zip(sources, brought))
    ]
    for copies in fetches(order, ahead, inputs, taps_ref, *brought[-2:], later):
        others += copies
    for copies in own:
        for copy in copies:
            copy.start()
    for copy in others:
        copy.start()
    for index, copies in enumerate(own):
        for copy in copies:
            copy.wait()
        make_parcel(
            index % 2, landed.at[index], taps.at[index], padded, extra, filtered_ref.at[index], outs[index]
        )
    for copy in others:
        copy.wait()


def near_kernel(landed, taps, first_ref, shared_ref, own_ref, filtered_ref, own_taps, padded, extra):
    rows = own_ref.shape[0]
    shared_ref[pl.ds(rows, rows), :] = first_ref[pl.ds(rows, rows), :]
    for index, out_ref in enumerate((shared_ref.at[pl.ds(0, rows)], own_ref)):
        make_parcel(
            index, landed.at[index], taps.at[index], padded, extra, filtered_ref.at[index], out_ref
        )
    own_taps[...] = taps[1]


def gather(order, in_refs, edges, firsts, pairs, rows):
    me = lax.axis_index("context")
    for mask, in_ref in zip(order, in_refs):
        block = me ^ mask
        edges[block] = in_ref[pl.ds(2 * rows, edges.shape[1]), :].astype(jnp.float32)
        for which in range(2):
            values = in_ref[pl.ds(which * rows, rows), :]
            firsts[block, which] = values[:16].astype(jnp.float32)[:8]
            pairs[block, :, pl.ds(which * LANES, LANES)] = values


def repair_heads(taps_ref, edges, firsts, joined, heads):
    blocks = edges.shape[0]
    span = taps_ref.shape[1]
    halo = span - 1
    joined[...] = jnp.zeros(joined.shape, jnp.float32)
    for block in range(blocks):
        joined[1, block, pl.ds(halo, 8), :] = firsts[block, 0]
        joined[2, block, pl.ds(halo, halo), :] = edges[block, pl.ds(halo, halo), :]
        joined[0, block, pl.ds(halo, halo), :] = edges[block, pl.ds(3 * halo, halo), :]
        if block > 0:
            for which, place in ((1, 0), (2, 2), (0, 4)):
                joined[which, block, pl.ds(0, halo), :] = edges[block - 1, pl.ds(place * halo, halo), :]
        filtered = []
        for which in range(3):
            running = jnp.zeros((8, LANES), jnp.float32)
            for offset in range(span):
                weight = taps_ref[which, pl.ds(offset, 1), :]
                running = running + weight * joined[which, block, pl.ds(halo - offset, 8), :]
            filtered.append(running)
            heads[block, which] = running
        cotangent = firsts[block, 1]
        heads[block, 3] = cotangent
        heads[block, 4] = filtered[1] * filtered[2]
        heads[block, 5] = cotangent * filtered[0]


def to_spectra(heads, pairs, forward, spec_x, spec_g, halo):
    blocks, rows, width = pairs.shape
    merged = blocks // spec_x.shape[0]
    for block in range(blocks):
        fresh = jnp.concatenate([heads[block, 4], heads[block, 5]], axis=1)
        head = head_rows(fresh, pairs[block, pl.ds(0, 16), :].astype(jnp.float32), halo)
        pairs[block, pl.ds(0, 16), :] = head.astype(jnp.bfloat16)
    for index in range(spec_x.shape[0]):
        signals = pairs[pl.ds(index * merged, merged)].reshape(merged * rows, width)
        spectrum = jnp.dot(forward, signals, preferred_element_type=jnp.float32)
        spec_x[index] = spectrum[:, :LANES]
        spec_g[index] = spectrum[:, LANES:]


def filter_kernel(h_ref, forward_hi, forward_lo, out_ref):
    blocks, two_rows, _ = out_ref.shape
    rows = two_rows // 2
    sign = jnp.where(lax.broadcasted_iota(jnp.int32, (rows, LANES), 0) % 2 == 0, 1.0, -1.0)

    def product(table, values):
        return lax.dot_general(
            table, values, (((1,), (1,)), ((), ())), preferred_element_type=jnp.float32
        )

    before = None
    for block in range(blocks):
        signal = h_ref[:, pl.ds(block * rows, rows)]
        high = signal.astype(jnp.bfloat16)
        low = (signal - high.astype(jnp.float32)).astype(jnp.bfloat16)
        spectrum = (
            product(forward_hi[...], high)
            + product(forward_lo[...], high)
            + product(forward_hi[...], low)
        )
        real, imag = spectrum[:rows], spectrum[rows:]
        if before is None:
            out_ref[block] = spectrum
        else:
            out_ref[block, pl.ds(0, rows), :] = real - sign * before[1]
            out_ref[block, pl.ds(rows, rows), :] = imag + sign * before[0]
        before = (real, imag)


def load_tile(ref, count, tile, bins):
    real = [ref[index, pl.ds(pl.multiple_of(tile * 8, 8), 8), :] for index in range(count)]
    imag = [ref[index, pl.ds(pl.multiple_of(bins + tile * 8, 8), 8), :] for index in range(count)]
    return (real, imag)


def mixed_products(left, right, sums, conjugate):
    (left_re, left_im), (right_re, right_im) = left, right
    results = []
    for pairs in sums:
        total_re, total_im = None, None
        for one, two in pairs:
            a, b, c, d = left_re[one], left_im[one], right_re[two], right_im[two]
            if conjugate:
                real, imag = a * c + b * d, a * d - b * c
            else:
                real, imag = a * c - b * d, a * d + b * c
            total_re = real if total_re is None else total_re + real
            total_im = imag if total_im is None else total_im + imag
        results.append((total_re, total_im))
    return results


def store_tiles(ref, first_lane, tiles, pair, bins):
    lanes = pl.ds(first_lane, LANES)
    for index, parts in enumerate(zip(*tiles)):
        for first, values in zip((0, bins), zip(*parts)):
            rows = pl.ds(pl.multiple_of(first + pair * 16, 16), 16)
            ref[index, rows, lanes] = jnp.concatenate(values, axis=0).astype(ref.dtype)


def convolve_kernel(order, taps_ref, spec_h, forward, inverse, *refs):
    count = len(order)
    first_ref, *others, shared_ref, own_ref = refs[: count - 1]
    size = own_ref.shape[0]
    in_refs = [first_ref.at[pl.ds(0, size)], shared_ref.at[pl.ds(size, size)], *others]
    in_refs += [shared_ref.at[pl.ds(0, size)], own_ref]
    out_refs, refs = refs[count - 1 : 2 * count - 1], refs[2 * count - 1 :]
    spec_x, spec_g, edges, firsts, joined, heads, pairs, spec_y, extra = refs
    me = lax.axis_index("context")
    rows = pairs.shape[1]
    halo = taps_ref.shape[1] - 1
    bins = inverse.shape[0]
    wide = spec_h.shape[0]
    gather(order, in_refs, edges, firsts, pairs, rows)
    repair_heads(taps_ref, edges, firsts, joined, heads)
    to_spectra(heads, pairs, forward[...], spec_x, spec_g, halo)

    def body(pair, carry):
        longs, backs = [], []
        for tile in (2 * pair, 2 * pair + 1):
            filt = load_tile(spec_h, wide, tile, bins)
            sums = [[(i - j, j) for j in range(i + 1)] for i in range(wide)]
            longs.append(mixed_products(filt, load_tile(spec_x, wide, tile, bins), sums, False))
            sums = [[(j - i, j) for j in range(i, wide)] for i in range(wide)]
            backs.append(mixed_products(filt, load_tile(spec_g, wide, tile, bins), sums, True))
        store_tiles(spec_y, 0, longs, pair, bins)
        store_tiles(spec_y, LANES, backs, pair, bins)
        return carry

    lax.fori_loop(0, bins // 16, body, 0, unroll=2)
    extra[...] = jnp.zeros(extra.shape, jnp.float32)
    for index in range(wide):
        both = jnp.dot(inverse[...], spec_y[index], preferred_element_type=jnp.float32).astype(jnp.bfloat16)
        for part in range(count // wide):
            block = index * (count // wide) + part
            here = both[part * rows : (part + 1) * rows]
            query_f, key_f, value_f, cotangent = [heads[block, which] for which in range(4)]
            head = here[:16].astype(jnp.float32)
            long_head, back_head = head[:8, :LANES], head[:8, LANES:]
            grad_key, grad_value = back_head * value_f, back_head * key_f
            back = head_rows(grad_key, head[:, LANES:], halo).astype(jnp.bfloat16)
            pairs[block, :, pl.ds(0, LANES)] = here[:, :LANES]
            pairs[block, :, pl.ds(LANES, LANES)] = jnp.concatenate([back, here[16:, LANES:]], axis=0)
            own = (query_f * long_head, grad_value)
            following = (cotangent * long_head, grad_key, grad_value)
            for place, value in enumerate(own):
                extra[block + 1, pl.ds(place * halo, halo), :] = value[:halo]
            for place, value in enumerate(following):
                extra[block, pl.ds((2 + place) * halo, halo), :] = value[:halo]
    for mask, out_ref in zip(order, out_refs):
        block = me ^ mask
        for which in range(2):
            out_ref[pl.ds(which * rows, rows), :] = pairs[block, :, pl.ds(which * LANES, LANES)]
        out_ref[pl.ds(2 * rows, extra.shape[1]), :] = extra[block + 1].astype(jnp.bfloat16)


def correlate_kernel(scale, spec_x, spec_g, inverse, parcel_ref, out_ref, parcel_out, spec_y):
    parcel_out[...] = parcel_ref[...]
    wide = spec_x.shape[0]
    bins = inverse.shape[0]

    def body(pair, carry):
        row = lax.broadcasted_iota(jnp.int32, (8, LANES), 0)
        sign = jnp.where(row % 2 == 0, 1.0, -1.0)
        tiles = []
        for tile in (2 * pair, 2 * pair + 1):
            real, imag = load_tile(spec_x, wide, tile, bins)
            window_re = [real[0]] + [real[i] - sign * imag[i - 1] for i in range(1, wide)]
            window_im = [imag[0]] + [imag[i] + sign * real[i - 1] for i in range(1, wide)]
            sums = [[(j - lag, j) for j in range(lag, wide)] for lag in range(wide)]
            grad = load_tile(spec_g, wide, tile, bins)
            tiles.append(mixed_products((window_re, window_im), grad, sums, True))
        store_tiles(spec_y, 0, tiles, pair, bins)
        return carry

    lax.fori_loop(0, bins // 16, body, 0, unroll=2)
    for index in range(wide):
        result = jnp.dot(inverse[...], spec_y[index], preferred_element_type=jnp.float32)
        out_ref[:, pl.ds(index * bins, bins)] = result.T * scale


def finish_channels(
    order, places, in_refs, g_ref, taps_ref, held, padded, extra, results, leave
):
    me = lax.axis_index("context")
    rows = g_ref.shape[0]
    span = taps_ref.shape[1]
    halo = span - 1
    held = [ref.at[index] for ref in held for index in range(ref.shape[0])]
    for index, (place, in_ref) in enumerate(zip(places, in_refs)):
        lanes = pl.ds(pl.multiple_of((me ^ order[place]) * LANES, LANES), LANES)
        slot = index % padded.shape[0]
        edge_rows = in_ref.shape[0] - 2 * rows
        query_f, key_f, value_f = [held[place][which] for which in range(3)]
        cotangent = g_ref[:, lanes].astype(jnp.float32)
        long_conv = in_ref[pl.ds(0, rows), :].astype(jnp.float32)
        back = in_ref[pl.ds(rows, rows), :].astype(jnp.float32)
        extra[slot, pl.ds(0, edge_rows), :] = in_ref[pl.ds(2 * rows, edge_rows), :].astype(jnp.float32)
        mixed = head_rows(extra[slot, pl.ds(0, 8), :], query_f * long_conv, halo)
        results[index, 3] = mixed.astype(jnp.bfloat16)
        leave(index, 3)
        grads = (
            cotangent * long_conv,
            head_rows(back[:8], back * value_f, halo),
            head_rows(extra[slot, pl.ds(halo, 8), :], back * key_f, halo),
        )
        for which, grad in enumerate(grads):
            padded[slot, which, pl.ds(0, rows), :] = grad.astype(jnp.bfloat16).astype(jnp.float32)
            padded[slot, which, pl.ds(rows, halo), :] = extra[slot, pl.ds((2 + which) * halo, halo), :]
            weights = tap_rows(taps_ref, which, lanes)
            running = weights[0] * padded[slot, which, pl.ds(0, rows), :]
            for offset in range(1, span):
                running = running + weights[offset] * padded[slot, which, pl.ds(offset, rows), :]
            results[index, which] = running.astype(jnp.bfloat16)
            leave(index, which)


def receive_kernel(order, places, g_ref, taps_ref, far_ref, near_ref, filter_ref, *refs):
    in_refs = refs[: len(places)]
    mixed_ref, grads_ref, filter_out, padded, extra, results, sems, filter_sem = refs[-8:]
    me = lax.axis_index("context")
    copies = []
    if filter_ref is not None:
        copies.append(pltpu.make_async_copy(filter_ref, filter_out.at[0], filter_sem))
        copies[-1].start()

    def leave(index, which):
        lanes = pl.ds(pl.multiple_of((me ^ order[places[index]]) * LANES, LANES), LANES)
        target = mixed_ref.at[:, lanes] if which == 3 else grads_ref.at[which, :, lanes]
        copies.append(pltpu.make_async_copy(results.at[index, which], target, sems.at[index, which]))
        copies[-1].start()

    held = (far_ref, near_ref)
    finish_channels(
        order, places, in_refs, g_ref, taps_ref, held, padded, extra, results, leave
    )
    for copy in copies:
        copy.wait()


def last_kernel(order, places, g_ref, taps_ref, far_ref, near_ref, *refs):
    in_refs, refs = refs[: len(places)], refs[len(places) + 2 :]
    mixed_ref, grads_ref, padded, extra, results, sems = refs
    receive_kernel(
        order, places, g_ref, taps_ref, far_ref, near_ref, None, *in_refs,
        mixed_ref, grads_ref, None, padded, extra, results, sems, None,
    )


def on_device(kernel, out_shape, scratch, args, in_hbm=(), unread=None, updates=(), cover=False):
    whole = pl.BlockSpec(memory_space=pltpu.VMEM)
    hbm = pl.BlockSpec(memory_space=pltpu.HBM)
    anywhere = pl.BlockSpec(memory_space=pl.ANY)
    fixed = [pltpu.with_memory_space_constraint(arg, pltpu.HBM) for arg in in_hbm]
    before = [] if unread is None else [unread]
    first_update = len(before) + len(fixed) + len(args)
    return pl.pallas_call(
        kernel if unread is None else lambda _, *refs: kernel(*refs),
        out_shape=out_shape,
        in_specs=[anywhere] * len(before) + [hbm] * len(fixed) + [whole] * len(args) + [hbm] * len(updates),
        out_specs=jax.tree.map(
            lambda out: whole if isinstance(out, jax.ShapeDtypeStruct) else hbm, out_shape
        ),
        input_output_aliases={first_update + place: place for place in range(len(updates))},
        scratch_shapes=[
            pltpu.VMEM(shape, jnp.float32) if isinstance(shape, tuple) else shape for shape in scratch
        ],
        compiler_params=pltpu.CompilerParams(vmem_limit_bytes=VMEM_BYTES),
        cost_estimate=COVER if cover else None,
    )(*before, *fixed, *args, *updates)


def exchange_order(count):
    return sorted(
        range(count),
        key=lambda mask: (mask == 0, -(mask >> 1).bit_count(), mask % 2, mask if mask % 2 else -mask),
    )


def exchange(parcel, mask):
    count = lax.axis_size("context")
    return lax.ppermute(parcel, "context", [(i, i ^ mask) for i in range(count)])


def block_shards(query_proj, key_proj, value_proj, short_taps, long_filter, grad_mixed):
    rows, channels = query_proj.shape
    blocks = lax.axis_size("context")
    halo = short_taps.shape[1] - 1
    seq_len = rows * blocks
    merged = 2
    wide = merged * rows
    forward_hi, forward_lo, inverse = [jnp.asarray(table) for table in block_tables(wide)]
    edge_rows = round_up(5 * halo, 16)
    order = exchange_order(blocks)
    parcels = [jax.ShapeDtypeStruct((2 * rows + edge_rows, LANES), jnp.bfloat16)] * blocks
    spectra = (blocks // merged, 2 * wide, LANES)
    own_taps = (*short_taps.shape[:2], LANES)
    far = [place for place in range(blocks) if order[place] > 1]
    near = [place for place in range(blocks) if order[place] <= 1]

    parcel = parcels[0]
    double = jax.ShapeDtypeStruct((2 * parcel.shape[0], LANES), jnp.bfloat16)
    made = [(2, 3, rows + 8, LANES), (2, edge_rows, LANES)]
    inputs = (4, rows, LANES)
    sources = (long_filter[0], forward_hi, forward_lo)

    def floats(*shape):
        return jax.ShapeDtypeStruct(shape, jnp.float32)

    first, *sent, far_filtered, filter_here, hi_here, lo_here, landed, taps = on_device(
        functools.partial(send_kernel, order, far, near, len(sources)),
        [double, *parcels[: len(far) - 2], floats(len(far), 3, rows, LANES)]
        + [jax.ShapeDtypeStruct(value.shape, value.dtype) for value in sources]
        + [
            jax.ShapeDtypeStruct((len(near), *inputs), jnp.bfloat16),
            floats(len(near), *own_taps),
        ],
        [
            pltpu.VMEM((len(far), *inputs), jnp.bfloat16),
            (len(far), *own_taps),
            *made,
            pltpu.SemaphoreType.DMA((len(far), 5)),
            pltpu.SemaphoreType.DMA((len(near), 5)),
            pltpu.SemaphoreType.DMA((len(sources),)),
        ],
        (),
        in_hbm=(query_proj, key_proj, value_proj, grad_mixed, short_taps, *sources),
    )
    first = exchange(first, order[0])
    others = [exchange(value, order[place]) for place, value in zip(far[2:], sent)]
    shared, kept_here, near_filtered, own = on_device(
        near_kernel,
        [double, parcel, floats(len(near), 3, rows, LANES), floats(*own_taps)],
        made,
        (landed, taps, first),
        cover=True,
    )
    arrived = (first, *others, exchange(shared, 1), kept_here)
    spec_h = on_device(
        filter_kernel,
        jax.ShapeDtypeStruct(spectra, jnp.float32),
        [],
        (filter_here, hi_here, lo_here),
        cover=True,
    )
    *results, spec_x, spec_g = on_device(
        functools.partial(convolve_kernel, order),
        parcels + [jax.ShapeDtypeStruct(spectra, jnp.float32)] * 2,
        [
            (blocks, edge_rows, LANES),
            (blocks, 2, 8, LANES),
            (3, blocks, 24, LANES),
            (blocks, 6, 8, LANES),
            pltpu.VMEM((blocks, rows, 2 * LANES), jnp.bfloat16),
            pltpu.VMEM((*spectra[:2], 2 * LANES), jnp.bfloat16),
            (blocks + 1, edge_rows, LANES),
        ],
        (own, spec_h, hi_here, inverse, *arrived),
    )
    returned = [exchange(results[place], order[place]) for place in far]
    filter_grad, parcel = on_device(
        functools.partial(correlate_kernel, 1.0 / math.sqrt(seq_len)),
        [jax.ShapeDtypeStruct(long_filter.shape[1:], jnp.float32), parcels[0]],
        [pltpu.VMEM(spectra, jnp.bfloat16)],
        (spec_x, spec_g, inverse, results[near[0]]),
        unread=returned[0],
    )
    returned += [exchange(parcel, order[near[0]]), results[near[1]]]
    late = far[len(far) // 2 - 1 :] + near[:-1]
    early = [place for place in range(blocks) if place not in late]
    outputs = (
        pltpu.HBM((rows, channels), jnp.bfloat16),
        pltpu.HBM((3, rows, channels), jnp.bfloat16),
        pltpu.HBM(long_filter.shape, jnp.float32),
    )

    def working(places):
        return [
            (2, 3, rows + 16, LANES),
            (2, edge_rows + 8, LANES),
            pltpu.VMEM((len(places), 4, rows, LANES), jnp.bfloat16),
            pltpu.SemaphoreType.DMA((len(places), 4)),
        ]

    common = (grad_mixed, short_taps, far_filtered, near_filtered)
    *begun, filter_grad = on_device(
        functools.partial(receive_kernel, order, early),
        outputs,
        [*working(early), pltpu.SemaphoreType.DMA(())],
        (*common, filter_grad, *(returned[place] for place in early)),
    )
    mixed_out, input_grads = on_device(
        functools.partial(last_kernel, order, late),
        outputs[:2],
        working(late),
        (*common, *(returned[place] for place in late)),
        updates=begun,
    )
    return (mixed_out, input_grads, filter_grad)


def shards(query_proj, key_proj, value_proj, short_taps, long_filter, grad_mixed):
    rows, channels = query_proj.shape
    halo = short_taps.shape[1] - 1
    blocks = lax.axis_size("context")
    power_of_two = blocks & (blocks - 1) == 0
    fits = power_of_two and blocks > 1 and channels == blocks * LANES and rows % 128 == 0 and halo <= 8
    chosen = block_shards if fits else general_shards
    return chosen(query_proj, key_proj, value_proj, short_taps, long_filter, grad_mixed)


def solution(mesh):
    return jax.shard_map(
        shards,
        mesh=mesh,
        in_specs=(
            P("context", "tensor"),
            P("context", "tensor"),
            P("context", "tensor"),
            P(None, None, "tensor"),
            P("tensor", "context", None),
            P("context", "tensor"),
        ),
        out_specs=(
            P("context", "tensor"),
            P(None, "context", "tensor"),
            P("tensor", "context", None),
        ),
        check_vma=False,
    )
```

```python
import functools
import math

import jax
import jax.numpy as jnp
import numpy as np
from jax import lax
from jax.experimental import pallas as pl
from jax.experimental.pallas import tpu as pltpu
from jax.sharding import PartitionSpec as P

precise = lax.Precision.HIGHEST


def from_behind(value, axis, steps):
    count = lax.axis_size(axis)
    first, last = (max(0, -steps), min(count, count - steps))
    return lax.ppermute(value, axis, [(source, source + steps) for source in range(first, last)])


def build_tables(blocks, tok_rows):
    outer_len = 2 * blocks
    full_len = outer_len * tok_rows
    k_one = jnp.arange(outer_len, dtype=jnp.int32)
    n_one = jnp.arange(blocks, dtype=jnp.int32)
    position = jnp.arange(tok_rows, dtype=jnp.int32)
    first_idx = k_one[:, None] * n_one[None, :] % outer_len
    first_angle = -2.0 * math.pi / outer_len * first_idx.astype(jnp.float32)
    second = position[:, None] * position[None, :] % tok_rows
    second_angle = -2.0 * math.pi / tok_rows * second.astype(jnp.float32)
    twist_idx = k_one[:, None] * position[None, :] % full_len
    twist_angle = -2.0 * math.pi / full_len * twist_idx.astype(jnp.float32)
    return (
        jnp.cos(first_angle),
        jnp.sin(first_angle),
        jnp.cos(second_angle),
        jnp.sin(second_angle),
        jnp.cos(twist_angle),
        jnp.sin(twist_angle),
    )


def transform(signal, tables):
    cos_first, sin_first, cos_second, sin_second, cos_twist, sin_twist = tables
    first_re = jnp.einsum("kn,gnm->gkm", cos_first, signal, precision=precise)
    first_im = jnp.einsum("kn,gnm->gkm", sin_first, signal, precision=precise)
    mid_re = first_re * cos_twist - first_im * sin_twist
    mid_im = first_re * sin_twist + first_im * cos_twist
    out_re = jnp.einsum("gkn,nm->gkm", mid_re, cos_second, precision=precise) - jnp.einsum(
        "gkn,nm->gkm", mid_im, sin_second, precision=precise
    )
    out_im = jnp.einsum("gkn,nm->gkm", mid_re, sin_second, precision=precise) + jnp.einsum(
        "gkn,nm->gkm", mid_im, cos_second, precision=precise
    )
    return (out_re, out_im)


def inverse(spec_re, spec_im, tables):
    cos_first, sin_first, cos_second, sin_second, cos_twist, sin_twist = tables
    full_len = cos_first.shape[0] * cos_second.shape[0]
    mid_re = jnp.einsum("gkn,nm->gkm", spec_re, cos_second, precision=precise) + jnp.einsum(
        "gkn,nm->gkm", spec_im, sin_second, precision=precise
    )
    mid_im = jnp.einsum("gkn,nm->gkm", spec_im, cos_second, precision=precise) - jnp.einsum(
        "gkn,nm->gkm", spec_re, sin_second, precision=precise
    )
    turn_re = mid_re * cos_twist + mid_im * sin_twist
    turn_im = mid_im * cos_twist - mid_re * sin_twist
    result = jnp.einsum("kn,gkm->gnm", cos_first, turn_re, precision=precise) + jnp.einsum(
        "kn,gkm->gnm", sin_first, turn_im, precision=precise
    )
    return result * (1.0 / full_len)


def causal_taps(series, preceding, tap_weights):
    tok_rows = series.shape[0]
    span = tap_weights.shape[0]
    joined = jnp.concatenate([preceding, series], axis=0).astype(jnp.float32)
    running = jnp.zeros(series.shape, jnp.float32)
    for offset in range(span):
        first_row = span - 1 - offset
        running = running + tap_weights[offset][None, :] * joined[first_row : first_row + tok_rows]
    return running


def reverse_taps(series, following, tap_weights):
    tok_rows = series.shape[0]
    span = tap_weights.shape[0]
    joined = jnp.concatenate([series, following], axis=0).astype(jnp.float32)
    running = jnp.zeros(series.shape, jnp.float32)
    for offset in range(span):
        running = running + tap_weights[offset][None, :] * joined[offset : offset + tok_rows]
    return running


def general_shards(query_proj, key_proj, value_proj, short_taps, long_filter, grad_mixed):
    tok_rows, channels = query_proj.shape
    blocks = lax.axis_size("context")
    halo_rows = short_taps.shape[1] - 1
    per_device = channels // blocks
    seq_len = tok_rows * blocks
    tables = build_tables(blocks, tok_rows)
    preceding = from_behind(
        (
            query_proj[tok_rows - halo_rows :],
            key_proj[tok_rows - halo_rows :],
            value_proj[tok_rows - halo_rows :],
        ),
        "context",
        1,
    )
    query_f = causal_taps(query_proj, preceding[0], short_taps[0])
    key_f = causal_taps(key_proj, preceding[1], short_taps[1])
    value_f = causal_taps(value_proj, preceding[2], short_taps[2])
    gated_prod = (key_f * value_f).astype(jnp.bfloat16)
    grad_f = grad_mixed.astype(jnp.float32)
    grad_long = (grad_f * query_f).astype(jnp.bfloat16)

    def to_spectrum(series):
        arranged = series.T.reshape(blocks, per_device, tok_rows)
        received = lax.all_to_all(arranged, "context", split_axis=0, concat_axis=2, tiled=True)
        item_count = received.shape[1]
        signal = received.reshape(item_count, blocks, tok_rows).astype(jnp.float32)
        return transform(signal, tables)

    def to_token_rows(spatial):
        arrived = lax.all_to_all(spatial, "context", split_axis=1, concat_axis=0, tiled=True)
        return arrived.reshape(channels, tok_rows).T

    gate_re, gate_im = to_spectrum(gated_prod)
    filter_re, filter_im = transform(long_filter.reshape(per_device, blocks, tok_rows), tables)
    long_spatial = inverse(
        gate_re * filter_re - gate_im * filter_im, gate_re * filter_im + gate_im * filter_re, tables
    ).astype(jnp.bfloat16)
    long_conv = to_token_rows(long_spatial)
    long_f = long_conv.astype(jnp.float32)
    mixed_out = (query_f * long_f).astype(jnp.bfloat16)
    grad_query_f = (grad_f * long_f).astype(jnp.bfloat16)
    grad_after = lax.optimization_barrier((grad_long, long_conv))[0]
    grad_re, grad_im = to_spectrum(grad_after)
    back_spatial = inverse(
        filter_re * grad_re + filter_im * grad_im, filter_re * grad_im - filter_im * grad_re, tables
    ).astype(jnp.bfloat16)
    corr_spatial = inverse(
        gate_re * grad_re + gate_im * grad_im, gate_re * grad_im - gate_im * grad_re, tables
    )
    grad_gated = to_token_rows(back_spatial).astype(jnp.float32)
    grad_key_f = (grad_gated * value_f).astype(jnp.bfloat16)
    grad_value_f = (grad_gated * key_f).astype(jnp.bfloat16)
    following = from_behind(
        (grad_query_f[:halo_rows], grad_key_f[:halo_rows], grad_value_f[:halo_rows]), "context", -1
    )
    input_grads = jnp.stack(
        [
            reverse_taps(grad_query_f, following[0], short_taps[0]),
            reverse_taps(grad_key_f, following[1], short_taps[1]),
            reverse_taps(grad_value_f, following[2], short_taps[2]),
        ]
    ).astype(jnp.bfloat16)
    filter_grad = (corr_spatial * (1.0 / math.sqrt(seq_len))).reshape(1, per_device, seq_len)
    return (mixed_out, input_grads, filter_grad)


LANES = 128
VMEM_BYTES = 48 * 1024 * 1024
COVER = pl.CostEstimate(flops=10**10, bytes_accessed=10**8, transcendentals=0)


def split_bf16(table):
    high = table.astype(jnp.bfloat16)
    low = (table - high.astype(np.float64)).astype(jnp.bfloat16)
    return (high, low)


@functools.cache
def block_tables(rows):
    bins = np.pi * (np.arange(rows) + 0.5)[:, None] / rows
    lag = np.arange(rows)[None, :]
    forward = np.concatenate([np.cos(bins * lag), -np.sin(bins * lag)], axis=0)
    forward_hi, forward_lo = split_bf16(forward)
    return (forward_hi, forward_lo, split_bf16(forward.T / rows)[0])


def round_up(count, unit):
    return (count + unit - 1) // unit * unit


def head_rows(fresh, whole, halo):
    row = lax.broadcasted_iota(jnp.int32, fresh.shape, 0)
    return jnp.concatenate([jnp.where(row < halo, fresh, whole[:8]), whole[8:]], axis=0)


def tap_rows(taps_ref, which, lanes):
    return [taps_ref[which, pl.ds(offset, 1), lanes] for offset in range(taps_ref.shape[1])]


def short_filter(padded, rows, weights):
    running = weights[0] * padded[pl.ds(8, rows), :]
    for offset in range(1, len(weights)):
        running = running + weights[offset] * padded[pl.ds(8 - offset, rows), :]
    return running


def make_parcel(slot, source, taps, padded, extra, filtered_ref, out_ref):
    rows = source.shape[1]
    halo = taps.shape[1] - 1
    padded[slot, :, pl.ds(0, 8), :] = jnp.zeros((3, 8, LANES), jnp.float32)
    extra[slot, pl.ds(5 * halo, extra.shape[1] - 5 * halo), :] = jnp.zeros(
        (extra.shape[1] - 5 * halo, LANES), jnp.float32
    )
    filtered = []
    for which in range(3):
        padded[slot, which, pl.ds(8, rows), :] = source[which].astype(jnp.float32)
        weights = tap_rows(taps, which, pl.ds(0, LANES))
        result = short_filter(padded.at[slot, which], rows, weights)
        filtered_ref[which] = result
        filtered.append(result)
    query_f, key_f, value_f = filtered
    cotangent = source[3].astype(jnp.float32)
    filtered_ref[3] = cotangent
    gated = head_rows(padded[slot, 1, pl.ds(8, 8), :], key_f * value_f, halo)
    grad_long = head_rows(cotangent[:8], cotangent * query_f, halo)
    out_ref[pl.ds(0, rows), :] = gated.astype(jnp.bfloat16)
    out_ref[pl.ds(rows, rows), :] = grad_long.astype(jnp.bfloat16)
    pieces = ((1, rows - halo), (2, 0), (2, rows - halo), (0, 0), (0, rows - halo))
    for position, (which, first) in enumerate(pieces):
        extra[slot, pl.ds(position * halo, halo), :] = padded[slot, which, pl.ds(8 + first, halo), :]
    out_ref[pl.ds(2 * rows, extra.shape[1]), :] = extra[slot].astype(jnp.bfloat16)


def fetches(order, places, inputs, taps_ref, landed, taps, arrivals):
    me = lax.axis_index("context")
    result = []
    for index, place in enumerate(places):
        lanes = pl.ds(pl.multiple_of((me ^ order[place]) * LANES, LANES), LANES)
        sources = [taps_ref.at[:, :, lanes]] + [ref.at[:, lanes] for ref in inputs]
        targets = [taps.at[index]] + [landed.at[index, which] for which in range(len(inputs))]
        result.append(
            [
                pltpu.make_async_copy(source, target, arrivals.at[index, number])
                for number, (source, target) in enumerate(zip(sources, targets))
            ]
        )
    return result


def send_kernel(order, places, ahead, extras, q_ref, k_ref, v_ref, g_ref, taps_ref, *refs):
    inputs = (q_ref, k_ref, v_ref, g_ref)
    sources, refs = refs[:extras], refs[extras:]
    first_ref, *outs = refs[: len(places) - 1]
    size = first_ref.shape[0] // 2
    outs = [first_ref.at[pl.ds(0, size)], first_ref.at[pl.ds(size, size)], *outs]
    filtered_ref, *brought = refs[len(places) - 1 : -7]
    landed, taps, padded, extra, arrivals, later, kept = refs[-7:]
    own = fetches(order, places, inputs, taps_ref, landed, taps, arrivals)
    others = [
        pltpu.make_async_copy(source, target, kept.at[index])
        for index, (source, target) in enumerate(zip(sources, brought))
    ]
    for copies in fetches(order, ahead, inputs, taps_ref, *brought[-2:], later):
        others += copies
    for copies in own:
        for copy in copies:
            copy.start()
    for copy in others:
        copy.start()
    for index, copies in enumerate(own):
        for copy in copies:
            copy.wait()
        make_parcel(
            index % 2, landed.at[index], taps.at[index], padded, extra, filtered_ref.at[index], outs[index]
        )
    for copy in others:
        copy.wait()


def near_kernel(landed, taps, first_ref, shared_ref, own_ref, filtered_ref, own_taps, padded, extra):
    rows = own_ref.shape[0]
    shared_ref[pl.ds(rows, rows), :] = first_ref[pl.ds(rows, rows), :]
    for index, out_ref in enumerate((shared_ref.at[pl.ds(0, rows)], own_ref)):
        make_parcel(
            index, landed.at[index], taps.at[index], padded, extra, filtered_ref.at[index], out_ref
        )
    own_taps[...] = taps[1]


def gather(order, in_refs, edges, firsts, pairs, rows):
    me = lax.axis_index("context")
    for mask, in_ref in zip(order, in_refs):
        block = me ^ mask
        edges[block] = in_ref[pl.ds(2 * rows, edges.shape[1]), :].astype(jnp.float32)
        for which in range(2):
            values = in_ref[pl.ds(which * rows, rows), :]
            firsts[block, which] = values[:16].astype(jnp.float32)[:8]
            pairs[block, :, pl.ds(which * LANES, LANES)] = values


def repair_heads(taps_ref, edges, firsts, joined, heads):
    blocks = edges.shape[0]
    span = taps_ref.shape[1]
    halo = span - 1
    joined[...] = jnp.zeros(joined.shape, jnp.float32)
    for block in range(blocks):
        joined[1, block, pl.ds(halo, 8), :] = firsts[block, 0]
        joined[2, block, pl.ds(halo, halo), :] = edges[block, pl.ds(halo, halo), :]
        joined[0, block, pl.ds(halo, halo), :] = edges[block, pl.ds(3 * halo, halo), :]
        if block > 0:
            for which, place in ((1, 0), (2, 2), (0, 4)):
                joined[which, block, pl.ds(0, halo), :] = edges[block - 1, pl.ds(place * halo, halo), :]
        filtered = []
        for which in range(3):
            running = jnp.zeros((8, LANES), jnp.float32)
            for offset in range(span):
                weight = taps_ref[which, pl.ds(offset, 1), :]
                running = running + weight * joined[which, block, pl.ds(halo - offset, 8), :]
            filtered.append(running)
            heads[block, which] = running
        cotangent = firsts[block, 1]
        heads[block, 3] = cotangent
        heads[block, 4] = filtered[1] * filtered[2]
        heads[block, 5] = cotangent * filtered[0]


def to_spectra(heads, pairs, forward, spec_x, spec_g, halo):
    blocks, rows, width = pairs.shape
    merged = blocks // spec_x.shape[0]
    for block in range(blocks):
        fresh = jnp.concatenate([heads[block, 4], heads[block, 5]], axis=1)
        head = head_rows(fresh, pairs[block, pl.ds(0, 16), :].astype(jnp.float32), halo)
        pairs[block, pl.ds(0, 16), :] = head.astype(jnp.bfloat16)
    for index in range(spec_x.shape[0]):
        signals = pairs[pl.ds(index * merged, merged)].reshape(merged * rows, width)
        spectrum = jnp.dot(forward, signals, preferred_element_type=jnp.float32)
        spec_x[index] = spectrum[:, :LANES]
        spec_g[index] = spectrum[:, LANES:]


def filter_kernel(h_ref, forward_hi, forward_lo, out_ref):
    blocks, two_rows, _ = out_ref.shape
    rows = two_rows // 2
    sign = jnp.where(lax.broadcasted_iota(jnp.int32, (rows, LANES), 0) % 2 == 0, 1.0, -1.0)

    def product(table, values):
        return lax.dot_general(
            table, values, (((1,), (1,)), ((), ())), preferred_element_type=jnp.float32
        )

    before = None
    for block in range(blocks):
        signal = h_ref[:, pl.ds(block * rows, rows)]
        high = signal.astype(jnp.bfloat16)
        low = (signal - high.astype(jnp.float32)).astype(jnp.bfloat16)
        spectrum = (
            product(forward_hi[...], high)
            + product(forward_lo[...], high)
            + product(forward_hi[...], low)
        )
        real, imag = spectrum[:rows], spectrum[rows:]
        if before is None:
            out_ref[block] = spectrum
        else:
            out_ref[block, pl.ds(0, rows), :] = real - sign * before[1]
            out_ref[block, pl.ds(rows, rows), :] = imag + sign * before[0]
        before = (real, imag)


def load_tile(ref, count, tile, bins):
    real = [ref[index, pl.ds(pl.multiple_of(tile * 8, 8), 8), :] for index in range(count)]
    imag = [ref[index, pl.ds(pl.multiple_of(bins + tile * 8, 8), 8), :] for index in range(count)]
    return (real, imag)


def mixed_products(left, right, sums, conjugate):
    (left_re, left_im), (right_re, right_im) = left, right
    results = []
    for pairs in sums:
        total_re, total_im = None, None
        for one, two in pairs:
            a, b, c, d = left_re[one], left_im[one], right_re[two], right_im[two]
            if conjugate:
                real, imag = a * c + b * d, a * d - b * c
            else:
                real, imag = a * c - b * d, a * d + b * c
            total_re = real if total_re is None else total_re + real
            total_im = imag if total_im is None else total_im + imag
        results.append((total_re, total_im))
    return results


def store_tiles(ref, first_lane, tiles, pair, bins):
    lanes = pl.ds(first_lane, LANES)
    for index, parts in enumerate(zip(*tiles)):
        for first, values in zip((0, bins), zip(*parts)):
            rows = pl.ds(pl.multiple_of(first + pair * 16, 16), 16)
            ref[index, rows, lanes] = jnp.concatenate(values, axis=0).astype(ref.dtype)


def convolve_kernel(order, taps_ref, spec_h, forward, inverse, *refs):
    count = len(order)
    first_ref, *others, shared_ref, own_ref = refs[: count - 1]
    size = own_ref.shape[0]
    in_refs = [first_ref.at[pl.ds(0, size)], shared_ref.at[pl.ds(size, size)], *others]
    in_refs += [shared_ref.at[pl.ds(0, size)], own_ref]
    first_out, *out_refs = refs[count - 1 : 2 * count - 2]
    out_refs = [first_out.at[pl.ds(0, size)], first_out.at[pl.ds(size, size)], *out_refs]
    refs = refs[2 * count - 2 :]
    spec_x, spec_g, edges, firsts, joined, heads, pairs, spec_y, extra = refs
    me = lax.axis_index("context")
    rows = pairs.shape[1]
    halo = taps_ref.shape[1] - 1
    bins = inverse.shape[0]
    wide = spec_h.shape[0]
    gather(order, in_refs, edges, firsts, pairs, rows)
    repair_heads(taps_ref, edges, firsts, joined, heads)
    to_spectra(heads, pairs, forward[...], spec_x, spec_g, halo)

    def body(pair, carry):
        longs, backs = [], []
        for tile in (2 * pair, 2 * pair + 1):
            filt = load_tile(spec_h, wide, tile, bins)
            sums = [[(i - j, j) for j in range(i + 1)] for i in range(wide)]
            longs.append(mixed_products(filt, load_tile(spec_x, wide, tile, bins), sums, False))
            sums = [[(j - i, j) for j in range(i, wide)] for i in range(wide)]
            backs.append(mixed_products(filt, load_tile(spec_g, wide, tile, bins), sums, True))
        store_tiles(spec_y, 0, longs, pair, bins)
        store_tiles(spec_y, LANES, backs, pair, bins)
        return carry

    lax.fori_loop(0, bins // 16, body, 0, unroll=8)
    extra[...] = jnp.zeros(extra.shape, jnp.float32)
    for index in range(wide):
        both = jnp.dot(inverse[...], spec_y[index], preferred_element_type=jnp.float32).astype(jnp.bfloat16)
        for part in range(count // wide):
            block = index * (count // wide) + part
            here = both[part * rows : (part + 1) * rows]
            query_f, key_f, value_f, cotangent = [heads[block, which] for which in range(4)]
            head = here[:16].astype(jnp.float32)
            long_head, back_head = head[:8, :LANES], head[:8, LANES:]
            grad_key, grad_value = back_head * value_f, back_head * key_f
            back = head_rows(grad_key, head[:, LANES:], halo).astype(jnp.bfloat16)
            pairs[block, :, pl.ds(0, LANES)] = here[:, :LANES]
            pairs[block, :, pl.ds(LANES, LANES)] = jnp.concatenate([back, here[16:, LANES:]], axis=0)
            own = (query_f * long_head, grad_value)
            following = (cotangent * long_head, grad_key, grad_value)
            for place, value in enumerate(own):
                extra[block + 1, pl.ds(place * halo, halo), :] = value[:halo]
            for place, value in enumerate(following):
                extra[block, pl.ds((2 + place) * halo, halo), :] = value[:halo]
    for mask, out_ref in zip(order, out_refs):
        block = me ^ mask
        for which in range(2):
            out_ref[pl.ds(which * rows, rows), :] = pairs[block, :, pl.ds(which * LANES, LANES)]
        out_ref[pl.ds(2 * rows, extra.shape[1]), :] = extra[block + 1].astype(jnp.bfloat16)


def share_kernel(filter_ref, parcel_ref, first_ref, shared_ref):
    rows = parcel_ref.shape[0]
    shared_ref[pl.ds(0, rows), :] = parcel_ref[...]
    shared_ref[pl.ds(rows, rows), :] = first_ref[pl.ds(rows, rows), :]


def correlate_kernel(scale, spec_x, spec_g, inverse, out_ref, spec_y):
    wide = spec_x.shape[0]
    bins = inverse.shape[0]

    def body(pair, carry):
        row = lax.broadcasted_iota(jnp.int32, (8, LANES), 0)
        sign = jnp.where(row % 2 == 0, 1.0, -1.0)
        tiles = []
        for tile in (2 * pair, 2 * pair + 1):
            real, imag = load_tile(spec_x, wide, tile, bins)
            window_re = [real[0]] + [real[i] - sign * imag[i - 1] for i in range(1, wide)]
            window_im = [imag[0]] + [imag[i] + sign * real[i - 1] for i in range(1, wide)]
            sums = [[(j - lag, j) for j in range(lag, wide)] for lag in range(wide)]
            grad = load_tile(spec_g, wide, tile, bins)
            tiles.append(mixed_products((window_re, window_im), grad, sums, True))
        store_tiles(spec_y, 0, tiles, pair, bins)
        return carry

    lax.fori_loop(0, bins // 16, body, 0, unroll=8)
    for index in range(wide):
        result = jnp.dot(inverse[...], spec_y[index], preferred_element_type=jnp.float32)
        out_ref[:, pl.ds(index * bins, bins)] = result.T * scale


def finish_channels(
    order, places, in_refs, taps_ref, held, padded, extra, results, leave
):
    me = lax.axis_index("context")
    rows = held[0].shape[2]
    span = taps_ref.shape[1]
    halo = span - 1
    held = [ref.at[index] for ref in held for index in range(ref.shape[0])]
    for index, (place, in_ref) in enumerate(zip(places, in_refs)):
        lanes = pl.ds(pl.multiple_of((me ^ order[place]) * LANES, LANES), LANES)
        slot = index % padded.shape[0]
        edge_rows = in_ref.shape[0] - 2 * rows
        query_f, key_f, value_f = [held[place][which] for which in range(3)]
        cotangent = held[place][3]
        long_conv = in_ref[pl.ds(0, rows), :].astype(jnp.float32)
        back = in_ref[pl.ds(rows, rows), :].astype(jnp.float32)
        extra[slot, pl.ds(0, edge_rows), :] = in_ref[pl.ds(2 * rows, edge_rows), :].astype(jnp.float32)
        mixed = head_rows(extra[slot, pl.ds(0, 8), :], query_f * long_conv, halo)
        results[index, 3] = mixed.astype(jnp.bfloat16)
        leave(index, 3)
        grads = (
            cotangent * long_conv,
            head_rows(back[:8], back * value_f, halo),
            head_rows(extra[slot, pl.ds(halo, 8), :], back * key_f, halo),
        )
        for which, grad in enumerate(grads):
            padded[slot, which, pl.ds(0, rows), :] = grad.astype(jnp.bfloat16).astype(jnp.float32)
            padded[slot, which, pl.ds(rows, halo), :] = extra[slot, pl.ds((2 + which) * halo, halo), :]
            weights = tap_rows(taps_ref, which, lanes)
            running = weights[0] * padded[slot, which, pl.ds(0, rows), :]
            for offset in range(1, span):
                running = running + weights[offset] * padded[slot, which, pl.ds(offset, rows), :]
            results[index, which] = running.astype(jnp.bfloat16)
            leave(index, which)


def receive_kernel(order, places, taps_ref, far_ref, near_ref, filter_ref, *refs):
    size = 2 * far_ref.shape[2] + round_up(5 * (taps_ref.shape[1] - 1), 16)
    in_refs = [ref.at[pl.ds((place == 1) * size, size)] for place, ref in zip(places, refs)]
    mixed_ref, grads_ref, filter_out, padded, extra, results, sems, filter_sem = refs[-8:]
    me = lax.axis_index("context")
    copies = []
    if filter_ref is not None:
        copies.append(pltpu.make_async_copy(filter_ref, filter_out.at[0], filter_sem))
        copies[-1].start()

    def leave(index, which):
        lanes = pl.ds(pl.multiple_of((me ^ order[places[index]]) * LANES, LANES), LANES)
        target = mixed_ref.at[:, lanes] if which == 3 else grads_ref.at[which, :, lanes]
        copies.append(pltpu.make_async_copy(results.at[index, which], target, sems.at[index, which]))
        copies[-1].start()

    held = (far_ref, near_ref)
    finish_channels(
        order, places, in_refs, taps_ref, held, padded, extra, results, leave
    )
    for copy in copies:
        copy.wait()


def last_kernel(order, places, taps_ref, far_ref, near_ref, *refs):
    in_refs, refs = refs[: len(places)], refs[len(places) + 2 :]
    mixed_ref, grads_ref, padded, extra, results, sems = refs
    receive_kernel(
        order, places, taps_ref, far_ref, near_ref, None, *in_refs,
        mixed_ref, grads_ref, None, padded, extra, results, sems, None,
    )


def on_device(kernel, out_shape, scratch, args, in_hbm=(), unread=None, updates=(), cover=False):
    whole = pl.BlockSpec(memory_space=pltpu.VMEM)
    hbm = pl.BlockSpec(memory_space=pltpu.HBM)
    anywhere = pl.BlockSpec(memory_space=pl.ANY)
    fixed = [pltpu.with_memory_space_constraint(arg, pltpu.HBM) for arg in in_hbm]
    before = [] if unread is None else [unread]
    first_update = len(before) + len(fixed) + len(args)
    return pl.pallas_call(
        kernel if unread is None else lambda _, *refs: kernel(*refs),
        out_shape=out_shape,
        in_specs=[anywhere] * len(before) + [hbm] * len(fixed) + [whole] * len(args) + [hbm] * len(updates),
        out_specs=jax.tree.map(
            lambda out: whole if isinstance(out, jax.ShapeDtypeStruct) else hbm, out_shape
        ),
        input_output_aliases={first_update + place: place for place in range(len(updates))},
        scratch_shapes=[
            pltpu.VMEM(shape, jnp.float32) if isinstance(shape, tuple) else shape for shape in scratch
        ],
        compiler_params=pltpu.CompilerParams(vmem_limit_bytes=VMEM_BYTES),
        cost_estimate=COVER if cover else None,
    )(*before, *fixed, *args, *updates)


def exchange_order(count):
    return sorted(
        range(count),
        key=lambda mask: (mask == 0, -(mask >> 1).bit_count(), mask % 2, mask if mask % 2 else -mask),
    )


def exchange(parcel, mask):
    count = lax.axis_size("context")
    return lax.ppermute(parcel, "context", [(i, i ^ mask) for i in range(count)])


def block_shards(query_proj, key_proj, value_proj, short_taps, long_filter, grad_mixed):
    rows, channels = query_proj.shape
    blocks = lax.axis_size("context")
    halo = short_taps.shape[1] - 1
    seq_len = rows * blocks
    merged = 2
    wide = merged * rows
    forward_hi, forward_lo, inverse = [jnp.asarray(table) for table in block_tables(wide)]
    edge_rows = round_up(5 * halo, 16)
    order = exchange_order(blocks)
    parcels = [jax.ShapeDtypeStruct((2 * rows + edge_rows, LANES), jnp.bfloat16)] * blocks
    spectra = (blocks // merged, 2 * wide, LANES)
    own_taps = (*short_taps.shape[:2], LANES)
    far = [place for place in range(blocks) if order[place] > 1]
    near = [place for place in range(blocks) if order[place] <= 1]

    parcel = parcels[0]
    double = jax.ShapeDtypeStruct((2 * parcel.shape[0], LANES), jnp.bfloat16)
    made = [(2, 3, rows + 8, LANES), (2, edge_rows, LANES)]
    inputs = (4, rows, LANES)
    sources = (long_filter[0], forward_hi, forward_lo)

    def floats(*shape):
        return jax.ShapeDtypeStruct(shape, jnp.float32)

    first, *sent, far_filtered, filter_here, hi_here, lo_here, landed, taps = on_device(
        functools.partial(send_kernel, order, far, near, len(sources)),
        [double, *parcels[: len(far) - 2], floats(len(far), 4, rows, LANES)]
        + [jax.ShapeDtypeStruct(value.shape, value.dtype) for value in sources]
        + [
            jax.ShapeDtypeStruct((len(near), *inputs), jnp.bfloat16),
            floats(len(near), *own_taps),
        ],
        [
            pltpu.VMEM((len(far), *inputs), jnp.bfloat16),
            (len(far), *own_taps),
            *made,
            pltpu.SemaphoreType.DMA((len(far), 5)),
            pltpu.SemaphoreType.DMA((len(near), 5)),
            pltpu.SemaphoreType.DMA((len(sources),)),
        ],
        (),
        in_hbm=(query_proj, key_proj, value_proj, grad_mixed, short_taps, *sources),
    )
    first = exchange(first, order[0])
    others = [exchange(value, order[place]) for place, value in zip(far[2:], sent)]
    shared, kept_here, near_filtered, own = on_device(
        near_kernel,
        [double, parcel, floats(len(near), 4, rows, LANES), floats(*own_taps)],
        made,
        (landed, taps, first),
        cover=True,
    )
    arrived = (first, *others, exchange(shared, 1), kept_here)
    spec_h = on_device(
        filter_kernel,
        jax.ShapeDtypeStruct(spectra, jnp.float32),
        [],
        (filter_here, hi_here, lo_here),
        cover=True,
    )
    *results, spec_x, spec_g = on_device(
        functools.partial(convolve_kernel, order),
        [double, *parcels[2:], floats(*spectra), floats(*spectra)],
        [
            (blocks, edge_rows, LANES),
            (blocks, 2, 8, LANES),
            (3, blocks, 24, LANES),
            (blocks, 6, 8, LANES),
            pltpu.VMEM((blocks, rows, 2 * LANES), jnp.bfloat16),
            pltpu.VMEM((*spectra[:2], 2 * LANES), jnp.bfloat16),
            (blocks + 1, edge_rows, LANES),
        ],
        (own, spec_h, hi_here, inverse, *arrived),
    )
    first, *sent = results
    first = exchange(first, order[0])
    others = [exchange(value, order[place]) for place, value in zip(far[2:], sent)]
    (filter_grad,) = on_device(
        functools.partial(correlate_kernel, 1.0 / math.sqrt(seq_len)),
        [floats(*long_filter.shape[1:])],
        [pltpu.VMEM(spectra, jnp.bfloat16)],
        (spec_x, spec_g, inverse),
    )
    (shared,) = on_device(share_kernel, [double], [], (filter_grad, sent[-2], first))
    shared = exchange(shared, 1)
    returned = [first, shared, *others, shared, sent[-1]]
    early = [0, *far[2:3], near[-1]]
    late = [place for place in range(blocks) if place not in early]
    outputs = (
        pltpu.HBM((rows, channels), jnp.bfloat16),
        pltpu.HBM((3, rows, channels), jnp.bfloat16),
        pltpu.HBM(long_filter.shape, jnp.float32),
    )

    def working(places):
        return [
            (2, 3, rows + 16, LANES),
            (2, edge_rows + 8, LANES),
            pltpu.VMEM((len(places), 4, rows, LANES), jnp.bfloat16),
            pltpu.SemaphoreType.DMA((len(places), 4)),
        ]

    common = (short_taps, far_filtered, near_filtered)
    *begun, filter_grad = on_device(
        functools.partial(receive_kernel, order, early),
        outputs,
        [*working(early), pltpu.SemaphoreType.DMA(())],
        (*common, filter_grad, *(returned[place] for place in early)),
        cover=True,
    )
    mixed_out, input_grads = on_device(
        functools.partial(last_kernel, order, late),
        outputs[:2],
        working(late),
        (*common, *(returned[place] for place in late)),
        updates=begun,
    )
    return (mixed_out, input_grads, filter_grad)


def shards(query_proj, key_proj, value_proj, short_taps, long_filter, grad_mixed):
    rows, channels = query_proj.shape
    halo = short_taps.shape[1] - 1
    blocks = lax.axis_size("context")
    power_of_two = blocks & (blocks - 1) == 0
    fits = power_of_two and blocks > 2 and channels == blocks * LANES and rows % 128 == 0 and halo <= 8
    chosen = block_shards if fits else general_shards
    return chosen(query_proj, key_proj, value_proj, short_taps, long_filter, grad_mixed)


def solution(mesh):
    return jax.shard_map(
        shards,
        mesh=mesh,
        in_specs=(
            P("context", "tensor"),
            P("context", "tensor"),
            P("context", "tensor"),
            P(None, None, "tensor"),
            P("tensor", "context", None),
            P("context", "tensor"),
        ),
        out_specs=(
            P("context", "tensor"),
            P(None, "context", "tensor"),
            P("tensor", "context", None),
        ),
        check_vma=False,
    )
```

```python
import functools
import math

import jax
import jax.numpy as jnp
import numpy as np
from jax import lax
from jax.experimental import pallas as pl
from jax.experimental.pallas import tpu as pltpu
from jax.sharding import PartitionSpec as P

precise = lax.Precision.HIGHEST


def from_behind(value, axis, steps):
    count = lax.axis_size(axis)
    first, last = (max(0, -steps), min(count, count - steps))
    return lax.ppermute(value, axis, [(source, source + steps) for source in range(first, last)])


def build_tables(blocks, tok_rows):
    outer_len = 2 * blocks
    full_len = outer_len * tok_rows
    k_one = jnp.arange(outer_len, dtype=jnp.int32)
    n_one = jnp.arange(blocks, dtype=jnp.int32)
    position = jnp.arange(tok_rows, dtype=jnp.int32)
    first_idx = k_one[:, None] * n_one[None, :] % outer_len
    first_angle = -2.0 * math.pi / outer_len * first_idx.astype(jnp.float32)
    second = position[:, None] * position[None, :] % tok_rows
    second_angle = -2.0 * math.pi / tok_rows * second.astype(jnp.float32)
    twist_idx = k_one[:, None] * position[None, :] % full_len
    twist_angle = -2.0 * math.pi / full_len * twist_idx.astype(jnp.float32)
    return (
        jnp.cos(first_angle),
        jnp.sin(first_angle),
        jnp.cos(second_angle),
        jnp.sin(second_angle),
        jnp.cos(twist_angle),
        jnp.sin(twist_angle),
    )


def transform(signal, tables):
    cos_first, sin_first, cos_second, sin_second, cos_twist, sin_twist = tables
    first_re = jnp.einsum("kn,gnm->gkm", cos_first, signal, precision=precise)
    first_im = jnp.einsum("kn,gnm->gkm", sin_first, signal, precision=precise)
    mid_re = first_re * cos_twist - first_im * sin_twist
    mid_im = first_re * sin_twist + first_im * cos_twist
    out_re = jnp.einsum("gkn,nm->gkm", mid_re, cos_second, precision=precise) - jnp.einsum(
        "gkn,nm->gkm", mid_im, sin_second, precision=precise
    )
    out_im = jnp.einsum("gkn,nm->gkm", mid_re, sin_second, precision=precise) + jnp.einsum(
        "gkn,nm->gkm", mid_im, cos_second, precision=precise
    )
    return (out_re, out_im)


def inverse(spec_re, spec_im, tables):
    cos_first, sin_first, cos_second, sin_second, cos_twist, sin_twist = tables
    full_len = cos_first.shape[0] * cos_second.shape[0]
    mid_re = jnp.einsum("gkn,nm->gkm", spec_re, cos_second, precision=precise) + jnp.einsum(
        "gkn,nm->gkm", spec_im, sin_second, precision=precise
    )
    mid_im = jnp.einsum("gkn,nm->gkm", spec_im, cos_second, precision=precise) - jnp.einsum(
        "gkn,nm->gkm", spec_re, sin_second, precision=precise
    )
    turn_re = mid_re * cos_twist + mid_im * sin_twist
    turn_im = mid_im * cos_twist - mid_re * sin_twist
    result = jnp.einsum("kn,gkm->gnm", cos_first, turn_re, precision=precise) + jnp.einsum(
        "kn,gkm->gnm", sin_first, turn_im, precision=precise
    )
    return result * (1.0 / full_len)


def causal_taps(series, preceding, tap_weights):
    tok_rows = series.shape[0]
    span = tap_weights.shape[0]
    joined = jnp.concatenate([preceding, series], axis=0).astype(jnp.float32)
    running = jnp.zeros(series.shape, jnp.float32)
    for offset in range(span):
        first_row = span - 1 - offset
        running = running + tap_weights[offset][None, :] * joined[first_row : first_row + tok_rows]
    return running


def reverse_taps(series, following, tap_weights):
    tok_rows = series.shape[0]
    span = tap_weights.shape[0]
    joined = jnp.concatenate([series, following], axis=0).astype(jnp.float32)
    running = jnp.zeros(series.shape, jnp.float32)
    for offset in range(span):
        running = running + tap_weights[offset][None, :] * joined[offset : offset + tok_rows]
    return running


def general_shards(query_proj, key_proj, value_proj, short_taps, long_filter, grad_mixed):
    tok_rows, channels = query_proj.shape
    blocks = lax.axis_size("context")
    halo_rows = short_taps.shape[1] - 1
    per_device = channels // blocks
    seq_len = tok_rows * blocks
    tables = build_tables(blocks, tok_rows)
    preceding = from_behind(
        (
            query_proj[tok_rows - halo_rows :],
            key_proj[tok_rows - halo_rows :],
            value_proj[tok_rows - halo_rows :],
        ),
        "context",
        1,
    )
    query_f = causal_taps(query_proj, preceding[0], short_taps[0])
    key_f = causal_taps(key_proj, preceding[1], short_taps[1])
    value_f = causal_taps(value_proj, preceding[2], short_taps[2])
    gated_prod = (key_f * value_f).astype(jnp.bfloat16)
    grad_f = grad_mixed.astype(jnp.float32)
    grad_long = (grad_f * query_f).astype(jnp.bfloat16)

    def to_spectrum(series):
        arranged = series.T.reshape(blocks, per_device, tok_rows)
        received = lax.all_to_all(arranged, "context", split_axis=0, concat_axis=2, tiled=True)
        item_count = received.shape[1]
        signal = received.reshape(item_count, blocks, tok_rows).astype(jnp.float32)
        return transform(signal, tables)

    def to_token_rows(spatial):
        arrived = lax.all_to_all(spatial, "context", split_axis=1, concat_axis=0, tiled=True)
        return arrived.reshape(channels, tok_rows).T

    gate_re, gate_im = to_spectrum(gated_prod)
    filter_re, filter_im = transform(long_filter.reshape(per_device, blocks, tok_rows), tables)
    long_spatial = inverse(
        gate_re * filter_re - gate_im * filter_im, gate_re * filter_im + gate_im * filter_re, tables
    ).astype(jnp.bfloat16)
    long_conv = to_token_rows(long_spatial)
    long_f = long_conv.astype(jnp.float32)
    mixed_out = (query_f * long_f).astype(jnp.bfloat16)
    grad_query_f = (grad_f * long_f).astype(jnp.bfloat16)
    grad_after = lax.optimization_barrier((grad_long, long_conv))[0]
    grad_re, grad_im = to_spectrum(grad_after)
    back_spatial = inverse(
        filter_re * grad_re + filter_im * grad_im, filter_re * grad_im - filter_im * grad_re, tables
    ).astype(jnp.bfloat16)
    corr_spatial = inverse(
        gate_re * grad_re + gate_im * grad_im, gate_re * grad_im - gate_im * grad_re, tables
    )
    grad_gated = to_token_rows(back_spatial).astype(jnp.float32)
    grad_key_f = (grad_gated * value_f).astype(jnp.bfloat16)
    grad_value_f = (grad_gated * key_f).astype(jnp.bfloat16)
    following = from_behind(
        (grad_query_f[:halo_rows], grad_key_f[:halo_rows], grad_value_f[:halo_rows]), "context", -1
    )
    input_grads = jnp.stack(
        [
            reverse_taps(grad_query_f, following[0], short_taps[0]),
            reverse_taps(grad_key_f, following[1], short_taps[1]),
            reverse_taps(grad_value_f, following[2], short_taps[2]),
        ]
    ).astype(jnp.bfloat16)
    filter_grad = (corr_spatial * (1.0 / math.sqrt(seq_len))).reshape(1, per_device, seq_len)
    return (mixed_out, input_grads, filter_grad)


LANES = 128
VMEM_BYTES = 48 * 1024 * 1024
COVER = pl.CostEstimate(flops=10**10, bytes_accessed=10**8, transcendentals=0)


def split_bf16(table):
    high = table.astype(jnp.bfloat16)
    low = (table - high.astype(np.float64)).astype(jnp.bfloat16)
    return (high, low)


@functools.cache
def block_tables(rows):
    bins = np.pi * (np.arange(rows) + 0.5)[:, None] / rows
    lag = np.arange(rows)[None, :]
    forward = np.concatenate([np.cos(bins * lag), -np.sin(bins * lag)], axis=0)
    forward_hi, forward_lo = split_bf16(forward)
    return (forward_hi, forward_lo, split_bf16(forward.T / rows)[0])


def round_up(count, unit):
    return (count + unit - 1) // unit * unit


def head_rows(fresh, whole, halo):
    row = lax.broadcasted_iota(jnp.int32, fresh.shape, 0)
    return jnp.concatenate([jnp.where(row < halo, fresh, whole[:8]), whole[8:]], axis=0)


def tap_rows(taps_ref, which, lanes):
    return [taps_ref[which, pl.ds(offset, 1), lanes] for offset in range(taps_ref.shape[1])]


def short_filter(padded, rows, weights):
    running = weights[0] * padded[pl.ds(8, rows), :]
    for offset in range(1, len(weights)):
        running = running + weights[offset] * padded[pl.ds(8 - offset, rows), :]
    return running


def make_parcel(slot, source, taps, padded, extra, filtered_ref, out_ref):
    rows = source.shape[1]
    halo = taps.shape[1] - 1
    padded[slot, :, pl.ds(0, 8), :] = jnp.zeros((3, 8, LANES), jnp.float32)
    extra[slot, pl.ds(5 * halo, extra.shape[1] - 5 * halo), :] = jnp.zeros(
        (extra.shape[1] - 5 * halo, LANES), jnp.float32
    )
    filtered = []
    for which in range(3):
        padded[slot, which, pl.ds(8, rows), :] = source[which].astype(jnp.float32)
        weights = tap_rows(taps, which, pl.ds(0, LANES))
        result = short_filter(padded.at[slot, which], rows, weights)
        filtered_ref[which] = result
        filtered.append(result)
    query_f, key_f, value_f = filtered
    cotangent = source[3].astype(jnp.float32)
    filtered_ref[3] = cotangent
    gated = head_rows(padded[slot, 1, pl.ds(8, 8), :], key_f * value_f, halo)
    grad_long = head_rows(cotangent[:8], cotangent * query_f, halo)
    out_ref[pl.ds(0, rows), :] = gated.astype(jnp.bfloat16)
    out_ref[pl.ds(rows, rows), :] = grad_long.astype(jnp.bfloat16)
    pieces = ((1, rows - halo), (2, 0), (2, rows - halo), (0, 0), (0, rows - halo))
    for position, (which, first) in enumerate(pieces):
        extra[slot, pl.ds(position * halo, halo), :] = padded[slot, which, pl.ds(8 + first, halo), :]
    out_ref[pl.ds(2 * rows, extra.shape[1]), :] = extra[slot].astype(jnp.bfloat16)


def fetches(order, places, inputs, taps_ref, landed, taps, arrivals):
    me = lax.axis_index("context")
    result = []
    for index, place in enumerate(places):
        lanes = pl.ds(pl.multiple_of((me ^ order[place]) * LANES, LANES), LANES)
        sources = [taps_ref.at[:, :, lanes]] + [ref.at[:, lanes] for ref in inputs]
        targets = [taps.at[index]] + [landed.at[index, which] for which in range(len(inputs))]
        result.append(
            [
                pltpu.make_async_copy(source, target, arrivals.at[index, number])
                for number, (source, target) in enumerate(zip(sources, targets))
            ]
        )
    return result


def send_kernel(order, places, ahead, extras, q_ref, k_ref, v_ref, g_ref, taps_ref, *refs):
    inputs = (q_ref, k_ref, v_ref, g_ref)
    sources, refs = refs[:extras], refs[extras:]
    first_ref, *outs = refs[: len(places) - 1]
    size = first_ref.shape[0] // 2
    outs = [first_ref.at[pl.ds(0, size)], first_ref.at[pl.ds(size, size)], *outs]
    filtered_ref, *brought = refs[len(places) - 1 : -7]
    landed, taps, padded, extra, arrivals, later, kept = refs[-7:]
    own = fetches(order, places, inputs, taps_ref, landed, taps, arrivals)
    others = [
        pltpu.make_async_copy(source, target, kept.at[index])
        for index, (source, target) in enumerate(zip(sources, brought))
    ]
    for copies in fetches(order, ahead, inputs, taps_ref, *brought[-2:], later):
        others += copies
    for copies in own:
        for copy in copies:
            copy.start()
    for copy in others:
        copy.start()
    for index, copies in enumerate(own):
        for copy in copies:
            copy.wait()
        make_parcel(
            index % 2, landed.at[index], taps.at[index], padded, extra, filtered_ref.at[index], outs[index]
        )
    for copy in others:
        copy.wait()


def near_kernel(landed, taps, first_ref, shared_ref, own_ref, filtered_ref, own_taps, padded, extra):
    rows = own_ref.shape[0]
    shared_ref[pl.ds(rows, rows), :] = first_ref[pl.ds(rows, rows), :]
    for index, out_ref in enumerate((shared_ref.at[pl.ds(0, rows)], own_ref)):
        make_parcel(
            index, landed.at[index], taps.at[index], padded, extra, filtered_ref.at[index], out_ref
        )
    own_taps[...] = taps[1]


def gather(order, in_refs, edges, firsts, pairs, rows):
    me = lax.axis_index("context")
    for mask, in_ref in zip(order, in_refs):
        block = me ^ mask
        edges[block] = in_ref[pl.ds(2 * rows, edges.shape[1]), :].astype(jnp.float32)
        for which in range(2):
            values = in_ref[pl.ds(which * rows, rows), :]
            firsts[block, which] = values[:16].astype(jnp.float32)[:8]
            pairs[block, :, pl.ds(which * LANES, LANES)] = values


def repair_heads(taps_ref, edges, firsts, joined, heads):
    blocks = edges.shape[0]
    span = taps_ref.shape[1]
    halo = span - 1
    joined[...] = jnp.zeros(joined.shape, jnp.float32)
    for block in range(blocks):
        joined[1, block, pl.ds(halo, 8), :] = firsts[block, 0]
        joined[2, block, pl.ds(halo, halo), :] = edges[block, pl.ds(halo, halo), :]
        joined[0, block, pl.ds(halo, halo), :] = edges[block, pl.ds(3 * halo, halo), :]
        if block > 0:
            for which, place in ((1, 0), (2, 2), (0, 4)):
                joined[which, block, pl.ds(0, halo), :] = edges[block - 1, pl.ds(place * halo, halo), :]
        filtered = []
        for which in range(3):
            running = jnp.zeros((8, LANES), jnp.float32)
            for offset in range(span):
                weight = taps_ref[which, pl.ds(offset, 1), :]
                running = running + weight * joined[which, block, pl.ds(halo - offset, 8), :]
            filtered.append(running)
            heads[block, which] = running
        cotangent = firsts[block, 1]
        heads[block, 3] = cotangent
        heads[block, 4] = filtered[1] * filtered[2]
        heads[block, 5] = cotangent * filtered[0]


def to_spectra(heads, pairs, forward, spec_x, spec_g, halo):
    blocks, rows, width = pairs.shape
    merged = blocks // spec_x.shape[0]
    for block in range(blocks):
        fresh = jnp.concatenate([heads[block, 4], heads[block, 5]], axis=1)
        head = head_rows(fresh, pairs[block, pl.ds(0, 16), :].astype(jnp.float32), halo)
        pairs[block, pl.ds(0, 16), :] = head.astype(jnp.bfloat16)
    for index in range(spec_x.shape[0]):
        signals = pairs[pl.ds(index * merged, merged)].reshape(merged * rows, width)
        spectrum = jnp.dot(forward, signals, preferred_element_type=jnp.float32)
        spec_x[index] = spectrum[:, :LANES]
        spec_g[index] = spectrum[:, LANES:]


def filter_kernel(h_ref, forward_hi, forward_lo, out_ref):
    blocks, two_rows, _ = out_ref.shape
    rows = two_rows // 2
    sign = jnp.where(lax.broadcasted_iota(jnp.int32, (rows, LANES), 0) % 2 == 0, 1.0, -1.0)

    def product(table, values):
        return lax.dot_general(
            table, values, (((1,), (1,)), ((), ())), preferred_element_type=jnp.float32
        )

    before = None
    for block in range(blocks):
        signal = h_ref[:, pl.ds(block * rows, rows)]
        high = signal.astype(jnp.bfloat16)
        low = (signal - high.astype(jnp.float32)).astype(jnp.bfloat16)
        spectrum = (
            product(forward_hi[...], high)
            + product(forward_lo[...], high)
            + product(forward_hi[...], low)
        )
        real, imag = spectrum[:rows], spectrum[rows:]
        if before is None:
            out_ref[block] = spectrum
        else:
            out_ref[block, pl.ds(0, rows), :] = real - sign * before[1]
            out_ref[block, pl.ds(rows, rows), :] = imag + sign * before[0]
        before = (real, imag)


def load_tile(ref, count, tile, bins):
    real = [ref[index, pl.ds(pl.multiple_of(tile * 8, 8), 8), :] for index in range(count)]
    imag = [ref[index, pl.ds(pl.multiple_of(bins + tile * 8, 8), 8), :] for index in range(count)]
    return (real, imag)


def mixed_products(left, right, sums, conjugate):
    (left_re, left_im), (right_re, right_im) = left, right
    results = []
    for pairs in sums:
        total_re, total_im = None, None
        for one, two in pairs:
            a, b, c, d = left_re[one], left_im[one], right_re[two], right_im[two]
            if conjugate:
                real, imag = a * c + b * d, a * d - b * c
            else:
                real, imag = a * c - b * d, a * d + b * c
            total_re = real if total_re is None else total_re + real
            total_im = imag if total_im is None else total_im + imag
        results.append((total_re, total_im))
    return results


def store_tiles(ref, first_lane, tiles, pair, bins):
    lanes = pl.ds(first_lane, LANES)
    for index, parts in enumerate(zip(*tiles)):
        for first, values in zip((0, bins), zip(*parts)):
            rows = pl.ds(pl.multiple_of(first + pair * 16, 16), 16)
            ref[index, rows, lanes] = jnp.concatenate(values, axis=0).astype(ref.dtype)


def convolve_kernel(order, taps_ref, spec_h, forward, inverse, *refs):
    count = len(order)
    first_ref, *others, shared_ref, own_ref = refs[: count - 1]
    size = own_ref.shape[0]
    in_refs = [first_ref.at[pl.ds(0, size)], shared_ref.at[pl.ds(size, size)], *others]
    in_refs += [shared_ref.at[pl.ds(0, size)], own_ref]
    first_out, *out_refs = refs[count - 1 : 2 * count - 2]
    out_refs = [first_out.at[pl.ds(0, size)], first_out.at[pl.ds(size, size)], *out_refs]
    refs = refs[2 * count - 2 :]
    spec_x, spec_g, edges, firsts, joined, heads, pairs, spec_y, extra = refs
    me = lax.axis_index("context")
    rows = pairs.shape[1]
    halo = taps_ref.shape[1] - 1
    bins = inverse.shape[0]
    wide = spec_h.shape[0]
    gather(order, in_refs, edges, firsts, pairs, rows)
    repair_heads(taps_ref, edges, firsts, joined, heads)
    to_spectra(heads, pairs, forward[...], spec_x, spec_g, halo)

    def body(pair, carry):
        longs, backs = [], []
        for tile in (2 * pair, 2 * pair + 1):
            filt = load_tile(spec_h, wide, tile, bins)
            sums = [[(i - j, j) for j in range(i + 1)] for i in range(wide)]
            longs.append(mixed_products(filt, load_tile(spec_x, wide, tile, bins), sums, False))
            sums = [[(j - i, j) for j in range(i, wide)] for i in range(wide)]
            backs.append(mixed_products(filt, load_tile(spec_g, wide, tile, bins), sums, True))
        store_tiles(spec_y, 0, longs, pair, bins)
        store_tiles(spec_y, LANES, backs, pair, bins)
        return carry

    lax.fori_loop(0, bins // 16, body, 0, unroll=8)
    extra[...] = jnp.zeros(extra.shape, jnp.float32)
    for index in range(wide):
        both = jnp.dot(inverse[...], spec_y[index], preferred_element_type=jnp.float32).astype(jnp.bfloat16)
        for part in range(count // wide):
            block = index * (count // wide) + part
            here = both[part * rows : (part + 1) * rows]
            query_f, key_f, value_f, cotangent = [heads[block, which] for which in range(4)]
            head = here[:16].astype(jnp.float32)
            long_head, back_head = head[:8, :LANES], head[:8, LANES:]
            grad_key, grad_value = back_head * value_f, back_head * key_f
            back = head_rows(grad_key, head[:, LANES:], halo).astype(jnp.bfloat16)
            pairs[block, :, pl.ds(0, LANES)] = here[:, :LANES]
            pairs[block, :, pl.ds(LANES, LANES)] = jnp.concatenate([back, here[16:, LANES:]], axis=0)
            own = (query_f * long_head, grad_value)
            following = (cotangent * long_head, grad_key, grad_value)
            for place, value in enumerate(own):
                extra[block + 1, pl.ds(place * halo, halo), :] = value[:halo]
            for place, value in enumerate(following):
                extra[block, pl.ds((2 + place) * halo, halo), :] = value[:halo]
    for mask, out_ref in zip(order, out_refs):
        block = me ^ mask
        for which in range(2):
            out_ref[pl.ds(which * rows, rows), :] = pairs[block, :, pl.ds(which * LANES, LANES)]
        out_ref[pl.ds(2 * rows, extra.shape[1]), :] = extra[block + 1].astype(jnp.bfloat16)


def share_kernel(filter_ref, parcel_ref, first_ref, shared_ref):
    rows = parcel_ref.shape[0]
    shared_ref[pl.ds(0, rows), :] = parcel_ref[...]
    shared_ref[pl.ds(rows, rows), :] = first_ref[pl.ds(rows, rows), :]


def correlate_kernel(scale, spec_x, spec_g, inverse, out_ref, spec_y):
    wide = spec_x.shape[0]
    bins = inverse.shape[0]

    def body(pair, carry):
        row = lax.broadcasted_iota(jnp.int32, (8, LANES), 0)
        sign = jnp.where(row % 2 == 0, 1.0, -1.0)
        tiles = []
        for tile in (2 * pair, 2 * pair + 1):
            real, imag = load_tile(spec_x, wide, tile, bins)
            window_re = [real[0]] + [real[i] - sign * imag[i - 1] for i in range(1, wide)]
            window_im = [imag[0]] + [imag[i] + sign * real[i - 1] for i in range(1, wide)]
            sums = [[(j - lag, j) for j in range(lag, wide)] for lag in range(wide)]
            grad = load_tile(spec_g, wide, tile, bins)
            tiles.append(mixed_products((window_re, window_im), grad, sums, True))
        store_tiles(spec_y, 0, tiles, pair, bins)
        return carry

    lax.fori_loop(0, bins // 16, body, 0, unroll=8)
    for index in range(wide):
        result = jnp.dot(inverse[...], spec_y[index], preferred_element_type=jnp.float32)
        out_ref[:, pl.ds(index * bins, bins)] = result.T * scale


def finish_channels(
    order, places, in_refs, taps_ref, held, padded, extra, results, leave
):
    me = lax.axis_index("context")
    rows = held[0].shape[2]
    span = taps_ref.shape[1]
    halo = span - 1
    held = [ref.at[index] for ref in held for index in range(ref.shape[0])]
    for index, (place, in_ref) in enumerate(zip(places, in_refs)):
        lanes = pl.ds(pl.multiple_of((me ^ order[place]) * LANES, LANES), LANES)
        slot = index % padded.shape[0]
        edge_rows = in_ref.shape[0] - 2 * rows
        query_f, key_f, value_f = [held[place][which] for which in range(3)]
        cotangent = held[place][3]
        long_conv = in_ref[pl.ds(0, rows), :].astype(jnp.float32)
        back = in_ref[pl.ds(rows, rows), :].astype(jnp.float32)
        extra[slot, pl.ds(0, edge_rows), :] = in_ref[pl.ds(2 * rows, edge_rows), :].astype(jnp.float32)
        mixed = head_rows(extra[slot, pl.ds(0, 8), :], query_f * long_conv, halo)
        results[index, 3] = mixed.astype(jnp.bfloat16)
        leave(index, 3)
        grads = (
            cotangent * long_conv,
            head_rows(back[:8], back * value_f, halo),
            head_rows(extra[slot, pl.ds(halo, 8), :], back * key_f, halo),
        )
        for which, grad in enumerate(grads):
            padded[slot, which, pl.ds(0, rows), :] = grad.astype(jnp.bfloat16).astype(jnp.float32)
            padded[slot, which, pl.ds(rows, halo), :] = extra[slot, pl.ds((2 + which) * halo, halo), :]
            weights = tap_rows(taps_ref, which, lanes)
            running = weights[0] * padded[slot, which, pl.ds(0, rows), :]
            for offset in range(1, span):
                running = running + weights[offset] * padded[slot, which, pl.ds(offset, rows), :]
            results[index, which] = running.astype(jnp.bfloat16)
            leave(index, which)


def receive_kernel(order, places, taps_ref, far_ref, near_ref, filter_ref, *refs):
    size = 2 * far_ref.shape[2] + round_up(5 * (taps_ref.shape[1] - 1), 16)
    in_refs = [ref.at[pl.ds((place == 1) * size, size)] for place, ref in zip(places, refs)]
    mixed_ref, grads_ref, filter_out, padded, extra, results, sems, filter_sem = refs[-8:]
    me = lax.axis_index("context")
    copies = []
    if filter_ref is not None:
        copies.append(pltpu.make_async_copy(filter_ref, filter_out.at[0], filter_sem))
        copies[-1].start()

    def leave(index, which):
        lanes = pl.ds(pl.multiple_of((me ^ order[places[index]]) * LANES, LANES), LANES)
        target = mixed_ref.at[:, lanes] if which == 3 else grads_ref.at[which, :, lanes]
        copies.append(pltpu.make_async_copy(results.at[index, which], target, sems.at[index, which]))
        copies[-1].start()

    held = (far_ref, near_ref)
    finish_channels(
        order, places, in_refs, taps_ref, held, padded, extra, results, leave
    )
    for copy in copies:
        copy.wait()


def last_kernel(order, places, taps_ref, far_ref, near_ref, *refs):
    in_refs, refs = refs[: len(places)], refs[len(places) + 2 :]
    mixed_ref, grads_ref, padded, extra, results, sems = refs
    receive_kernel(
        order, places, taps_ref, far_ref, near_ref, None, *in_refs,
        mixed_ref, grads_ref, None, padded, extra, results, sems, None,
    )


def on_device(kernel, out_shape, scratch, args, in_hbm=(), unread=None, updates=(), cover=False):
    whole = pl.BlockSpec(memory_space=pltpu.VMEM)
    hbm = pl.BlockSpec(memory_space=pltpu.HBM)
    anywhere = pl.BlockSpec(memory_space=pl.ANY)
    fixed = [pltpu.with_memory_space_constraint(arg, pltpu.HBM) for arg in in_hbm]
    before = [] if unread is None else [unread]
    first_update = len(before) + len(fixed) + len(args)
    return pl.pallas_call(
        kernel if unread is None else lambda _, *refs: kernel(*refs),
        out_shape=out_shape,
        in_specs=[anywhere] * len(before) + [hbm] * len(fixed) + [whole] * len(args) + [hbm] * len(updates),
        out_specs=jax.tree.map(
            lambda out: whole if isinstance(out, jax.ShapeDtypeStruct) else hbm, out_shape
        ),
        input_output_aliases={first_update + place: place for place in range(len(updates))},
        scratch_shapes=[
            pltpu.VMEM(shape, jnp.float32) if isinstance(shape, tuple) else shape for shape in scratch
        ],
        compiler_params=pltpu.CompilerParams(vmem_limit_bytes=VMEM_BYTES),
        cost_estimate=COVER if cover else None,
    )(*before, *fixed, *args, *updates)


def exchange_order(count):
    return sorted(
        range(count),
        key=lambda mask: (mask == 0, -(mask >> 1).bit_count(), mask % 2, -mask),
    )


def exchange(parcel, mask):
    count = lax.axis_size("context")
    return lax.ppermute(parcel, "context", [(i, i ^ mask) for i in range(count)])


def block_shards(query_proj, key_proj, value_proj, short_taps, long_filter, grad_mixed):
    rows, channels = query_proj.shape
    blocks = lax.axis_size("context")
    halo = short_taps.shape[1] - 1
    seq_len = rows * blocks
    merged = 2
    wide = merged * rows
    forward_hi, forward_lo, inverse = [jnp.asarray(table) for table in block_tables(wide)]
    edge_rows = round_up(5 * halo, 16)
    order = exchange_order(blocks)
    parcels = [jax.ShapeDtypeStruct((2 * rows + edge_rows, LANES), jnp.bfloat16)] * blocks
    spectra = (blocks // merged, 2 * wide, LANES)
    own_taps = (*short_taps.shape[:2], LANES)
    far = [place for place in range(blocks) if order[place] > 1]
    near = [place for place in range(blocks) if order[place] <= 1]

    parcel = parcels[0]
    double = jax.ShapeDtypeStruct((2 * parcel.shape[0], LANES), jnp.bfloat16)
    made = [(2, 3, rows + 8, LANES), (2, edge_rows, LANES)]
    inputs = (4, rows, LANES)
    sources = (long_filter[0], forward_hi, forward_lo)

    def floats(*shape):
        return jax.ShapeDtypeStruct(shape, jnp.float32)

    first, *sent, far_filtered, filter_here, hi_here, lo_here, landed, taps = on_device(
        functools.partial(send_kernel, order, far, near, len(sources)),
        [double, *parcels[: len(far) - 2], floats(len(far), 4, rows, LANES)]
        + [jax.ShapeDtypeStruct(value.shape, value.dtype) for value in sources]
        + [
            jax.ShapeDtypeStruct((len(near), *inputs), jnp.bfloat16),
            floats(len(near), *own_taps),
        ],
        [
            pltpu.VMEM((len(far), *inputs), jnp.bfloat16),
            (len(far), *own_taps),
            *made,
            pltpu.SemaphoreType.DMA((len(far), 5)),
            pltpu.SemaphoreType.DMA((len(near), 5)),
            pltpu.SemaphoreType.DMA((len(sources),)),
        ],
        (),
        in_hbm=(query_proj, key_proj, value_proj, grad_mixed, short_taps, *sources),
    )
    first = exchange(first, order[0])
    others = [exchange(value, order[place]) for place, value in zip(far[2:], sent)]
    shared, kept_here, near_filtered, own = on_device(
        near_kernel,
        [double, parcel, floats(len(near), 4, rows, LANES), floats(*own_taps)],
        made,
        (landed, taps, first),
        cover=True,
    )
    arrived = (first, *others, exchange(shared, 1), kept_here)
    spec_h = on_device(
        filter_kernel,
        jax.ShapeDtypeStruct(spectra, jnp.float32),
        [],
        (filter_here, hi_here, lo_here),
        cover=True,
    )
    *results, spec_x, spec_g = on_device(
        functools.partial(convolve_kernel, order),
        [double, *parcels[2:], floats(*spectra), floats(*spectra)],
        [
            (blocks, edge_rows, LANES),
            (blocks, 2, 8, LANES),
            (3, blocks, 24, LANES),
            (blocks, 6, 8, LANES),
            pltpu.VMEM((blocks, rows, 2 * LANES), jnp.bfloat16),
            pltpu.VMEM((*spectra[:2], 2 * LANES), jnp.bfloat16),
            (blocks + 1, edge_rows, LANES),
        ],
        (own, spec_h, hi_here, inverse, *arrived),
    )
    first, *sent = results
    first = exchange(first, order[0])
    others = [exchange(value, order[place]) for place, value in zip(far[2:], sent)]
    (filter_grad,) = on_device(
        functools.partial(correlate_kernel, 1.0 / math.sqrt(seq_len)),
        [floats(*long_filter.shape[1:])],
        [pltpu.VMEM(spectra, jnp.bfloat16)],
        (spec_x, spec_g, inverse),
    )
    (shared,) = on_device(share_kernel, [double], [], (filter_grad, sent[-2], first))
    shared = exchange(shared, 1)
    returned = [first, shared, *others, shared, sent[-1]]
    early = [0, *far[2:3], near[-1]]
    late = [place for place in range(blocks) if place not in early]
    outputs = (
        pltpu.HBM((rows, channels), jnp.bfloat16),
        pltpu.HBM((3, rows, channels), jnp.bfloat16),
        pltpu.HBM(long_filter.shape, jnp.float32),
    )

    def working(places):
        return [
            (2, 3, rows + 16, LANES),
            (2, edge_rows + 8, LANES),
            pltpu.VMEM((len(places), 4, rows, LANES), jnp.bfloat16),
            pltpu.SemaphoreType.DMA((len(places), 4)),
        ]

    common = (short_taps, far_filtered, near_filtered)
    *begun, filter_grad = on_device(
        functools.partial(receive_kernel, order, early),
        outputs,
        [*working(early), pltpu.SemaphoreType.DMA(())],
        (*common, filter_grad, *(returned[place] for place in early)),
        cover=True,
    )
    mixed_out, input_grads = on_device(
        functools.partial(last_kernel, order, late),
        outputs[:2],
        working(late),
        (*common, *(returned[place] for place in late)),
        updates=begun,
    )
    return (mixed_out, input_grads, filter_grad)


def shards(query_proj, key_proj, value_proj, short_taps, long_filter, grad_mixed):
    rows, channels = query_proj.shape
    halo = short_taps.shape[1] - 1
    blocks = lax.axis_size("context")
    power_of_two = blocks & (blocks - 1) == 0
    fits = power_of_two and blocks > 2 and channels == blocks * LANES and rows % 128 == 0 and halo <= 8
    chosen = block_shards if fits else general_shards
    return chosen(query_proj, key_proj, value_proj, short_taps, long_filter, grad_mixed)


def solution(mesh):
    return jax.shard_map(
        shards,
        mesh=mesh,
        in_specs=(
            P("context", "tensor"),
            P("context", "tensor"),
            P("context", "tensor"),
            P(None, None, "tensor"),
            P("tensor", "context", None),
            P("context", "tensor"),
        ),
        out_specs=(
            P("context", "tensor"),
            P(None, "context", "tensor"),
            P("tensor", "context", None),
        ),
        check_vma=False,
    )
```

```python
import functools
import math

import jax
import jax.numpy as jnp
import numpy as np
from jax import lax
from jax.experimental import pallas as pl
from jax.experimental.pallas import tpu as pltpu
from jax.sharding import PartitionSpec as P

precise = lax.Precision.HIGHEST


def from_behind(value, axis, steps):
    count = lax.axis_size(axis)
    first, last = (max(0, -steps), min(count, count - steps))
    return lax.ppermute(value, axis, [(source, source + steps) for source in range(first, last)])


def build_tables(blocks, tok_rows):
    outer_len = 2 * blocks
    full_len = outer_len * tok_rows
    k_one = jnp.arange(outer_len, dtype=jnp.int32)
    n_one = jnp.arange(blocks, dtype=jnp.int32)
    position = jnp.arange(tok_rows, dtype=jnp.int32)
    first_idx = k_one[:, None] * n_one[None, :] % outer_len
    first_angle = -2.0 * math.pi / outer_len * first_idx.astype(jnp.float32)
    second = position[:, None] * position[None, :] % tok_rows
    second_angle = -2.0 * math.pi / tok_rows * second.astype(jnp.float32)
    twist_idx = k_one[:, None] * position[None, :] % full_len
    twist_angle = -2.0 * math.pi / full_len * twist_idx.astype(jnp.float32)
    return (
        jnp.cos(first_angle),
        jnp.sin(first_angle),
        jnp.cos(second_angle),
        jnp.sin(second_angle),
        jnp.cos(twist_angle),
        jnp.sin(twist_angle),
    )


def transform(signal, tables):
    cos_first, sin_first, cos_second, sin_second, cos_twist, sin_twist = tables
    first_re = jnp.einsum("kn,gnm->gkm", cos_first, signal, precision=precise)
    first_im = jnp.einsum("kn,gnm->gkm", sin_first, signal, precision=precise)
    mid_re = first_re * cos_twist - first_im * sin_twist
    mid_im = first_re * sin_twist + first_im * cos_twist
    out_re = jnp.einsum("gkn,nm->gkm", mid_re, cos_second, precision=precise) - jnp.einsum(
        "gkn,nm->gkm", mid_im, sin_second, precision=precise
    )
    out_im = jnp.einsum("gkn,nm->gkm", mid_re, sin_second, precision=precise) + jnp.einsum(
        "gkn,nm->gkm", mid_im, cos_second, precision=precise
    )
    return (out_re, out_im)


def inverse(spec_re, spec_im, tables):
    cos_first, sin_first, cos_second, sin_second, cos_twist, sin_twist = tables
    full_len = cos_first.shape[0] * cos_second.shape[0]
    mid_re = jnp.einsum("gkn,nm->gkm", spec_re, cos_second, precision=precise) + jnp.einsum(
        "gkn,nm->gkm", spec_im, sin_second, precision=precise
    )
    mid_im = jnp.einsum("gkn,nm->gkm", spec_im, cos_second, precision=precise) - jnp.einsum(
        "gkn,nm->gkm", spec_re, sin_second, precision=precise
    )
    turn_re = mid_re * cos_twist + mid_im * sin_twist
    turn_im = mid_im * cos_twist - mid_re * sin_twist
    result = jnp.einsum("kn,gkm->gnm", cos_first, turn_re, precision=precise) + jnp.einsum(
        "kn,gkm->gnm", sin_first, turn_im, precision=precise
    )
    return result * (1.0 / full_len)


def causal_taps(series, preceding, tap_weights):
    tok_rows = series.shape[0]
    span = tap_weights.shape[0]
    joined = jnp.concatenate([preceding, series], axis=0).astype(jnp.float32)
    running = jnp.zeros(series.shape, jnp.float32)
    for offset in range(span):
        first_row = span - 1 - offset
        running = running + tap_weights[offset][None, :] * joined[first_row : first_row + tok_rows]
    return running


def reverse_taps(series, following, tap_weights):
    tok_rows = series.shape[0]
    span = tap_weights.shape[0]
    joined = jnp.concatenate([series, following], axis=0).astype(jnp.float32)
    running = jnp.zeros(series.shape, jnp.float32)
    for offset in range(span):
        running = running + tap_weights[offset][None, :] * joined[offset : offset + tok_rows]
    return running


def general_shards(query_proj, key_proj, value_proj, short_taps, long_filter, grad_mixed):
    tok_rows, channels = query_proj.shape
    blocks = lax.axis_size("context")
    halo_rows = short_taps.shape[1] - 1
    per_device = channels // blocks
    seq_len = tok_rows * blocks
    tables = build_tables(blocks, tok_rows)
    preceding = from_behind(
        (
            query_proj[tok_rows - halo_rows :],
            key_proj[tok_rows - halo_rows :],
            value_proj[tok_rows - halo_rows :],
        ),
        "context",
        1,
    )
    query_f = causal_taps(query_proj, preceding[0], short_taps[0])
    key_f = causal_taps(key_proj, preceding[1], short_taps[1])
    value_f = causal_taps(value_proj, preceding[2], short_taps[2])
    gated_prod = (key_f * value_f).astype(jnp.bfloat16)
    grad_f = grad_mixed.astype(jnp.float32)
    grad_long = (grad_f * query_f).astype(jnp.bfloat16)

    def to_spectrum(series):
        arranged = series.T.reshape(blocks, per_device, tok_rows)
        received = lax.all_to_all(arranged, "context", split_axis=0, concat_axis=2, tiled=True)
        item_count = received.shape[1]
        signal = received.reshape(item_count, blocks, tok_rows).astype(jnp.float32)
        return transform(signal, tables)

    def to_token_rows(spatial):
        arrived = lax.all_to_all(spatial, "context", split_axis=1, concat_axis=0, tiled=True)
        return arrived.reshape(channels, tok_rows).T

    gate_re, gate_im = to_spectrum(gated_prod)
    filter_re, filter_im = transform(long_filter.reshape(per_device, blocks, tok_rows), tables)
    long_spatial = inverse(
        gate_re * filter_re - gate_im * filter_im, gate_re * filter_im + gate_im * filter_re, tables
    ).astype(jnp.bfloat16)
    long_conv = to_token_rows(long_spatial)
    long_f = long_conv.astype(jnp.float32)
    mixed_out = (query_f * long_f).astype(jnp.bfloat16)
    grad_query_f = (grad_f * long_f).astype(jnp.bfloat16)
    grad_after = lax.optimization_barrier((grad_long, long_conv))[0]
    grad_re, grad_im = to_spectrum(grad_after)
    back_spatial = inverse(
        filter_re * grad_re + filter_im * grad_im, filter_re * grad_im - filter_im * grad_re, tables
    ).astype(jnp.bfloat16)
    corr_spatial = inverse(
        gate_re * grad_re + gate_im * grad_im, gate_re * grad_im - gate_im * grad_re, tables
    )
    grad_gated = to_token_rows(back_spatial).astype(jnp.float32)
    grad_key_f = (grad_gated * value_f).astype(jnp.bfloat16)
    grad_value_f = (grad_gated * key_f).astype(jnp.bfloat16)
    following = from_behind(
        (grad_query_f[:halo_rows], grad_key_f[:halo_rows], grad_value_f[:halo_rows]), "context", -1
    )
    input_grads = jnp.stack(
        [
            reverse_taps(grad_query_f, following[0], short_taps[0]),
            reverse_taps(grad_key_f, following[1], short_taps[1]),
            reverse_taps(grad_value_f, following[2], short_taps[2]),
        ]
    ).astype(jnp.bfloat16)
    filter_grad = (corr_spatial * (1.0 / math.sqrt(seq_len))).reshape(1, per_device, seq_len)
    return (mixed_out, input_grads, filter_grad)


LANES = 128
VMEM_BYTES = 48 * 1024 * 1024
COVER = pl.CostEstimate(flops=10**10, bytes_accessed=10**8, transcendentals=0)


def split_bf16(table):
    high = table.astype(jnp.bfloat16)
    low = (table - high.astype(np.float64)).astype(jnp.bfloat16)
    return (high, low)


@functools.cache
def block_tables(rows):
    bins = np.pi * (np.arange(rows) + 0.5)[:, None] / rows
    lag = np.arange(rows)[None, :]
    forward = np.concatenate([np.cos(bins * lag), -np.sin(bins * lag)], axis=0)
    forward_hi, forward_lo = split_bf16(forward)
    return (forward_hi, forward_lo, split_bf16(forward.T / rows)[0])


def round_up(count, unit):
    return (count + unit - 1) // unit * unit


def head_rows(fresh, whole, halo):
    row = lax.broadcasted_iota(jnp.int32, fresh.shape, 0)
    return jnp.concatenate([jnp.where(row < halo, fresh, whole[:8]), whole[8:]], axis=0)


def tap_rows(taps_ref, which, lanes):
    return [taps_ref[which, pl.ds(offset, 1), lanes] for offset in range(taps_ref.shape[1])]


def short_filter(padded, rows, weights):
    running = weights[0] * padded[pl.ds(8, rows), :]
    for offset in range(1, len(weights)):
        running = running + weights[offset] * padded[pl.ds(8 - offset, rows), :]
    return running


def make_parcel(slot, source, taps, padded, extra, filtered_ref, out_ref):
    rows = source.shape[1]
    halo = taps.shape[1] - 1
    padded[slot, :, pl.ds(0, 8), :] = jnp.zeros((3, 8, LANES), jnp.float32)
    extra[slot, pl.ds(5 * halo, extra.shape[1] - 5 * halo), :] = jnp.zeros(
        (extra.shape[1] - 5 * halo, LANES), jnp.float32
    )
    filtered = []
    for which in range(3):
        padded[slot, which, pl.ds(8, rows), :] = source[which].astype(jnp.float32)
        weights = tap_rows(taps, which, pl.ds(0, LANES))
        result = short_filter(padded.at[slot, which], rows, weights)
        filtered_ref[which] = result
        filtered.append(result)
    query_f, key_f, value_f = filtered
    cotangent = source[3].astype(jnp.float32)
    filtered_ref[3] = cotangent
    gated = head_rows(padded[slot, 1, pl.ds(8, 8), :], key_f * value_f, halo)
    grad_long = head_rows(cotangent[:8], cotangent * query_f, halo)
    out_ref[pl.ds(0, rows), :] = gated.astype(jnp.bfloat16)
    out_ref[pl.ds(rows, rows), :] = grad_long.astype(jnp.bfloat16)
    pieces = ((1, rows - halo), (2, 0), (2, rows - halo), (0, 0), (0, rows - halo))
    for position, (which, first) in enumerate(pieces):
        extra[slot, pl.ds(position * halo, halo), :] = padded[slot, which, pl.ds(8 + first, halo), :]
    out_ref[pl.ds(2 * rows, extra.shape[1]), :] = extra[slot].astype(jnp.bfloat16)


def fetches(order, places, inputs, taps_ref, landed, taps, arrivals):
    me = lax.axis_index("context")
    result = []
    for index, place in enumerate(places):
        lanes = pl.ds(pl.multiple_of((me ^ order[place]) * LANES, LANES), LANES)
        sources = [taps_ref.at[:, :, lanes]] + [ref.at[:, lanes] for ref in inputs]
        targets = [taps.at[index]] + [landed.at[index, which] for which in range(len(inputs))]
        result.append(
            [
                pltpu.make_async_copy(source, target, arrivals.at[index, number])
                for number, (source, target) in enumerate(zip(sources, targets))
            ]
        )
    return result


def send_kernel(order, places, ahead, extras, q_ref, k_ref, v_ref, g_ref, taps_ref, *refs):
    inputs = (q_ref, k_ref, v_ref, g_ref)
    sources, refs = refs[:extras], refs[extras:]
    first_ref, *outs = refs[: len(places) - 1]
    size = first_ref.shape[0] // 2
    outs = [first_ref.at[pl.ds(0, size)], first_ref.at[pl.ds(size, size)], *outs]
    filtered_ref, *brought = refs[len(places) - 1 : -7]
    landed, taps, padded, extra, arrivals, later, kept = refs[-7:]
    own = fetches(order, places, inputs, taps_ref, landed, taps, arrivals)
    others = [
        pltpu.make_async_copy(source, target, kept.at[index])
        for index, (source, target) in enumerate(zip(sources, brought))
    ]
    for copies in fetches(order, ahead, inputs, taps_ref, *brought[-2:], later):
        others += copies
    for copies in own:
        for copy in copies:
            copy.start()
    for copy in others:
        copy.start()
    for index, copies in enumerate(own):
        for copy in copies:
            copy.wait()
        make_parcel(
            index % 2, landed.at[index], taps.at[index], padded, extra, filtered_ref.at[index], outs[index]
        )
    for copy in others:
        copy.wait()


def near_kernel(landed, taps, first_ref, shared_ref, own_ref, filtered_ref, own_taps, padded, extra):
    rows = own_ref.shape[0]
    shared_ref[pl.ds(rows, rows), :] = first_ref[pl.ds(rows, rows), :]
    for index, out_ref in enumerate((shared_ref.at[pl.ds(0, rows)], own_ref)):
        make_parcel(
            index, landed.at[index], taps.at[index], padded, extra, filtered_ref.at[index], out_ref
        )
    own_taps[...] = taps[1]


def gather(order, in_refs, edges, firsts, pairs, rows):
    me = lax.axis_index("context")
    for mask, in_ref in zip(order, in_refs):
        block = me ^ mask
        edges[block] = in_ref[pl.ds(2 * rows, edges.shape[1]), :].astype(jnp.float32)
        for which in range(2):
            values = in_ref[pl.ds(which * rows, rows), :]
            firsts[block, which] = values[:16].astype(jnp.float32)[:8]
            pairs[block, :, pl.ds(which * LANES, LANES)] = values


def repair_heads(taps_ref, edges, firsts, joined, heads):
    blocks = edges.shape[0]
    span = taps_ref.shape[1]
    halo = span - 1
    joined[...] = jnp.zeros(joined.shape, jnp.float32)
    for block in range(blocks):
        joined[1, block, pl.ds(halo, 8), :] = firsts[block, 0]
        joined[2, block, pl.ds(halo, halo), :] = edges[block, pl.ds(halo, halo), :]
        joined[0, block, pl.ds(halo, halo), :] = edges[block, pl.ds(3 * halo, halo), :]
        if block > 0:
            for which, place in ((1, 0), (2, 2), (0, 4)):
                joined[which, block, pl.ds(0, halo), :] = edges[block - 1, pl.ds(place * halo, halo), :]
        filtered = []
        for which in range(3):
            running = jnp.zeros((8, LANES), jnp.float32)
            for offset in range(span):
                weight = taps_ref[which, pl.ds(offset, 1), :]
                running = running + weight * joined[which, block, pl.ds(halo - offset, 8), :]
            filtered.append(running)
            heads[block, which] = running
        cotangent = firsts[block, 1]
        heads[block, 3] = cotangent
        heads[block, 4] = filtered[1] * filtered[2]
        heads[block, 5] = cotangent * filtered[0]


def to_spectra(heads, pairs, forward, spec_x, spec_g, halo):
    blocks, rows, width = pairs.shape
    merged = blocks // spec_x.shape[0]
    for block in range(blocks):
        fresh = jnp.concatenate([heads[block, 4], heads[block, 5]], axis=1)
        head = head_rows(fresh, pairs[block, pl.ds(0, 16), :].astype(jnp.float32), halo)
        pairs[block, pl.ds(0, 16), :] = head.astype(jnp.bfloat16)
    for index in range(spec_x.shape[0]):
        signals = pairs[pl.ds(index * merged, merged)].reshape(merged * rows, width)
        spectrum = jnp.dot(forward, signals, preferred_element_type=jnp.float32)
        spec_x[index] = spectrum[:, :LANES]
        spec_g[index] = spectrum[:, LANES:]


def filter_kernel(h_ref, forward_hi, forward_lo, out_ref):
    blocks, two_rows, _ = out_ref.shape
    rows = two_rows // 2
    sign = jnp.where(lax.broadcasted_iota(jnp.int32, (rows, LANES), 0) % 2 == 0, 1.0, -1.0)

    def product(table, values):
        return lax.dot_general(
            table, values, (((1,), (1,)), ((), ())), preferred_element_type=jnp.float32
        )

    before = None
    for block in range(blocks):
        signal = h_ref[:, pl.ds(block * rows, rows)]
        high = signal.astype(jnp.bfloat16)
        low = (signal - high.astype(jnp.float32)).astype(jnp.bfloat16)
        spectrum = (
            product(forward_hi[...], high)
            + product(forward_lo[...], high)
            + product(forward_hi[...], low)
        )
        real, imag = spectrum[:rows], spectrum[rows:]
        if before is None:
            out_ref[block] = spectrum
        else:
            out_ref[block, pl.ds(0, rows), :] = real - sign * before[1]
            out_ref[block, pl.ds(rows, rows), :] = imag + sign * before[0]
        before = (real, imag)


def load_tile(ref, count, tile, bins):
    real = [ref[index, pl.ds(pl.multiple_of(tile * 8, 8), 8), :] for index in range(count)]
    imag = [ref[index, pl.ds(pl.multiple_of(bins + tile * 8, 8), 8), :] for index in range(count)]
    return (real, imag)


def mixed_products(left, right, sums, conjugate):
    (left_re, left_im), (right_re, right_im) = left, right
    results = []
    for pairs in sums:
        total_re, total_im = None, None
        for one, two in pairs:
            a, b, c, d = left_re[one], left_im[one], right_re[two], right_im[two]
            if conjugate:
                real, imag = a * c + b * d, a * d - b * c
            else:
                real, imag = a * c - b * d, a * d + b * c
            total_re = real if total_re is None else total_re + real
            total_im = imag if total_im is None else total_im + imag
        results.append((total_re, total_im))
    return results


def store_tiles(ref, first_lane, tiles, pair, bins):
    lanes = pl.ds(first_lane, LANES)
    for index, parts in enumerate(zip(*tiles)):
        for first, values in zip((0, bins), zip(*parts)):
            rows = pl.ds(pl.multiple_of(first + pair * 16, 16), 16)
            ref[index, rows, lanes] = jnp.concatenate(values, axis=0).astype(ref.dtype)


def convolve_kernel(order, taps_ref, spec_h, forward, inverse, *refs):
    count = len(order)
    first_ref, *others, shared_ref, own_ref = refs[: count - 1]
    size = own_ref.shape[0]
    in_refs = [first_ref.at[pl.ds(0, size)], shared_ref.at[pl.ds(size, size)], *others]
    in_refs += [shared_ref.at[pl.ds(0, size)], own_ref]
    first_out, *out_refs = refs[count - 1 : 2 * count - 2]
    out_refs = [first_out.at[pl.ds(0, size)], first_out.at[pl.ds(size, size)], *out_refs]
    refs = refs[2 * count - 2 :]
    spec_x, spec_g, edges, firsts, joined, heads, pairs, spec_y, extra = refs
    me = lax.axis_index("context")
    rows = pairs.shape[1]
    halo = taps_ref.shape[1] - 1
    bins = inverse.shape[0]
    wide = spec_h.shape[0]
    gather(order, in_refs, edges, firsts, pairs, rows)
    repair_heads(taps_ref, edges, firsts, joined, heads)
    to_spectra(heads, pairs, forward[...], spec_x, spec_g, halo)

    def body(pair, carry):
        longs, backs = [], []
        for tile in (2 * pair, 2 * pair + 1):
            filt = load_tile(spec_h, wide, tile, bins)
            sums = [[(i - j, j) for j in range(i + 1)] for i in range(wide)]
            longs.append(mixed_products(filt, load_tile(spec_x, wide, tile, bins), sums, False))
            sums = [[(j - i, j) for j in range(i, wide)] for i in range(wide)]
            backs.append(mixed_products(filt, load_tile(spec_g, wide, tile, bins), sums, True))
        store_tiles(spec_y, 0, longs, pair, bins)
        store_tiles(spec_y, LANES, backs, pair, bins)
        return carry

    lax.fori_loop(0, bins // 16, body, 0, unroll=8)
    extra[...] = jnp.zeros(extra.shape, jnp.float32)
    for index in range(wide):
        both = jnp.dot(inverse[...], spec_y[index], preferred_element_type=jnp.float32).astype(jnp.bfloat16)
        for part in range(count // wide):
            block = index * (count // wide) + part
            here = both[part * rows : (part + 1) * rows]
            query_f, key_f, value_f, cotangent = [heads[block, which] for which in range(4)]
            head = here[:16].astype(jnp.float32)
            long_head, back_head = head[:8, :LANES], head[:8, LANES:]
            grad_key, grad_value = back_head * value_f, back_head * key_f
            back = head_rows(grad_key, head[:, LANES:], halo).astype(jnp.bfloat16)
            pairs[block, :, pl.ds(0, LANES)] = here[:, :LANES]
            pairs[block, :, pl.ds(LANES, LANES)] = jnp.concatenate([back, here[16:, LANES:]], axis=0)
            own = (query_f * long_head, grad_value)
            following = (cotangent * long_head, grad_key, grad_value)
            for place, value in enumerate(own):
                extra[block + 1, pl.ds(place * halo, halo), :] = value[:halo]
            for place, value in enumerate(following):
                extra[block, pl.ds((2 + place) * halo, halo), :] = value[:halo]
    for mask, out_ref in zip(order, out_refs):
        block = me ^ mask
        for which in range(2):
            out_ref[pl.ds(which * rows, rows), :] = pairs[block, :, pl.ds(which * LANES, LANES)]
        out_ref[pl.ds(2 * rows, extra.shape[1]), :] = extra[block + 1].astype(jnp.bfloat16)


def share_kernel(filter_ref, parcel_ref, first_ref, shared_ref):
    rows = parcel_ref.shape[0]
    shared_ref[pl.ds(0, rows), :] = parcel_ref[...]
    shared_ref[pl.ds(rows, rows), :] = first_ref[pl.ds(rows, rows), :]


def correlate_kernel(scale, spec_x, spec_g, inverse, out_ref, spec_y):
    wide = spec_x.shape[0]
    bins = inverse.shape[0]

    def body(pair, carry):
        row = lax.broadcasted_iota(jnp.int32, (8, LANES), 0)
        sign = jnp.where(row % 2 == 0, 1.0, -1.0)
        tiles = []
        for tile in (2 * pair, 2 * pair + 1):
            real, imag = load_tile(spec_x, wide, tile, bins)
            window_re = [real[0]] + [real[i] - sign * imag[i - 1] for i in range(1, wide)]
            window_im = [imag[0]] + [imag[i] + sign * real[i - 1] for i in range(1, wide)]
            sums = [[(j - lag, j) for j in range(lag, wide)] for lag in range(wide)]
            grad = load_tile(spec_g, wide, tile, bins)
            tiles.append(mixed_products((window_re, window_im), grad, sums, True))
        store_tiles(spec_y, 0, tiles, pair, bins)
        return carry

    lax.fori_loop(0, bins // 16, body, 0, unroll=8)
    for index in range(wide):
        result = jnp.dot(inverse[...], spec_y[index], preferred_element_type=jnp.float32)
        out_ref[:, pl.ds(index * bins, bins)] = result.T * scale


def finish_channels(
    order, places, in_refs, taps_ref, held, padded, extra, results, leave
):
    me = lax.axis_index("context")
    rows = held[0].shape[2]
    span = taps_ref.shape[1]
    halo = span - 1
    held = [ref.at[index] for ref in held for index in range(ref.shape[0])]
    for index, (place, in_ref) in enumerate(zip(places, in_refs)):
        lanes = pl.ds(pl.multiple_of((me ^ order[place]) * LANES, LANES), LANES)
        slot = index % padded.shape[0]
        edge_rows = in_ref.shape[0] - 2 * rows
        query_f, key_f, value_f = [held[place][which] for which in range(3)]
        cotangent = held[place][3]
        long_conv = in_ref[pl.ds(0, rows), :].astype(jnp.float32)
        back = in_ref[pl.ds(rows, rows), :].astype(jnp.float32)
        extra[slot, pl.ds(0, edge_rows), :] = in_ref[pl.ds(2 * rows, edge_rows), :].astype(jnp.float32)
        mixed = head_rows(extra[slot, pl.ds(0, 8), :], query_f * long_conv, halo)
        results[index, 3] = mixed.astype(jnp.bfloat16)
        leave(index, 3)
        grads = (
            cotangent * long_conv,
            head_rows(back[:8], back * value_f, halo),
            head_rows(extra[slot, pl.ds(halo, 8), :], back * key_f, halo),
        )
        for which, grad in enumerate(grads):
            padded[slot, which, pl.ds(0, rows), :] = grad.astype(jnp.bfloat16).astype(jnp.float32)
            padded[slot, which, pl.ds(rows, halo), :] = extra[slot, pl.ds((2 + which) * halo, halo), :]
            weights = tap_rows(taps_ref, which, lanes)
            running = weights[0] * padded[slot, which, pl.ds(0, rows), :]
            for offset in range(1, span):
                running = running + weights[offset] * padded[slot, which, pl.ds(offset, rows), :]
            results[index, which] = running.astype(jnp.bfloat16)
            leave(index, which)


def receive_kernel(order, places, taps_ref, far_ref, near_ref, filter_ref, *refs):
    size = 2 * far_ref.shape[2] + round_up(5 * (taps_ref.shape[1] - 1), 16)
    in_refs = [ref.at[pl.ds((place == 1) * size, size)] for place, ref in zip(places, refs)]
    mixed_ref, grads_ref, filter_out, padded, extra, results, sems, filter_sem = refs[-8:]
    me = lax.axis_index("context")
    copies = []
    if filter_ref is not None:
        copies.append(pltpu.make_async_copy(filter_ref, filter_out.at[0], filter_sem))
        copies[-1].start()

    def leave(index, which):
        lanes = pl.ds(pl.multiple_of((me ^ order[places[index]]) * LANES, LANES), LANES)
        target = mixed_ref.at[:, lanes] if which == 3 else grads_ref.at[which, :, lanes]
        copies.append(pltpu.make_async_copy(results.at[index, which], target, sems.at[index, which]))
        copies[-1].start()

    held = (far_ref, near_ref)
    finish_channels(
        order, places, in_refs, taps_ref, held, padded, extra, results, leave
    )
    for copy in copies:
        copy.wait()


def last_kernel(order, places, taps_ref, far_ref, near_ref, *refs):
    in_refs, refs = refs[: len(places)], refs[len(places) + 2 :]
    mixed_ref, grads_ref, padded, extra, results, sems = refs
    receive_kernel(
        order, places, taps_ref, far_ref, near_ref, None, *in_refs,
        mixed_ref, grads_ref, None, padded, extra, results, sems, None,
    )


def on_device(kernel, out_shape, scratch, args, in_hbm=(), unread=None, updates=(), cover=False):
    whole = pl.BlockSpec(memory_space=pltpu.VMEM)
    hbm = pl.BlockSpec(memory_space=pltpu.HBM)
    anywhere = pl.BlockSpec(memory_space=pl.ANY)
    fixed = [pltpu.with_memory_space_constraint(arg, pltpu.HBM) for arg in in_hbm]
    before = [] if unread is None else [unread]
    first_update = len(before) + len(fixed) + len(args)
    return pl.pallas_call(
        kernel if unread is None else lambda _, *refs: kernel(*refs),
        out_shape=out_shape,
        in_specs=[anywhere] * len(before) + [hbm] * len(fixed) + [whole] * len(args) + [hbm] * len(updates),
        out_specs=jax.tree.map(
            lambda out: whole if isinstance(out, jax.ShapeDtypeStruct) else hbm, out_shape
        ),
        input_output_aliases={first_update + place: place for place in range(len(updates))},
        scratch_shapes=[
            pltpu.VMEM(shape, jnp.float32) if isinstance(shape, tuple) else shape for shape in scratch
        ],
        compiler_params=pltpu.CompilerParams(vmem_limit_bytes=VMEM_BYTES),
        cost_estimate=COVER if cover else None,
    )(*before, *fixed, *args, *updates)


def exchange_order(count):
    return sorted(
        range(count),
        key=lambda mask: (mask == 0, -(mask >> 1).bit_count(), mask % 2, -mask),
    )


def exchange(parcel, mask):
    count = lax.axis_size("context")
    return lax.ppermute(parcel, "context", [(i, i ^ mask) for i in range(count)])


def block_shards(query_proj, key_proj, value_proj, short_taps, long_filter, grad_mixed):
    rows, channels = query_proj.shape
    blocks = lax.axis_size("context")
    halo = short_taps.shape[1] - 1
    seq_len = rows * blocks
    merged = 2
    wide = merged * rows
    forward_hi, forward_lo, inverse = [jnp.asarray(table) for table in block_tables(wide)]
    edge_rows = round_up(5 * halo, 16)
    order = exchange_order(blocks)
    parcels = [jax.ShapeDtypeStruct((2 * rows + edge_rows, LANES), jnp.bfloat16)] * blocks
    spectra = (blocks // merged, 2 * wide, LANES)
    own_taps = (*short_taps.shape[:2], LANES)
    far = [place for place in range(blocks) if order[place] > 1]
    near = [place for place in range(blocks) if order[place] <= 1]

    parcel = parcels[0]
    double = jax.ShapeDtypeStruct((2 * parcel.shape[0], LANES), jnp.bfloat16)
    made = [(2, 3, rows + 8, LANES), (2, edge_rows, LANES)]
    inputs = (4, rows, LANES)
    sources = (long_filter[0], forward_hi, forward_lo)

    def floats(*shape):
        return jax.ShapeDtypeStruct(shape, jnp.float32)

    first, *sent, far_filtered, filter_here, hi_here, lo_here, landed, taps = on_device(
        functools.partial(send_kernel, order, far, near, len(sources)),
        [double, *parcels[: len(far) - 2], floats(len(far), 4, rows, LANES)]
        + [jax.ShapeDtypeStruct(value.shape, value.dtype) for value in sources]
        + [
            jax.ShapeDtypeStruct((len(near), *inputs), jnp.bfloat16),
            floats(len(near), *own_taps),
        ],
        [
            pltpu.VMEM((len(far), *inputs), jnp.bfloat16),
            (len(far), *own_taps),
            *made,
            pltpu.SemaphoreType.DMA((len(far), 5)),
            pltpu.SemaphoreType.DMA((len(near), 5)),
            pltpu.SemaphoreType.DMA((len(sources),)),
        ],
        (),
        in_hbm=(query_proj, key_proj, value_proj, grad_mixed, short_taps, *sources),
    )
    first = exchange(first, order[0])
    others = [exchange(value, order[place]) for place, value in zip(far[2:], sent)]
    shared, kept_here, near_filtered, own = on_device(
        near_kernel,
        [double, parcel, floats(len(near), 4, rows, LANES), floats(*own_taps)],
        made,
        (landed, taps, first),
        cover=True,
    )
    arrived = (first, *others, exchange(shared, 1), kept_here)
    spec_h = on_device(
        filter_kernel,
        jax.ShapeDtypeStruct(spectra, jnp.float32),
        [],
        (filter_here, hi_here, lo_here),
        cover=True,
    )
    *results, spec_x, spec_g = on_device(
        functools.partial(convolve_kernel, order),
        [double, *parcels[2:], floats(*spectra), floats(*spectra)],
        [
            (blocks, edge_rows, LANES),
            (blocks, 2, 8, LANES),
            (3, blocks, 24, LANES),
            (blocks, 6, 8, LANES),
            pltpu.VMEM((blocks, rows, 2 * LANES), jnp.bfloat16),
            pltpu.VMEM((*spectra[:2], 2 * LANES), jnp.bfloat16),
            (blocks + 1, edge_rows, LANES),
        ],
        (own, spec_h, hi_here, inverse, *arrived),
    )
    first, *sent = results
    first = exchange(first, order[0])
    others = [exchange(value, order[place]) for place, value in zip(far[2:], sent)]
    (filter_grad,) = on_device(
        functools.partial(correlate_kernel, 1.0 / math.sqrt(seq_len)),
        [floats(*long_filter.shape[1:])],
        [pltpu.VMEM(spectra, jnp.bfloat16)],
        (spec_x, spec_g, inverse),
    )
    (shared,) = on_device(share_kernel, [double], [], (filter_grad, sent[-2], first))
    shared = exchange(shared, 1)
    returned = [first, shared, *others, shared, sent[-1]]
    early = [0, near[-1]]
    late = [place for place in range(blocks) if place not in early]
    outputs = (
        pltpu.HBM((rows, channels), jnp.bfloat16),
        pltpu.HBM((3, rows, channels), jnp.bfloat16),
        pltpu.HBM(long_filter.shape, jnp.float32),
    )

    def working(places):
        return [
            (2, 3, rows + 16, LANES),
            (2, edge_rows + 8, LANES),
            pltpu.VMEM((len(places), 4, rows, LANES), jnp.bfloat16),
            pltpu.SemaphoreType.DMA((len(places), 4)),
        ]

    common = (short_taps, far_filtered, near_filtered)
    *begun, filter_grad = on_device(
        functools.partial(receive_kernel, order, early),
        outputs,
        [*working(early), pltpu.SemaphoreType.DMA(())],
        (*common, filter_grad, *(returned[place] for place in early)),
        cover=True,
    )
    mixed_out, input_grads = on_device(
        functools.partial(last_kernel, order, late),
        outputs[:2],
        working(late),
        (*common, *(returned[place] for place in late)),
        updates=begun,
    )
    return (mixed_out, input_grads, filter_grad)


def shards(query_proj, key_proj, value_proj, short_taps, long_filter, grad_mixed):
    rows, channels = query_proj.shape
    halo = short_taps.shape[1] - 1
    blocks = lax.axis_size("context")
    power_of_two = blocks & (blocks - 1) == 0
    fits = power_of_two and blocks > 2 and channels == blocks * LANES and rows % 128 == 0 and halo <= 8
    chosen = block_shards if fits else general_shards
    return chosen(query_proj, key_proj, value_proj, short_taps, long_filter, grad_mixed)


def solution(mesh):
    return jax.shard_map(
        shards,
        mesh=mesh,
        in_specs=(
            P("context", "tensor"),
            P("context", "tensor"),
            P("context", "tensor"),
            P(None, None, "tensor"),
            P("tensor", "context", None),
            P("context", "tensor"),
        ),
        out_specs=(
            P("context", "tensor"),
            P(None, "context", "tensor"),
            P("tensor", "context", None),
        ),
        check_vma=False,
    )
```
